128 devices in a mesh: gy: 8 (over y_lo, z), gx: 16 (over y_hi, x, core).
Axes of the slice: x: 4, y: 4 (y_hi: 2, y_lo: 2; y = y_hi * 2 + y_lo), z: 4, core: 2. Of those that a mesh axis runs over, the one named last changes fastest.
Arguments:
- base_prod: bfloat16 [8, 1024, 4096], P(None, 'gy', 'gx'), may hold values from 0.5 to 2
- resident: float32 [1024, 4096], P('gy', 'gx'), may hold values from 0.2 to 5
- floor_space: float32 [1024, 4096], P('gy', 'gx'), may hold values from 0.5 to 2
- bracket: int32 [1024, 4096], P('gy', 'gx'), may hold values from 0 to 7
- tax_rate: float32 [8], replicated, may hold values from 0.05 to 0.45
- mixing: float32 [8, 8], replicated, may hold values from 0.02 to 0.2
- spill_decay: float32 [8], replicated, may hold values from 0.5 to 4
- commute_decay: float32 [8], replicated, may hold values from 0.5 to 4
- pair_dest: int32 [65536, 1], P(('gy', 'gx')), may hold values from 0 to 127; in each aligned block of 512 rows (0 to 511, 512 to 1023, ...) at most 8 rows name the same one
- pair_src: int32 [65536], P(('gy', 'gx')), may hold values from 0 to 2047
- pair_dst: int32 [65536], P(('gy', 'gx')), may hold values from 0 to 2047
- pair_count: int32 [65536], P(('gy', 'gx')), may hold values from 1 to 8
Outputs:
- wage_level: float32 [8, 1024, 4096], P(None, 'gy', 'gx')
- rent_level: float32 [1024, 4096], P('gy', 'gx')
The draws below stay inside these ranges and needn't reach their ends.
Inputs may be any that keep to these rules, and one draw needn't show every extreme that they name: `pair_dest`: pair p leaves tile p // 512; among the pairs of one anchor tile no destination tile is named more than 8 times.
All inputs are finite; a program needn't handle non-finite values.
Results may differ from the reference program's by a relative error of at most 0.0003.
Values may be sent and summed in bfloat16 or wider, within the bound.
A program may use at most 64 MiB of HBM per device.

```python
import math
import jax
import jax.numpy as jnp
import numpy as np
from jax import lax

SECTORS = 8
HALF = 64
BRACKETS = 8
ITERS = 3
ROWS_DEV = 128
COLS_DEV = 256
P_DEV = 512
TILES_Y = 8
TILES_X = 16
TILES = 128
CAP = 8
NY = 1024
NX = 4096
STRIPS = 2048
PAIRS = 65536


def touch_ends(entries, rng, smallest, largest):
    dims = entries.shape
    place = [jax.random.randint(jax.random.fold_in(rng, axis), (), 0, dims[axis]) for axis in range(len(dims))]
    entries = entries.at[tuple(place)].set(smallest)
    longest = dims.index(max(dims))
    place[longest] = (place[longest] + 1) % dims[longest]
    return entries.at[tuple(place)].set(largest)


def steps_of(key, dims, cuts, low, largest):
    def one(position, shards_of):
        heights = jax.random.uniform(jax.random.fold_in(jax.random.fold_in(key, 6), position), (shards_of,), jnp.float32, low / len(cuts), largest / len(cuts))
        return jnp.repeat(jnp.exp(heights), dims[position] // shards_of).reshape((-1,) + (1,) * (len(dims) - position - 1))

    gain = one(*cuts[0])
    for cut in cuts[1:]:
        gain = gain * one(*cut)
    return gain


def shared_out(rng, own, number, rows, number_of, top, bound, lean):
    ranking = jax.random.permutation(rng, number_of)
    heavy_load, usual = portions_of(number_of, rows * top, bound, lean, True), portions_of(number_of, rows * top, bound, lean, False)
    places = jnp.arange(number_of)

    def named(sizes, offset_by):
        used = int((sizes > 0).sum())
        fixed = max(1, used // 4)
        passed = fixed + (places - fixed + offset_by * (used - fixed)) % max(1, number_of - fixed)
        return jnp.zeros((number_of,), jnp.int32).at[ranking[jnp.where(places < fixed, places, passed)]].set(jnp.asarray(sizes, jnp.int32))

    sizes = jnp.where(number % 4 == 0, named(heavy_load, number // 4), named(usual, number - number // 4 - 1))
    mixed = jax.random.permutation(jax.random.fold_in(own, 3), number_of)
    donor, taker = mixed[0:number_of // 2 * 2:2], mixed[1:number_of // 2 * 2:2]
    margin = jnp.minimum(sizes[donor] - 1, bound - sizes[taker]) // 2
    margin = jnp.where((donor == ranking[0]) | (taker == ranking[0]) | (sizes[taker] == 0), 0, jnp.maximum(margin, 0))
    passed = jax.random.randint(jax.random.fold_in(own, 4), (number_of // 2,), 0, 1 << 20) % (margin + 1)
    sizes = sizes.at[donor].add(-passed).at[taker].add(passed)
    members = jnp.searchsorted(jnp.cumsum(sizes), jnp.arange(rows * top), side="right").astype(jnp.int32)
    grid = members.reshape(top, rows).T
    grid = grid[jax.random.permutation(jax.random.fold_in(own, 1), rows)]
    offset_by = jax.random.randint(jax.random.fold_in(own, 2), (rows, 1), 0, top)
    return jnp.take_along_axis(grid, (jnp.arange(top)[None, :] + offset_by) % top, axis=1)


def portions_of(amount, total, bound, skew, full):
    weights = [(1 << 20) // math.isqrt(standing ** skew) + 1 for standing in range(1, amount + 1)]
    largest = bound if full else min(bound, max(-(-total // amount), total * weights[0] // sum(weights)))
    least = 1 if total - largest >= amount - 1 else 0
    given, spare = [largest] + [least] * (amount - 1), total - largest - least * (amount - 1)
    while spare > 0:
        candidates = [i for i in range(1, amount) if given[i] < largest] or [i for i in range(1, amount) if given[i] < bound]
        pool, left = sum([weights[i] for i in candidates]), spare
        for i in candidates:
            addition = min(bound - given[i], max(1, left * weights[i] // pool), spare)
            given[i] = given[i] + addition
            spare = spare - addition
    return np.array(given)


def setup_inputs(seed: int = 0) -> dict:
    keys = jax.random.split(jax.random.key(seed), 13)
    base_prod = jnp.clip(jnp.exp(math.log(2.0) - 1.3862944 * jax.random.uniform(keys[0], (SECTORS, NY, NX), jnp.float32) ** steps_of(keys[0], (SECTORS, NY, NX), ((1, 8), (2, 16)), -0.2, 0.2)), 0.5, 2.0).astype(jnp.bfloat16)
    resident = jnp.clip(jnp.exp(math.log(5.0) - 3.218876 * jax.random.uniform(keys[1], (NY, NX), jnp.float32) ** steps_of(keys[1], (NY, NX), ((0, 8), (1, 16)), -0.2, 0.2)), 0.2, 5.0)
    floor_space = jnp.clip(jnp.exp(math.log(2.0) - 1.3862944 * jax.random.uniform(keys[2], (NY, NX), jnp.float32) ** steps_of(keys[2], (NY, NX), ((0, 8), (1, 16)), -0.2, 0.2)), 0.5, 2.0)
    bracket = touch_ends(jax.random.randint(keys[3], (NY, NX), 0, BRACKETS), jax.random.fold_in(keys[3], 1), 0, BRACKETS - 1).astype(jnp.int32)
    tax_rate = jnp.clip(jax.random.uniform(keys[4], (BRACKETS,), jnp.float32, 0.05, 0.45), 0.05, 0.45)
    mixing = jnp.clip(jax.random.uniform(keys[5], (SECTORS, SECTORS), jnp.float32, 0.02, 0.2), 0.02, 0.2)
    spill_decay = jnp.clip(jnp.exp(jax.random.uniform(keys[6], (SECTORS,), jnp.float32, math.log(0.5), math.log(4.0))), 0.5, 4.0)
    commute_decay = jnp.clip(jnp.exp(jax.random.uniform(keys[7], (SECTORS,), jnp.float32, math.log(0.5), math.log(4.0))), 0.5, 4.0)
    pair_dest_keys = jax.random.split(jax.random.fold_in(keys[8], 1), PAIRS // P_DEV)
    pair_dest_turns = jax.random.permutation(jax.random.fold_in(keys[8], 3), PAIRS // P_DEV)
    pair_dest = jax.vmap(lambda own, number: shared_out(jax.random.fold_in(keys[8], 2), own, number, P_DEV, TILES, 1, CAP, 2))(pair_dest_keys, pair_dest_turns).reshape((PAIRS, 1))
    pair_src = touch_ends(jax.random.randint(keys[9], (PAIRS,), 0, STRIPS), jax.random.fold_in(keys[9], 1), 0, STRIPS - 1).astype(jnp.int32)
    pair_dst = touch_ends(jax.random.randint(keys[10], (PAIRS,), 0, STRIPS), jax.random.fold_in(keys[10], 1), 0, STRIPS - 1).astype(jnp.int32)
    pair_count = touch_ends(jax.random.randint(keys[11], (PAIRS,), 1, 9), jax.random.fold_in(keys[11], 1), 1, 8).astype(jnp.int32)
    return dict(base_prod=base_prod, resident=resident, floor_space=floor_space, bracket=bracket, tax_rate=tax_rate, mixing=mixing, spill_decay=spill_decay, commute_decay=commute_decay, pair_dest=pair_dest, pair_src=pair_src, pair_dst=pair_dst, pair_count=pair_count)


EPS_FRECHET = 3.0
BETA_WAGE = 0.3
FAR_SCALE = 0.125

def tap_bands(decay_rate):
    offset = jnp.abs(jnp.arange(2 * HALF + 1).astype(jnp.float32) - HALF) / HALF
    unscaled = jnp.exp(-decay_rate[:, None] * offset[None, :])
    tap_row = (unscaled / lax.optimization_barrier(jnp.sum(unscaled, axis=1, keepdims=True))).astype(jnp.bfloat16)
    block_size = 2 * HALF
    tap_lag = (jnp.arange(2 * block_size)[:, None] - jnp.arange(block_size)[None, :]).astype(jnp.int32)
    inside = (tap_lag >= 0) & (tap_lag <= 2 * HALF)
    picked = tap_row[:, jnp.clip(tap_lag, 0, 2 * HALF)]
    banded = jnp.where(inside[None], picked, jnp.zeros_like(picked))
    return (banded[:, :block_size], banded[:, block_size:])

def column_pass(source, band_upper, band_lower):
    block_size = 2 * HALF
    blocks = source.reshape(source.shape[0], -1, block_size)
    result = jnp.einsum('ynk,kc->ync', blocks[:, :-1], band_upper, precision=lax.Precision.HIGHEST)
    result = result + jnp.einsum('ynk,kc->ync', blocks[:, 1:], band_lower, precision=lax.Precision.HIGHEST)
    return result.reshape(source.shape[0], -1)

def row_pass(source, band_upper, band_lower):
    block_size = 2 * HALF
    blocks = source.reshape(-1, block_size, source.shape[1])
    result = jnp.einsum('nkx,kc->ncx', blocks[:-1], band_upper, precision=lax.Precision.HIGHEST)
    result = result + jnp.einsum('nkx,kc->ncx', blocks[1:], band_lower, precision=lax.Precision.HIGHEST)
    return result.reshape(-1, source.shape[1])

def correlate(source, kernel_pair):

    def per_sector(operands):
        plane_field, upper_band, lower_band = operands
        upper_band = upper_band.astype(jnp.float32)
        lower_band = lower_band.astype(jnp.float32)
        plane_field = lax.optimization_barrier(plane_field)
        padded = jnp.pad(plane_field.astype(jnp.float32), ((0, 0), (HALF, HALF)))
        middle = column_pass(padded, upper_band, lower_band).astype(jnp.bfloat16)
        middle = lax.optimization_barrier(middle)
        padded = jnp.pad(middle.astype(jnp.float32), ((HALF, HALF), (0, 0)))
        return row_pass(padded, upper_band, lower_band)
    return lax.map(per_sector, (source, kernel_pair[0], kernel_pair[1]))

def long_commutes(supply, pair_dest, pair_src, pair_dst, pair_count):
    supply = lax.optimization_barrier(supply)
    strip_table = supply.reshape(SECTORS, TILES_Y, ROWS_DEV, TILES_X, COLS_DEV // 16, 16)
    strip_table = strip_table.transpose(1, 3, 2, 4, 0, 5).reshape(TILES * STRIPS, SECTORS * 16).astype(jnp.float32)
    anchor = (jnp.arange(PAIRS) // P_DEV).astype(jnp.int32)
    src_rows = anchor * STRIPS + pair_src.astype(jnp.int32)
    dst_rows = pair_dest[:, 0].astype(jnp.int32) * STRIPS + pair_dst.astype(jnp.int32)
    carried = strip_table[src_rows] * pair_count.astype(jnp.float32)[:, None]
    accumulated = jnp.zeros_like(strip_table).at[dst_rows].add(carried)
    accumulated = accumulated.reshape(TILES_Y, TILES_X, ROWS_DEV, COLS_DEV // 16, SECTORS, 16)
    return accumulated.transpose(4, 0, 2, 1, 3, 5).reshape(SECTORS, NY, NX)

def reference(base_prod, resident, floor_space, bracket, tax_rate, mixing, spill_decay, commute_decay, pair_dest, pair_src, pair_dst, pair_count):
    kernel_comm = tap_bands(commute_decay)
    kernel_spill = tap_bands(spill_decay)
    base_float = base_prod.astype(jnp.float32)
    wage_level = base_float
    rent_level = jnp.ones_like(resident)
    tax_cell = tax_rate[bracket]
    population = jnp.sum(resident)
    for iteration in range(ITERS):
        wage_power = wage_level * wage_level * wage_level
        sector_share = wage_power / lax.optimization_barrier(jnp.sum(wage_power, axis=0))
        supply = (resident[None] * sector_share).astype(jnp.bfloat16)
        near_flow = correlate(supply, kernel_comm)
        far_flow = long_commutes(supply, pair_dest, pair_src, pair_dst, pair_count)
        labor_force = near_flow + FAR_SCALE * far_flow
        spillover = correlate(labor_force.astype(jnp.bfloat16), kernel_spill)
        mixed_logs = jnp.einsum('st,tyx->syx', mixing, jnp.log(1.0 + spillover), precision=lax.Precision.HIGHEST)
        productivity = base_float * jnp.exp(mixed_logs)
        income = lax.optimization_barrier(jnp.sum(sector_share * wage_level, axis=0))
        revenue = jnp.sum(resident * tax_cell * income)
        net_income = (1.0 - tax_cell) * income + revenue / population
        rent_level = jnp.sqrt(rent_level * resident * net_income / floor_space)
        wage_level = productivity * jnp.exp(-BETA_WAGE * jnp.log(1.0 + labor_force))
    return (wage_level, rent_level)
```

```python
import functools

import jax
import jax.numpy as jnp
from jax import lax
from jax.experimental import pallas as pl
from jax.experimental.pallas import tpu as pltpu
from jax.sharding import PartitionSpec as P

HALF = 64
ITERS = 3
SECTORS = 8
CAP = 8
BETA_WAGE = 0.3
FAR_SCALE = 0.125
ROWS = 128
COLS = 256
GROUPS = COLS // 16
PAIRS2 = SECTORS // 2
CHUNK = 16
MESH = pl.DeviceIdType.MESH
F32 = jnp.float32
BF16 = jnp.bfloat16


def swap_blocks(values):
    values = list(values)
    block = lax.broadcasted_iota(jnp.int32, values[0].shape, 1) // 16
    for d in (1, 2, 4):
        low = (block & d) == 0
        for a in range(8):
            if a & d:
                continue
            b = a + d
            first, second = values[a], values[b]
            values[a] = jnp.where(low, first, pltpu.roll(second, 16 * d, 1))
            values[b] = jnp.where(low, pltpu.roll(first, 128 - 16 * d, 1), second)
    return values


def kernel(
    tiles_y,
    tiles_x,
    base_ref,
    resident_ref,
    floor_ref,
    bracket_ref,
    pairs_ref,
    tax_ref,
    mixing_ref,
    spill_ref,
    commute_ref,
    wage_ref,
    rent_ref,
    ext,
    edge_out,
    edge_in,
    mid,
    near,
    labor,
    tap_row,
    band_row,
    band_col,
    band_edge,
    table,
    source_hot,
    slot_hot,
    place,
    far,
    one_out,
    one_in,
    two_out,
    two_in,
    sum_out,
    sum_in,
    total_out,
    total_in,
    rate_ref,
    income_ref,
    row_send,
    row_recv,
    edge_send,
    edge_recv,
    one_send,
    one_recv,
    two_send,
    two_recv,
    sum_send,
    sum_recv,
):
    my = lax.axis_index("gy")
    mx = lax.axis_index("gx")
    slots_x = tiles_y * CAP
    slots_y = tiles_x * CAP
    slots = tiles_x * slots_x
    far_pairs = pairs_ref.shape[1]

    barrier = pltpu.get_barrier_semaphore()

    def greet_x(j, carry):
        pl.semaphore_signal(
            barrier, inc=1, device_id=(my, lax.rem(mx + j, tiles_x)), device_id_type=MESH
        )
        return carry

    def greet_y(j, carry):
        pl.semaphore_signal(
            barrier, inc=1, device_id=(lax.rem(my + j, tiles_y), mx), device_id_type=MESH
        )
        return carry

    lax.fori_loop(1, tiles_x, greet_x, 0)
    lax.fori_loop(1, tiles_y, greet_y, 0)

    @pl.when(my == 0)
    def _():
        ext[:, :, 0:HALF, :] = jnp.zeros((2 * ITERS, SECTORS, HALF, COLS), BF16)

    @pl.when(my == tiles_y - 1)
    def _():
        ext[:, :, HALF + ROWS :, :] = jnp.zeros((2 * ITERS, SECTORS, HALF, COLS), BF16)

    @pl.when(mx == 0)
    def _():
        edge_in[:, 0] = jnp.zeros((2 * ITERS, PAIRS2, ROWS, 128), BF16)

    @pl.when(mx == tiles_x - 1)
    def _():
        edge_in[:, 1] = jnp.zeros((2 * ITERS, PAIRS2, ROWS, 128), BF16)

    def row_copy(e, i, way):
        start = HALF if way == 0 else ROWS
        land = HALF + ROWS if way == 0 else 0
        target = my - 1 if way == 0 else my + 1
        return pltpu.make_async_remote_copy(
            src_ref=ext.at[e, pl.ds(2 * i, 2), pl.ds(start, HALF), :],
            dst_ref=ext.at[e, pl.ds(2 * i, 2), pl.ds(land, HALF), :],
            send_sem=row_send.at[e, way],
            recv_sem=row_recv.at[e, way, i],
            device_id=(target, mx),
            device_id_type=MESH,
        )

    def row_drain(e, way):
        start = HALF if way == 0 else ROWS
        target = my - 1 if way == 0 else my + 1
        return pltpu.make_async_remote_copy(
            src_ref=ext.at[e, :, pl.ds(start, HALF), :],
            dst_ref=ext.at[e, :, pl.ds(start, HALF), :],
            send_sem=row_send.at[e, way],
            recv_sem=row_recv.at[e, way, 0],
            device_id=(target, mx),
            device_id_type=MESH,
        )

    can_row = (my > 0, my < tiles_y - 1)
    can_edge = (mx > 0, mx < tiles_x - 1)

    def send_rows(e, way):
        @pl.when(can_row[way])
        def _():
            for i in range(PAIRS2):
                row_copy(e, i, way).start()

    def edge_copy(e, i, way):
        target = mx - 1 if way == 0 else mx + 1
        return pltpu.make_async_remote_copy(
            src_ref=edge_out.at[e, way, i],
            dst_ref=edge_in.at[e, 1 - way, i],
            send_sem=edge_send.at[e, way],
            recv_sem=edge_recv.at[e, way, i],
            device_id=(my, target),
            device_id_type=MESH,
        )

    def edge_drain(e, way):
        target = mx - 1 if way == 0 else mx + 1
        return pltpu.make_async_remote_copy(
            src_ref=edge_out.at[e, way],
            dst_ref=edge_in.at[e, 1 - way],
            send_sem=edge_send.at[e, way],
            recv_sem=edge_recv.at[e, way, 0],
            device_id=(my, target),
            device_id_type=MESH,
        )

    lane128 = lax.broadcasted_iota(jnp.int32, (ROWS, 128), 1)

    def rows_pass(e, kind):
        def one(i, carry):
            for way in range(2):

                @pl.when(can_row[1 - way])
                def _():
                    row_copy(e, i, way).wait_recv()

            ends = []
            for k in range(2):
                s = 2 * i + k
                passed = jnp.dot(
                    band_row[kind * SECTORS + s], ext[e, s], preferred_element_type=F32
                )
                mid[s] = passed.astype(BF16)
                ends.append((passed[:, 0:128], passed[:, 128:256]))
            first, second = ends
            low = lane128 < HALF
            edge_out[e, 0, i] = jnp.where(low, first[0], pltpu.roll(second[0], HALF, 1)).astype(
                BF16
            )
            edge_out[e, 1, i] = jnp.where(low, pltpu.roll(second[1], HALF, 1), first[1]).astype(
                BF16
            )
            for way in range(2):

                @pl.when(can_edge[way])
                def _():
                    edge_copy(e, i, way).start()

            return carry

        lax.fori_loop(0, PAIRS2, one, 0)

    def columns_pass(e, kind, result):
        def one(i, carry):
            for way in range(2):

                @pl.when(can_edge[1 - way])
                def _():
                    edge_copy(e, i, way).wait_recv()

            for k in range(2):
                s = 2 * i + k
                b = kind * SECTORS + s
                value = jnp.dot(mid[s], band_col[b], preferred_element_type=F32)
                value += jnp.dot(
                    edge_in[e, 0, i], band_edge[b, 0:128, :], preferred_element_type=F32
                )
                value += jnp.dot(
                    edge_in[e, 1, i], band_edge[b, 128:256, :], preferred_element_type=F32
                )
                result[s] = value
            return carry

        lax.fori_loop(0, PAIRS2, one, 0)

    def make_bands(kind):
        u = lax.broadcasted_iota(jnp.int32, (COLS, COLS), 0)
        x = lax.broadcasted_iota(jnp.int32, (COLS, COLS), 1)
        inside = jnp.abs(u - x) <= 128

        def one(s, carry):
            b = kind * SECTORS + s
            line = jnp.broadcast_to(tap_row[pl.ds(b, 1), :], (ROWS, COLS))
            rows_band = pltpu.roll(line, 0, 1, stride=1, stride_axis=0)
            band_row[b] = rows_band.astype(BF16)
            circle = jnp.concatenate(
                [pltpu.roll(rows_band, COLS - HALF, 1), pltpu.roll(rows_band, HALF, 1)], axis=0
            )
            band_col[b] = jnp.where(inside, circle, 0.0).astype(BF16)
            rest = jnp.where(inside, 0.0, circle)
            even = jnp.concatenate([rest[128:256], rest[0:128]], axis=0)
            odd = jnp.concatenate(
                [rest[192:256], rest[128:192], rest[64:128], rest[0:64]], axis=0
            )
            band_edge[b] = jnp.where(lax.rem(s, 2) == 0, even, odd).astype(BF16)
            return carry

        lax.fori_loop(0, SECTORS, one, 0)

    def first_copy(a, x):
        return pltpu.make_async_remote_copy(
            src_ref=one_out.at[a, x],
            dst_ref=one_in.at[a, mx],
            send_sem=one_send.at[a],
            recv_sem=one_recv.at[a],
            device_id=(my, x),
            device_id_type=MESH,
        )

    def first_all(a):
        return pltpu.make_async_remote_copy(
            src_ref=one_out.at[a, pl.ds(0, tiles_x - 1)],
            dst_ref=one_in.at[a, pl.ds(0, tiles_x - 1)],
            send_sem=one_send.at[a],
            recv_sem=one_recv.at[a],
            device_id=(my, lax.rem(mx + 1, tiles_x)),
            device_id_type=MESH,
        )

    def second_copy(a, y):
        return pltpu.make_async_remote_copy(
            src_ref=two_out.at[a, y],
            dst_ref=two_in.at[a, my],
            send_sem=two_send.at[a],
            recv_sem=two_recv.at[a],
            device_id=(y, mx),
            device_id_type=MESH,
        )

    def second_all(a):
        return pltpu.make_async_remote_copy(
            src_ref=two_out.at[a, pl.ds(0, tiles_y - 1)],
            dst_ref=two_in.at[a, pl.ds(0, tiles_y - 1)],
            send_sem=two_send.at[a],
            recv_sem=two_recv.at[a],
            device_id=(lax.rem(my + 1, tiles_y), mx),
            device_id_type=MESH,
        )

    def start_first(a):
        def one(j, carry):
            first_copy(a, lax.rem(mx + j, tiles_x)).start()
            return carry

        lax.fori_loop(1, tiles_x, one, 0)
        one_in[a, mx] = one_out[a, mx]

    def pass_on(a):
        first_all(a).wait_recv()
        for i in range(tiles_x // 2):
            pieces = [
                one_in[a, 2 * i + k].astype(F32).reshape(tiles_y, CAP, 128) for k in range(2)
            ]
            two_out[a, :, 2 * i * CAP : 2 * (i + 1) * CAP, :] = jnp.concatenate(
                pieces, axis=1
            ).astype(BF16)

        def one(j, carry):
            second_copy(a, lax.rem(my + j, tiles_y)).start()
            return carry

        lax.fori_loop(1, tiles_y, one, 0)
        two_in[a, my] = two_out[a, my]

    def sum_copy(x):
        return pltpu.make_async_remote_copy(
            src_ref=sum_out,
            dst_ref=sum_in.at[mx],
            send_sem=sum_send.at[0],
            recv_sem=sum_recv.at[0],
            device_id=(my, x),
            device_id_type=MESH,
        )

    def total_copy(y):
        return pltpu.make_async_remote_copy(
            src_ref=total_out,
            dst_ref=total_in.at[my],
            send_sem=sum_send.at[1],
            recv_sem=sum_recv.at[1],
            device_id=(y, mx),
            device_id_type=MESH,
        )

    def sum_all():
        return pltpu.make_async_remote_copy(
            src_ref=sum_in.at[pl.ds(0, tiles_x - 1)],
            dst_ref=sum_in.at[pl.ds(0, tiles_x - 1)],
            send_sem=sum_send.at[0],
            recv_sem=sum_recv.at[0],
            device_id=(my, lax.rem(mx + 1, tiles_x)),
            device_id_type=MESH,
        )

    def total_all():
        return pltpu.make_async_remote_copy(
            src_ref=total_in.at[pl.ds(0, tiles_y - 1)],
            dst_ref=total_in.at[pl.ds(0, tiles_y - 1)],
            send_sem=sum_send.at[1],
            recv_sem=sum_recv.at[1],
            device_id=(lax.rem(my + 1, tiles_y), mx),
            device_id_type=MESH,
        )

    def shares(it, r, h, wages, revenue):
        rows = pl.ds(r, CHUNK)
        lanes = slice(128 * h, 128 * h + 128)
        powers = [w * w * w for w in wages]
        inverse = 1.0 / sum(powers[1:], powers[0])
        people = resident_ref[rows, lanes]
        share = [p * inverse for p in powers]
        income = sum([q * w for q, w in zip(share[1:], wages[1:])], share[0] * wages[0])
        income_ref[it, rows, lanes] = income
        supply = [people * q for q in share]
        for s in range(SECTORS):
            ext[2 * it, s, pl.ds(HALF + r, CHUNK), lanes] = supply[s].astype(BF16)
        for g, strip in enumerate(swap_blocks(supply)):
            table[pl.ds((8 * h + g) * ROWS + r, CHUNK), :] = strip.astype(BF16)
        gain = people * rate_ref[rows, lanes] * income
        return revenue + gain[0:8] + gain[8:16]

    def gather(a):
        picked = jnp.dot(source_hot[...], table[...], preferred_element_type=F32).astype(BF16)
        ordered = jnp.dot(slot_hot[...], picked, preferred_element_type=F32).astype(BF16)
        one_out[a] = ordered.reshape(tiles_x, slots_x, 128)

    zero = jnp.zeros((8, 128), F32)

    def first_chunk(c, carry):
        people_sum, revenue = carry
        r = pl.multiple_of(c * CHUNK, CHUNK)
        rows = pl.ds(r, CHUNK)
        for h in range(2):
            lanes = slice(128 * h, 128 * h + 128)
            bracket = bracket_ref[rows, lanes]
            rate = jnp.zeros((CHUNK, 128), F32)
            for b in range(8):
                rate = jnp.where(bracket == b, tax_ref[b], rate)
            rate_ref[rows, lanes] = rate
            people = resident_ref[rows, lanes]
            people_sum = people_sum + people[0:8] + people[8:16]
            wages = [base_ref[s, rows, lanes].astype(F32) for s in range(SECTORS)]
            revenue = shares(0, r, h, wages, revenue)
        return people_sum, revenue

    people_sum, revenue0 = lax.fori_loop(0, ROWS // CHUNK, first_chunk, (zero, zero))
    pl.semaphore_wait(barrier, tiles_x - 1 + tiles_y - 1)
    send_rows(0, 0)
    send_rows(0, 1)

    across = pairs_ref[...].T
    dest_row, slot_base = pairs_ref[0:1, :], pairs_ref[1:2, :]
    earlier = lax.broadcasted_iota(jnp.int32, (far_pairs, far_pairs), 0) < (
        lax.broadcasted_iota(jnp.int32, (far_pairs, far_pairs), 1)
    )
    same = (across[:, 0:1] == dest_row) & earlier
    rank = jnp.sum(jnp.where(same, 1.0, 0.0), axis=0, keepdims=True)
    slot_of = (slot_base + rank).astype(jnp.int32)
    slot_ids = lax.broadcasted_iota(jnp.int32, (slots, far_pairs), 0)
    slot_hot[...] = jnp.where(slot_ids == slot_of, 1.0, 0.0).astype(BF16)
    strip_ids = lax.broadcasted_iota(jnp.int32, (far_pairs, GROUPS * ROWS), 1)
    source_hot[...] = jnp.where(
        strip_ids == across[:, 2:3].astype(jnp.int32), 1.0, 0.0
    ).astype(BF16)
    one_out[ITERS] = (
        jnp.dot(slot_hot[...], across.astype(BF16), preferred_element_type=F32)
        .astype(BF16)
        .reshape(tiles_x, slots_x, 128)
    )
    start_first(ITERS)
    gather(0)
    start_first(0)

    sector = lax.broadcasted_iota(jnp.int32, (2 * SECTORS, COLS), 0)
    tap = lax.broadcasted_iota(jnp.int32, (2 * SECTORS, COLS), 1)
    decay = jnp.zeros((2 * SECTORS, COLS), F32)
    for s in range(SECTORS):
        decay = jnp.where(sector == s, commute_ref[s], decay)
        decay = jnp.where(sector == SECTORS + s, spill_ref[s], decay)
    offset = jnp.abs(tap - HALF).astype(F32) / HALF
    unscaled = jnp.where(tap <= 2 * HALF, jnp.exp(-decay * offset), 0.0)
    tap_row[...] = (unscaled / jnp.sum(unscaled, axis=1, keepdims=True)).astype(BF16).astype(F32)
    make_bands(0)

    pass_on(ITERS)

    def build_place():
        second_all(ITERS).wait_recv()
        routing = two_in[ITERS].reshape(slots, 128)
        line = lax.broadcasted_iota(jnp.int32, (16, 128), 0)
        lane = lax.broadcasted_iota(jnp.int32, (16, 128), 1)
        pick = jnp.where((line == 0) & (lane == 3), 1.0, 0.0)
        pick = jnp.where((line == 0) & (lane == 4), float(ROWS), pick)
        pick = jnp.where((line == 1) & (lane == 5), 1.0, pick).astype(BF16)
        found = lax.dot_general(
            pick, routing, (((1,), (1,)), ((), ())), preferred_element_type=F32
        )
        where_to, weight = found[0:1, :].astype(jnp.int32), found[1:2, :]

        def one(g, carry):
            strip = g * ROWS + lax.broadcasted_iota(jnp.int32, (ROWS, slots), 0)
            place[pl.ds(pl.multiple_of(g * ROWS, ROWS), ROWS), :] = jnp.where(
                strip == where_to, weight, 0.0
            ).astype(BF16)
            return carry

        lax.fori_loop(0, GROUPS, one, 0)

    revenues = [revenue0]
    for it in range(ITERS):
        if it > 0:
            send_rows(2 * it, 0)
            send_rows(2 * it, 1)
            gather(it)
            start_first(it)
        if it == ITERS - 1:
            line = lax.broadcasted_iota(jnp.int32, (8, 128), 0)
            parts = zero
            for k, part in enumerate([people_sum] + revenues):
                parts = jnp.where(line == k, jnp.sum(part, axis=0, keepdims=True), parts)
            sum_out[...] = parts

            def start_sum(j, carry):
                sum_copy(lax.rem(mx + j, tiles_x)).start()
                return carry

            lax.fori_loop(1, tiles_x, start_sum, 0)
            sum_in[mx] = parts
        rows_pass(2 * it, 0)
        pass_on(it)
        if it == ITERS - 1:
            sum_all().wait_recv()
            halfway = jnp.sum(sum_in[...], axis=0)
            total_out[...] = halfway

            def start_total(j, carry):
                total_copy(lax.rem(my + j, tiles_y)).start()
                return carry

            lax.fori_loop(1, tiles_y, start_total, 0)
            total_in[my] = halfway
        columns_pass(2 * it, 0, near)
        if it == 0:
            build_place()
        second_all(it).wait_recv()
        far[...] = jnp.dot(
            place[...], two_in[it].reshape(slots, 128), preferred_element_type=F32
        )

        def labor_chunk(c, carry):
            r = pl.multiple_of(c * CHUNK, CHUNK)
            for h in range(2):
                lanes = slice(128 * h, 128 * h + 128)
                strips = [far[pl.ds((8 * h + g) * ROWS + r, CHUNK), :] for g in range(8)]
                for s, flow in enumerate(swap_blocks(strips)):
                    value = near[s, pl.ds(r, CHUNK), lanes] + FAR_SCALE * flow
                    labor[s, pl.ds(r, CHUNK), lanes] = value
                    ext[2 * it + 1, s, pl.ds(HALF + r, CHUNK), lanes] = value.astype(BF16)
            return carry

        lax.fori_loop(0, HALF // CHUNK, labor_chunk, 0)
        send_rows(2 * it + 1, 0)
        lax.fori_loop(HALF // CHUNK, ROWS // CHUNK, labor_chunk, 0)
        send_rows(2 * it + 1, 1)
        if it == 0:
            make_bands(1)
        if it == ITERS - 1:
            total_all().wait_recv()
            sums = jnp.sum(jnp.sum(total_in[...], axis=0), axis=1, keepdims=True)
            people_all = sums[0:1, 0:1]
            transfers = [sums[1 + k : 2 + k, 0:1] / people_all for k in range(ITERS)]

            def rent_chunk(c, carry):
                rows = pl.ds(pl.multiple_of(c * CHUNK, CHUNK), CHUNK)
                keep = 1.0 - rate_ref[rows, :]
                people, space = resident_ref[rows, :], floor_ref[rows, :]
                rent = None
                for k in range(ITERS):
                    net = keep * income_ref[k, rows, :] + transfers[k]
                    level = people if rent is None else rent * people
                    rent = jnp.sqrt(level * net / space)
                rent_ref[rows, :] = rent
                return carry

            lax.fori_loop(0, ROWS // CHUNK, rent_chunk, 0)
        rows_pass(2 * it + 1, 1)
        columns_pass(2 * it + 1, 1, near)

        def wage_chunk(c, revenue):
            r = pl.multiple_of(c * CHUNK, CHUNK)
            rows = pl.ds(r, CHUNK)
            for h in range(2):
                lanes = slice(128 * h, 128 * h + 128)
                logs = [jnp.log(1.0 + near[s, rows, lanes]) for s in range(SECTORS)]
                wages = []
                for s in range(SECTORS):
                    power = -BETA_WAGE * jnp.log(1.0 + labor[s, rows, lanes])
                    for t in range(SECTORS):
                        power = power + mixing_ref[s, t] * logs[t]
                    wages.append(base_ref[s, rows, lanes].astype(F32) * jnp.exp(power))
                if it == ITERS - 1:
                    for s in range(SECTORS):
                        wage_ref[s, rows, lanes] = wages[s]
                else:
                    revenue = shares(it + 1, r, h, wages, revenue)
            return revenue

        revenues.append(lax.fori_loop(0, ROWS // CHUNK, wage_chunk, zero))

    for e in range(2 * ITERS):
        for way in range(2):

            @pl.when(can_row[way])
            def _():
                row_drain(e, way).wait_send()

            @pl.when(can_edge[way])
            def _():
                edge_drain(e, way).wait_send()

    for a in range(ITERS + 1):
        first_all(a).wait_send()
        second_all(a).wait_send()
    sum_all().wait_send()
    total_all().wait_send()


def body(
    base_prod,
    resident,
    floor_space,
    bracket,
    tax_rate,
    mixing,
    spill_decay,
    commute_decay,
    pair_dest,
    pair_src,
    pair_dst,
    pair_count,
):
    tiles_y = lax.axis_size("gy")
    tiles_x = lax.axis_size("gx")
    slots = tiles_y * tiles_x * CAP
    far_pairs = pair_src.shape[0]
    dest = pair_dest[:, 0]
    pairs = jnp.stack(
        [
            dest,
            (dest % tiles_x) * (tiles_y * CAP) + (dest // tiles_x) * CAP,
            (pair_src % GROUPS) * ROWS + pair_src // GROUPS,
            pair_dst // GROUPS,
            pair_dst % GROUPS,
            pair_count,
        ],
        axis=0,
    ).astype(F32)
    pairs = jnp.pad(pairs, ((0, 122), (0, 0)))
    vmem = pl.BlockSpec(memory_space=pltpu.VMEM)
    smem = pl.BlockSpec(memory_space=pltpu.SMEM)
    exchanges = 2 * ITERS
    dma = pltpu.SemaphoreType.DMA
    return pl.pallas_call(
        functools.partial(kernel, tiles_y, tiles_x),
        out_shape=(
            jax.ShapeDtypeStruct(base_prod.shape, F32),
            jax.ShapeDtypeStruct(resident.shape, F32),
        ),
        in_specs=[vmem] * 5 + [smem] * 4,
        out_specs=(vmem, vmem),
        scratch_shapes=[
            pltpu.VMEM((exchanges, SECTORS, ROWS + 2 * HALF, COLS), BF16),
            pltpu.VMEM((exchanges, 2, PAIRS2, ROWS, 128), BF16),
            pltpu.VMEM((exchanges, 2, PAIRS2, ROWS, 128), BF16),
            pltpu.VMEM((SECTORS, ROWS, COLS), BF16),
            pltpu.VMEM((SECTORS, ROWS, COLS), F32),
            pltpu.VMEM((SECTORS, ROWS, COLS), F32),
            pltpu.VMEM((2 * SECTORS, COLS), F32),
            pltpu.VMEM((2 * SECTORS, ROWS, COLS), BF16),
            pltpu.VMEM((2 * SECTORS, COLS, COLS), BF16),
            pltpu.VMEM((2 * SECTORS, COLS, COLS), BF16),
            pltpu.VMEM((GROUPS * ROWS, 128), BF16),
            pltpu.VMEM((far_pairs, GROUPS * ROWS), BF16),
            pltpu.VMEM((slots, far_pairs), BF16),
            pltpu.VMEM((GROUPS * ROWS, slots), BF16),
            pltpu.VMEM((GROUPS * ROWS, 128), F32),
            pltpu.VMEM((ITERS + 1, tiles_x, tiles_y * CAP, 128), BF16),
            pltpu.VMEM((ITERS + 1, tiles_x, tiles_y * CAP, 128), BF16),
            pltpu.VMEM((ITERS + 1, tiles_y, tiles_x * CAP, 128), BF16),
            pltpu.VMEM((ITERS + 1, tiles_y, tiles_x * CAP, 128), BF16),
            pltpu.VMEM((8, 128), F32),
            pltpu.VMEM((tiles_x, 8, 128), F32),
            pltpu.VMEM((8, 128), F32),
            pltpu.VMEM((tiles_y, 8, 128), F32),
            pltpu.VMEM((ROWS, COLS), F32),
            pltpu.VMEM((ITERS, ROWS, COLS), F32),
            dma((exchanges, 2)),
            dma((exchanges, 2, PAIRS2)),
            dma((exchanges, 2)),
            dma((exchanges, 2, PAIRS2)),
            dma((ITERS + 1,)),
            dma((ITERS + 1,)),
            dma((ITERS + 1,)),
            dma((ITERS + 1,)),
            dma((2,)),
            dma((2,)),
        ],
        compiler_params=pltpu.CompilerParams(
            collective_id=0, has_side_effects=True, vmem_limit_bytes=60 * 1024 * 1024
        ),
    )(
        base_prod,
        resident,
        floor_space,
        bracket,
        pairs,
        tax_rate,
        mixing,
        spill_decay,
        commute_decay,
    )


def solution(mesh):
    return jax.shard_map(
        body,
        mesh=mesh,
        in_specs=(
            P(None, "gy", "gx"),
            P("gy", "gx"),
            P("gy", "gx"),
            P("gy", "gx"),
            P(),
            P(),
            P(),
            P(),
            P(("gy", "gx"), None),
            P(("gy", "gx")),
            P(("gy", "gx")),
            P(("gy", "gx")),
        ),
        out_specs=(P(None, "gy", "gx"), P("gy", "gx")),
        check_vma=False,
    )
```

```python
import functools

import jax
import jax.numpy as jnp
from jax import lax
from jax.experimental import pallas as pl
from jax.experimental.pallas import tpu as pltpu
from jax.sharding import PartitionSpec as P

HALF = 64
ITERS = 3
SECTORS = 8
CAP = 8
BETA_WAGE = 0.3
FAR_SCALE = 0.125
ROWS = 128
COLS = 256
GROUPS = COLS // 16
PAIRS2 = SECTORS // 2
CHUNK = 16
STEPS = HALF // CHUNK
MESH = pl.DeviceIdType.MESH
F32 = jnp.float32
BF16 = jnp.bfloat16


def swap_blocks(values):
    values = [pltpu.roll(v, 16 * s, 1) if s else v for s, v in enumerate(values)]
    block = lax.broadcasted_iota(jnp.int32, values[0].shape, 1) // 16
    for d in (1, 2, 4):
        moved = (block & d) != 0
        values = [jnp.where(moved, values[(a + d) % 8], values[a]) for a in range(8)]
    values = [values[-g % 8] for g in range(8)]
    return [pltpu.roll(v, 128 - 16 * g, 1) if g else v for g, v in enumerate(values)]


def kernel(
    tiles_y,
    tiles_x,
    base_ref,
    resident_ref,
    floor_ref,
    bracket_ref,
    pairs_ref,
    scalar_ref,
    power_ref,
    rent_ref,
    ext,
    edge_out,
    edge_in,
    mid,
    near,
    labor,
    tap_row,
    band_row,
    band_col,
    band_edge,
    table,
    source_hot,
    slot_hot,
    place,
    far,
    one_out,
    one_in,
    two_out,
    two_in,
    sum_out,
    sum_in,
    total_out,
    total_in,
    rate_ref,
    income_ref,
    row_send,
    row_recv,
    edge_send,
    edge_recv,
    one_send,
    one_recv,
    two_send,
    two_recv,
    sum_send,
    sum_recv,
):
    my = lax.axis_index("gy")
    mx = lax.axis_index("gx")
    slots_x = tiles_y * CAP
    slots_y = tiles_x * CAP
    slots = tiles_x * slots_x
    far_pairs = pairs_ref.shape[1]

    barrier = pltpu.get_barrier_semaphore()

    def greet_x(j, carry):
        pl.semaphore_signal(
            barrier, inc=1, device_id=(my, lax.rem(mx + j, tiles_x)), device_id_type=MESH
        )
        return carry

    def greet_y(j, carry):
        pl.semaphore_signal(
            barrier, inc=1, device_id=(lax.rem(my + j, tiles_y), mx), device_id_type=MESH
        )
        return carry

    lax.fori_loop(1, tiles_x, greet_x, 0)
    lax.fori_loop(1, tiles_y, greet_y, 0)

    def row_copy(e, j, way):
        start = HALF if way == 0 else ROWS
        land = HALF + ROWS if way == 0 else 0
        target = my - 1 if way == 0 else my + 1
        step = pl.multiple_of(j * CHUNK, CHUNK)
        return pltpu.make_async_remote_copy(
            src_ref=ext.at[e, :, pl.ds(start + step, CHUNK), :],
            dst_ref=ext.at[e, :, pl.ds(land + step, CHUNK), :],
            send_sem=row_send.at[e, way],
            recv_sem=row_recv.at[e, way, j],
            device_id=(target, mx),
            device_id_type=MESH,
        )

    def row_drain(e, way):
        start = HALF if way == 0 else ROWS
        target = my - 1 if way == 0 else my + 1
        return pltpu.make_async_remote_copy(
            src_ref=ext.at[e, :, pl.ds(start, HALF), :],
            dst_ref=ext.at[e, :, pl.ds(start, HALF), :],
            send_sem=row_send.at[e, way],
            recv_sem=row_recv.at[e, way, 0],
            device_id=(target, mx),
            device_id_type=MESH,
        )

    can_row = (my > 0, my < tiles_y - 1)
    can_edge = (mx > 0, mx < tiles_x - 1)

    def send_rows(e, j):
        for way in range(2):

            @pl.when(can_row[way])
            def _():
                row_copy(e, j, way).start()

    def wait_rows(e):
        for way in range(2):

            @pl.when(can_row[1 - way])
            def _():
                for j in range(STEPS):
                    row_copy(e, j, way).wait_recv()

    def edge_copy(e, i, way):
        target = mx - 1 if way == 0 else mx + 1
        return pltpu.make_async_remote_copy(
            src_ref=edge_out.at[e, way, pl.ds(2 * i, 2)],
            dst_ref=edge_in.at[e, 1 - way, pl.ds(2 * i, 2)],
            send_sem=edge_send.at[e, way],
            recv_sem=edge_recv.at[e, way, i],
            device_id=(my, target),
            device_id_type=MESH,
        )

    def edge_drain(e, way):
        target = mx - 1 if way == 0 else mx + 1
        return pltpu.make_async_remote_copy(
            src_ref=edge_out.at[e, way],
            dst_ref=edge_in.at[e, 1 - way],
            send_sem=edge_send.at[e, way],
            recv_sem=edge_recv.at[e, way, 0],
            device_id=(my, target),
            device_id_type=MESH,
        )

    lane128 = lax.broadcasted_iota(jnp.int32, (ROWS, 128), 1)

    def rows_pass(e, kind):
        wait_rows(e)

        def one(half, carry):
            for k in range(2):
                i = 2 * half + k
                ends = []
                for s in (2 * i, 2 * i + 1):
                    passed = jnp.dot(
                        band_row[kind * SECTORS + s], ext[e, s], preferred_element_type=F32
                    )
                    mid[s] = passed.astype(BF16)
                    ends.append((passed[:, 0:128], passed[:, 128:256]))
                first, second = ends
                low = lane128 < HALF
                edge_out[e, 0, i] = jnp.where(
                    low, first[0], pltpu.roll(second[0], HALF, 1)
                ).astype(BF16)
                edge_out[e, 1, i] = jnp.where(
                    low, pltpu.roll(second[1], HALF, 1), first[1]
                ).astype(BF16)
            for way in range(2):

                @pl.when(can_edge[way])
                def _():
                    edge_copy(e, half, way).start()

            return carry

        lax.fori_loop(0, 2, one, 0)

    def columns_pass(e, kind, result):
        def one(half, carry):
            for way in range(2):

                @pl.when(can_edge[1 - way])
                def _():
                    edge_copy(e, half, way).wait_recv()

            for k in range(4):
                s = 4 * half + k
                i = 2 * half + k // 2
                b = kind * SECTORS + s
                value = jnp.dot(mid[s], band_col[b], preferred_element_type=F32)
                value += jnp.dot(
                    edge_in[e, 0, i], band_edge[b, 0:128, :], preferred_element_type=F32
                )
                value += jnp.dot(
                    edge_in[e, 1, i], band_edge[b, 128:256, :], preferred_element_type=F32
                )
                result[s] = value
            return carry

        lax.fori_loop(0, 2, one, 0)

    def make_bands(kind):
        u = lax.broadcasted_iota(jnp.int32, (COLS, COLS), 0)
        x = lax.broadcasted_iota(jnp.int32, (COLS, COLS), 1)
        inside = jnp.abs(u - x) <= 128

        def one(s, carry):
            b = kind * SECTORS + s
            line = jnp.broadcast_to(tap_row[pl.ds(b, 1), :], (ROWS, COLS))
            rows_band = pltpu.roll(line, 0, 1, stride=1, stride_axis=0)
            band_row[b] = rows_band.astype(BF16)
            circle = jnp.concatenate(
                [pltpu.roll(rows_band, COLS - HALF, 1), pltpu.roll(rows_band, HALF, 1)], axis=0
            )
            band_col[b] = jnp.where(inside, circle, 0.0).astype(BF16)
            rest = jnp.where(inside, 0.0, circle)
            even = jnp.concatenate([rest[128:256], rest[0:128]], axis=0)
            odd = jnp.concatenate(
                [rest[192:256], rest[128:192], rest[64:128], rest[0:64]], axis=0
            )
            band_edge[b] = jnp.where(lax.rem(s, 2) == 0, even, odd).astype(BF16)
            return carry

        lax.fori_loop(0, SECTORS, one, 0)

    def first_copy(a, x):
        return pltpu.make_async_remote_copy(
            src_ref=one_out.at[a, x],
            dst_ref=one_in.at[a, mx],
            send_sem=one_send.at[a],
            recv_sem=one_recv.at[a],
            device_id=(my, x),
            device_id_type=MESH,
        )

    def first_all(a):
        return pltpu.make_async_remote_copy(
            src_ref=one_out.at[a, pl.ds(0, tiles_x - 1)],
            dst_ref=one_in.at[a, pl.ds(0, tiles_x - 1)],
            send_sem=one_send.at[a],
            recv_sem=one_recv.at[a],
            device_id=(my, lax.rem(mx + 1, tiles_x)),
            device_id_type=MESH,
        )

    def second_copy(a, y):
        return pltpu.make_async_remote_copy(
            src_ref=two_out.at[a, y],
            dst_ref=two_in.at[a, my],
            send_sem=two_send.at[a],
            recv_sem=two_recv.at[a],
            device_id=(y, mx),
            device_id_type=MESH,
        )

    def second_all(a):
        return pltpu.make_async_remote_copy(
            src_ref=two_out.at[a, pl.ds(0, tiles_y - 1)],
            dst_ref=two_in.at[a, pl.ds(0, tiles_y - 1)],
            send_sem=two_send.at[a],
            recv_sem=two_recv.at[a],
            device_id=(lax.rem(my + 1, tiles_y), mx),
            device_id_type=MESH,
        )

    def start_first(a):
        def one(j, carry):
            first_copy(a, lax.rem(mx + j, tiles_x)).start()
            return carry

        lax.fori_loop(1, tiles_x, one, 0)
        one_in[a, mx] = one_out[a, mx]

    def pass_on(a):
        first_all(a).wait_recv()
        for i in range(tiles_x // 2):
            pieces = [
                one_in[a, 2 * i + k].astype(F32).reshape(tiles_y, CAP, 128) for k in range(2)
            ]
            two_out[a, :, 2 * i * CAP : 2 * (i + 1) * CAP, :] = jnp.concatenate(
                pieces, axis=1
            ).astype(BF16)

        def one(j, carry):
            second_copy(a, lax.rem(my + j, tiles_y)).start()
            return carry

        lax.fori_loop(1, tiles_y, one, 0)
        two_in[a, my] = two_out[a, my]

    def sum_copy(x):
        return pltpu.make_async_remote_copy(
            src_ref=sum_out,
            dst_ref=sum_in.at[mx],
            send_sem=sum_send.at[0],
            recv_sem=sum_recv.at[0],
            device_id=(my, x),
            device_id_type=MESH,
        )

    def total_copy(y):
        return pltpu.make_async_remote_copy(
            src_ref=total_out,
            dst_ref=total_in.at[my],
            send_sem=sum_send.at[1],
            recv_sem=sum_recv.at[1],
            device_id=(y, mx),
            device_id_type=MESH,
        )

    def sum_all():
        return pltpu.make_async_remote_copy(
            src_ref=sum_in.at[pl.ds(0, tiles_x - 1)],
            dst_ref=sum_in.at[pl.ds(0, tiles_x - 1)],
            send_sem=sum_send.at[0],
            recv_sem=sum_recv.at[0],
            device_id=(my, lax.rem(mx + 1, tiles_x)),
            device_id_type=MESH,
        )

    def total_all():
        return pltpu.make_async_remote_copy(
            src_ref=total_in.at[pl.ds(0, tiles_y - 1)],
            dst_ref=total_in.at[pl.ds(0, tiles_y - 1)],
            send_sem=sum_send.at[1],
            recv_sem=sum_recv.at[1],
            device_id=(lax.rem(my + 1, tiles_y), mx),
            device_id_type=MESH,
        )

    def unit(r, h):
        return pl.ds(r, CHUNK), pl.ds(pl.multiple_of(128 * h, 128), 128)

    def strip_rows(r, h, g):
        return pl.ds(pl.multiple_of((8 * h + g) * ROWS + r, CHUNK), CHUNK)

    def over_cells(work, sent, carry, wide):
        def step(j, carry):
            def one(u, carry):
                for k in range(wide):
                    number = u * wide + k
                    r = pl.multiple_of((number // 2) * HALF + j * CHUNK, CHUNK)
                    carry = work(r, number % 2, carry)
                return carry

            carry = one(0, carry) if wide == 4 else lax.fori_loop(0, 4 // wide, one, carry)
            if sent is not None:
                send_rows(sent, j)
            return carry

        return lax.fori_loop(0, STEPS, step, carry)

    def shares(it, r, h, wages, revenue):
        rows, lanes = unit(r, h)
        powers = [w * w * w for w in wages]
        inverse = 1.0 / sum(powers[1:], powers[0])
        people = resident_ref[rows, lanes]
        share = [p * inverse for p in powers]
        income = sum([q * w for q, w in zip(share[1:], wages[1:])], share[0] * wages[0])
        income_ref[it, rows, lanes] = income
        supply = [people * q for q in share]
        for s in range(SECTORS):
            ext[2 * it, s, pl.ds(HALF + r, CHUNK), lanes] = supply[s].astype(BF16)
        for g, strip in enumerate(swap_blocks(supply)):
            table[strip_rows(r, h, g), :] = strip.astype(BF16)
        gain = people * rate_ref[rows, lanes] * income
        return revenue + gain[0:8] + gain[8:16]

    def gather(a):
        picked = jnp.dot(source_hot[...], table[...], preferred_element_type=F32).astype(BF16)
        ordered = jnp.dot(slot_hot[...], picked, preferred_element_type=F32).astype(BF16)
        one_out[a] = ordered.reshape(tiles_x, slots_x, 128)

    zero = jnp.zeros((8, 128), F32)

    def first_cells(r, h, carry):
        people_sum, revenue = carry
        rows, lanes = unit(r, h)
        bracket = bracket_ref[rows, lanes]
        rate = jnp.zeros((CHUNK, 128), F32)
        for b in range(8):
            rate = jnp.where(bracket == b, scalar_ref[b], rate)
        rate_ref[rows, lanes] = rate
        people = resident_ref[rows, lanes]
        people_sum = people_sum + people[0:8] + people[8:16]
        wages = [base_ref[s, rows, lanes].astype(F32) for s in range(SECTORS)]
        return people_sum, shares(0, r, h, wages, revenue)

    pl.semaphore_wait(barrier, tiles_x - 1 + tiles_y - 1)
    people_sum, revenue0 = over_cells(first_cells, 0, (zero, zero), 4)

    across = pairs_ref[...].T
    dest_row, slot_base = pairs_ref[0:1, :], pairs_ref[1:2, :]
    earlier = lax.broadcasted_iota(jnp.int32, (far_pairs, far_pairs), 0) < (
        lax.broadcasted_iota(jnp.int32, (far_pairs, far_pairs), 1)
    )
    same = (across[:, 0:1] == dest_row) & earlier
    rank = jnp.sum(jnp.where(same, 1.0, 0.0), axis=0, keepdims=True)
    slot_of = (slot_base + rank).astype(jnp.int32)
    slot_ids = lax.broadcasted_iota(jnp.int32, (slots, far_pairs), 0)
    slot_hot[...] = jnp.where(slot_ids == slot_of, 1.0, 0.0).astype(BF16)
    strip_ids = lax.broadcasted_iota(jnp.int32, (far_pairs, GROUPS * ROWS), 1)
    source_hot[...] = jnp.where(
        strip_ids == across[:, 2:3].astype(jnp.int32), 1.0, 0.0
    ).astype(BF16)
    one_out[ITERS] = (
        jnp.dot(slot_hot[...], across.astype(BF16), preferred_element_type=F32)
        .astype(BF16)
        .reshape(tiles_x, slots_x, 128)
    )
    start_first(ITERS)
    gather(0)
    start_first(0)

    @pl.when(my == 0)
    def _():
        ext[:, :, 0:HALF, :] = jnp.zeros((2 * ITERS, SECTORS, HALF, COLS), BF16)

    @pl.when(my == tiles_y - 1)
    def _():
        ext[:, :, HALF + ROWS :, :] = jnp.zeros((2 * ITERS, SECTORS, HALF, COLS), BF16)

    @pl.when(mx == 0)
    def _():
        edge_in[:, 0] = jnp.zeros((2 * ITERS, PAIRS2, ROWS, 128), BF16)

    @pl.when(mx == tiles_x - 1)
    def _():
        edge_in[:, 1] = jnp.zeros((2 * ITERS, PAIRS2, ROWS, 128), BF16)

    sector = lax.broadcasted_iota(jnp.int32, (2 * SECTORS, COLS), 0)
    tap = lax.broadcasted_iota(jnp.int32, (2 * SECTORS, COLS), 1)
    decay = jnp.zeros((2 * SECTORS, COLS), F32)
    for s in range(SECTORS):
        decay = jnp.where(sector == s, scalar_ref[8 + s], decay)
        decay = jnp.where(sector == SECTORS + s, scalar_ref[16 + s], decay)
    offset = jnp.abs(tap - HALF).astype(F32) / HALF
    unscaled = jnp.where(tap <= 2 * HALF, jnp.exp(-decay * offset), 0.0)
    tap_row[...] = (unscaled / jnp.sum(unscaled, axis=1, keepdims=True)).astype(BF16).astype(F32)
    make_bands(0)

    pass_on(ITERS)

    def build_place():
        second_all(ITERS).wait_recv()
        routing = two_in[ITERS].reshape(slots, 128)
        line = lax.broadcasted_iota(jnp.int32, (16, 128), 0)
        lane = lax.broadcasted_iota(jnp.int32, (16, 128), 1)
        pick = jnp.where((line == 0) & (lane == 3), 1.0, 0.0)
        pick = jnp.where((line == 0) & (lane == 4), float(ROWS), pick)
        pick = jnp.where((line == 1) & (lane == 5), 1.0, pick).astype(BF16)
        found = lax.dot_general(
            pick, routing, (((1,), (1,)), ((), ())), preferred_element_type=F32
        )
        where_to, weight = found[0:1, :].astype(jnp.int32), found[1:2, :]

        def one(g, carry):
            strip = g * ROWS + lax.broadcasted_iota(jnp.int32, (ROWS, slots), 0)
            place[pl.ds(pl.multiple_of(g * ROWS, ROWS), ROWS), :] = jnp.where(
                strip == where_to, weight, 0.0
            ).astype(BF16)
            return carry

        lax.fori_loop(0, GROUPS, one, 0)

    revenues = [revenue0]
    for it in range(ITERS):
        if it > 0:
            gather(it)
            start_first(it)
        if it == ITERS - 1:
            line = lax.broadcasted_iota(jnp.int32, (8, 128), 0)
            parts = zero
            for k, part in enumerate([people_sum] + revenues):
                parts = jnp.where(line == k, jnp.sum(part, axis=0, keepdims=True), parts)
            sum_out[...] = parts

            def start_sum(j, carry):
                sum_copy(lax.rem(mx + j, tiles_x)).start()
                return carry

            lax.fori_loop(1, tiles_x, start_sum, 0)
            sum_in[mx] = parts
        rows_pass(2 * it, 0)
        pass_on(it)
        if it == ITERS - 1:
            sum_all().wait_recv()
            halfway = jnp.sum(sum_in[...], axis=0)
            total_out[...] = halfway

            def start_total(j, carry):
                total_copy(lax.rem(my + j, tiles_y)).start()
                return carry

            lax.fori_loop(1, tiles_y, start_total, 0)
            total_in[my] = halfway
        columns_pass(2 * it, 0, near)
        if it == 0:
            build_place()
        second_all(it).wait_recv()
        far[...] = jnp.dot(
            place[...], two_in[it].reshape(slots, 128), preferred_element_type=F32
        )

        def labor_cells(r, h, carry):
            rows, lanes = unit(r, h)
            strips = [far[strip_rows(r, h, g), :] for g in range(8)]
            for s, flow in enumerate(swap_blocks(strips)):
                value = near[s, rows, lanes] + FAR_SCALE * flow
                labor[s, rows, lanes] = value
                ext[2 * it + 1, s, pl.ds(HALF + r, CHUNK), lanes] = value.astype(BF16)
            return carry

        over_cells(labor_cells, 2 * it + 1, 0, 4)
        if it == 0:
            make_bands(1)
        if it == ITERS - 1:
            total_all().wait_recv()
            sums = jnp.sum(jnp.sum(total_in[...], axis=0), axis=1, keepdims=True)
            people_all = sums[0:1, 0:1]
            transfers = [sums[1 + k : 2 + k, 0:1] / people_all for k in range(ITERS)]

            def rent_chunk(c, carry):
                rows = pl.ds(pl.multiple_of(c * CHUNK, CHUNK), CHUNK)
                keep = 1.0 - rate_ref[rows, :]
                people, space = resident_ref[rows, :], floor_ref[rows, :]
                ratio = people / space
                square = None
                for k in range(ITERS):
                    net = keep * income_ref[k, rows, :] + transfers[k]
                    level = ratio if square is None else jnp.sqrt(square) * ratio
                    square = level * net
                rent_ref[rows, :] = square
                return carry

            lax.fori_loop(0, ROWS // CHUNK, rent_chunk, 0)
        rows_pass(2 * it + 1, 1)
        columns_pass(2 * it + 1, 1, near)

        def wage_cells(r, h, revenue):
            rows, lanes = unit(r, h)
            logs = [jnp.log(1.0 + near[s, rows, lanes]) for s in range(SECTORS)]
            wages = []
            for s in range(SECTORS):
                power = -BETA_WAGE * jnp.log(1.0 + labor[s, rows, lanes])
                for t in range(SECTORS):
                    power = power + scalar_ref[24 + SECTORS * s + t] * logs[t]
                if it == ITERS - 1:
                    power_ref[s, rows, lanes] = power
                else:
                    wages.append(base_ref[s, rows, lanes].astype(F32) * jnp.exp(power))
            if it < ITERS - 1:
                revenue = shares(it + 1, r, h, wages, revenue)
            return revenue

        sent = 2 * it + 2 if it < ITERS - 1 else None
        revenues.append(over_cells(wage_cells, sent, zero, 2))

    for e in range(2 * ITERS):
        for way in range(2):

            @pl.when(can_row[way])
            def _():
                row_drain(e, way).wait_send()

            @pl.when(can_edge[way])
            def _():
                edge_drain(e, way).wait_send()

    for a in range(ITERS + 1):
        first_all(a).wait_send()
        second_all(a).wait_send()
    sum_all().wait_send()
    total_all().wait_send()


def body(
    base_prod,
    resident,
    floor_space,
    bracket,
    tax_rate,
    mixing,
    spill_decay,
    commute_decay,
    pair_dest,
    pair_src,
    pair_dst,
    pair_count,
):
    tiles_y = lax.axis_size("gy")
    tiles_x = lax.axis_size("gx")
    slots = tiles_y * tiles_x * CAP
    far_pairs = pair_src.shape[0]
    dest = pair_dest[:, 0]
    pairs = jnp.stack(
        [
            dest,
            (dest % tiles_x) * (tiles_y * CAP) + (dest // tiles_x) * CAP,
            (pair_src % GROUPS) * ROWS + pair_src // GROUPS,
            pair_dst // GROUPS,
            pair_dst % GROUPS,
            pair_count,
        ],
        axis=0,
    ).astype(F32)
    pairs = jnp.pad(pairs, ((0, 122), (0, 0)))
    vmem = pl.BlockSpec(memory_space=pltpu.VMEM)
    smem = pl.BlockSpec(memory_space=pltpu.SMEM)
    exchanges = 2 * ITERS
    dma = pltpu.SemaphoreType.DMA
    scalars = jnp.concatenate([tax_rate, commute_decay, spill_decay, mixing.reshape(-1)])
    power, square = pl.pallas_call(
        functools.partial(kernel, tiles_y, tiles_x),
        out_shape=(
            jax.ShapeDtypeStruct(base_prod.shape, F32),
            jax.ShapeDtypeStruct(resident.shape, F32),
        ),
        in_specs=[vmem] * 5 + [smem],
        out_specs=(vmem, vmem),
        scratch_shapes=[
            pltpu.VMEM((exchanges, SECTORS, ROWS + 2 * HALF, COLS), BF16),
            pltpu.VMEM((exchanges, 2, PAIRS2, ROWS, 128), BF16),
            pltpu.VMEM((exchanges, 2, PAIRS2, ROWS, 128), BF16),
            pltpu.VMEM((SECTORS, ROWS, COLS), BF16),
            pltpu.VMEM((SECTORS, ROWS, COLS), F32),
            pltpu.VMEM((SECTORS, ROWS, COLS), F32),
            pltpu.VMEM((2 * SECTORS, COLS), F32),
            pltpu.VMEM((2 * SECTORS, ROWS, COLS), BF16),
            pltpu.VMEM((2 * SECTORS, COLS, COLS), BF16),
            pltpu.VMEM((2 * SECTORS, COLS, COLS), BF16),
            pltpu.VMEM((GROUPS * ROWS, 128), BF16),
            pltpu.VMEM((far_pairs, GROUPS * ROWS), BF16),
            pltpu.VMEM((slots, far_pairs), BF16),
            pltpu.VMEM((GROUPS * ROWS, slots), BF16),
            pltpu.VMEM((GROUPS * ROWS, 128), F32),
            pltpu.VMEM((ITERS + 1, tiles_x, tiles_y * CAP, 128), BF16),
            pltpu.VMEM((ITERS + 1, tiles_x, tiles_y * CAP, 128), BF16),
            pltpu.VMEM((ITERS + 1, tiles_y, tiles_x * CAP, 128), BF16),
            pltpu.VMEM((ITERS + 1, tiles_y, tiles_x * CAP, 128), BF16),
            pltpu.VMEM((8, 128), F32),
            pltpu.VMEM((tiles_x, 8, 128), F32),
            pltpu.VMEM((8, 128), F32),
            pltpu.VMEM((tiles_y, 8, 128), F32),
            pltpu.VMEM((ROWS, COLS), F32),
            pltpu.VMEM((ITERS, ROWS, COLS), F32),
            dma((exchanges, 2)),
            dma((exchanges, 2, STEPS)),
            dma((exchanges, 2)),
            dma((exchanges, 2, 2)),
            dma((ITERS + 1,)),
            dma((ITERS + 1,)),
            dma((ITERS + 1,)),
            dma((ITERS + 1,)),
            dma((2,)),
            dma((2,)),
        ],
        compiler_params=pltpu.CompilerParams(
            collective_id=0, has_side_effects=True, vmem_limit_bytes=60 * 1024 * 1024
        ),
    )(
        base_prod,
        resident,
        floor_space,
        bracket,
        pairs,
        scalars,
    )
    return base_prod.astype(F32) * jnp.exp(power), jnp.sqrt(square)


def solution(mesh):
    return jax.shard_map(
        body,
        mesh=mesh,
        in_specs=(
            P(None, "gy", "gx"),
            P("gy", "gx"),
            P("gy", "gx"),
            P("gy", "gx"),
            P(),
            P(),
            P(),
            P(),
            P(("gy", "gx"), None),
            P(("gy", "gx")),
            P(("gy", "gx")),
            P(("gy", "gx")),
        ),
        out_specs=(P(None, "gy", "gx"), P("gy", "gx")),
        check_vma=False,
    )
```

```python
import functools

import jax
import jax.numpy as jnp
from jax import lax
from jax.experimental import pallas as pl
from jax.experimental.pallas import tpu as pltpu
from jax.sharding import PartitionSpec as P

HALF = 64
ITERS = 3
SECTORS = 8
CAP = 8
BETA_WAGE = 0.3
FAR_SCALE = 0.125
ROWS = 128
COLS = 256
GROUPS = COLS // 16
PAIRS2 = SECTORS // 2
CHUNK = 16
STEPS = HALF // CHUNK
MESH = pl.DeviceIdType.MESH
F32 = jnp.float32
BF16 = jnp.bfloat16


def swap_blocks(values):
    values = [pltpu.roll(v, 16 * s, 1) if s else v for s, v in enumerate(values)]
    block = lax.broadcasted_iota(jnp.int32, values[0].shape, 1) // 16
    for d in (1, 2, 4):
        moved = (block & d) != 0
        values = [jnp.where(moved, values[(a + d) % 8], values[a]) for a in range(8)]
    values = [values[-g % 8] for g in range(8)]
    return [pltpu.roll(v, 128 - 16 * g, 1) if g else v for g, v in enumerate(values)]


def kernel(
    tiles_y,
    tiles_x,
    base_ref,
    resident_ref,
    floor_ref,
    bracket_ref,
    dest_ref,
    src_ref,
    dst_ref,
    count_ref,
    tax_any,
    commute_any,
    spill_any,
    mixing_any,
    power_ref,
    rent_ref,
    ext,
    edge_out,
    edge_in,
    mid,
    near,
    labor,
    tap_row,
    band_row,
    band_col,
    band_edge,
    table,
    source_hot,
    slot_hot,
    place,
    far,
    one_out,
    one_in,
    two_out,
    two_in,
    sum_out,
    sum_in,
    total_out,
    total_in,
    rate_ref,
    income_ref,
    last_in,
    tax_ref,
    commute_ref,
    spill_ref,
    mixing_ref,
    load_sem,
    row_send,
    row_recv,
    edge_send,
    edge_recv,
    one_send,
    one_recv,
    two_send,
    two_recv,
    sum_send,
    sum_recv,
):
    my = lax.axis_index("gy")
    mx = lax.axis_index("gx")
    chips_x = tiles_x // 2
    chips = tiles_y * chips_x
    core = lax.rem(mx, 2)
    chip_x = mx // 2
    sibling = mx + 1 - 2 * core
    beyond = lax.rem(mx + 2 * core - 1 + tiles_x, tiles_x)
    mine = my * chips_x + chip_x
    slots = tiles_y * tiles_x * CAP
    far_pairs = dest_ref.shape[1]

    loads = [
        pltpu.make_async_copy(source, target, load_sem.at[k])
        for k, (source, target) in enumerate(
            (
                (tax_any, tax_ref),
                (commute_any, commute_ref),
                (spill_any, spill_ref),
                (mixing_any, mixing_ref),
            )
        )
    ]
    for load in loads:
        load.start()

    barrier = pltpu.get_barrier_semaphore()

    def chip_at(j):
        return lax.rem(my + j // chips_x, tiles_y), lax.rem(chip_x + lax.rem(j, chips_x), chips_x)

    def greet(y, x):
        pl.semaphore_signal(barrier, inc=1, device_id=(y, x), device_id_type=MESH)

    def greet_chip(j, carry):
        y, x = chip_at(j)
        greet(y, 2 * x + core)
        return carry

    greet(my, sibling)
    greet(my, beyond)
    lax.fori_loop(1, chips, greet_chip, 0)

    def row_copy(e, j, way):
        start = HALF if way == 0 else ROWS
        land = HALF + ROWS if way == 0 else 0
        target = my - 1 if way == 0 else my + 1
        step = pl.multiple_of(j * CHUNK, CHUNK)
        return pltpu.make_async_remote_copy(
            src_ref=ext.at[e, :, pl.ds(start + step, CHUNK), :],
            dst_ref=ext.at[e, :, pl.ds(land + step, CHUNK), :],
            send_sem=row_send.at[e, way],
            recv_sem=row_recv.at[e, way, j],
            device_id=(target, mx),
            device_id_type=MESH,
        )

    def row_drain(e, way):
        start = HALF if way == 0 else ROWS
        target = my - 1 if way == 0 else my + 1
        return pltpu.make_async_remote_copy(
            src_ref=ext.at[e, :, pl.ds(start, HALF), :],
            dst_ref=ext.at[e, :, pl.ds(start, HALF), :],
            send_sem=row_send.at[e, way],
            recv_sem=row_recv.at[e, way, 0],
            device_id=(target, mx),
            device_id_type=MESH,
        )

    can_row = (my > 0, my < tiles_y - 1)
    can_edge = (mx > 0, mx < tiles_x - 1)

    def send_rows(e, j):
        for way in range(2):

            @pl.when(can_row[way])
            def _():
                row_copy(e, j, way).start()

    def wait_rows(e):
        for way in range(2):

            @pl.when(can_row[1 - way])
            def _():
                for j in range(STEPS):
                    row_copy(e, j, way).wait_recv()

    def edge_copy(e, i, way):
        target = mx - 1 if way == 0 else mx + 1
        return pltpu.make_async_remote_copy(
            src_ref=edge_out.at[e, way, pl.ds(2 * i, 2)],
            dst_ref=edge_in.at[e, 1 - way, pl.ds(2 * i, 2)],
            send_sem=edge_send.at[e, way],
            recv_sem=edge_recv.at[e, way, i],
            device_id=(my, target),
            device_id_type=MESH,
        )

    def edge_drain(e, way):
        target = mx - 1 if way == 0 else mx + 1
        return pltpu.make_async_remote_copy(
            src_ref=edge_out.at[e, way],
            dst_ref=edge_in.at[e, 1 - way],
            send_sem=edge_send.at[e, way],
            recv_sem=edge_recv.at[e, way, 0],
            device_id=(my, target),
            device_id_type=MESH,
        )

    lane128 = lax.broadcasted_iota(jnp.int32, (ROWS, 128), 1)

    def rows_pass(e, kind):
        wait_rows(e)

        def one(half, carry):
            for k in range(2):
                i = 2 * half + k
                ends = []
                for s in (2 * i, 2 * i + 1):
                    passed = jnp.dot(
                        band_row[kind * SECTORS + s], ext[e, s], preferred_element_type=F32
                    )
                    mid[s] = passed.astype(BF16)
                    ends.append((passed[:, 0:128], passed[:, 128:256]))
                first, second = ends
                low = lane128 < HALF
                edge_out[e, 0, i] = jnp.where(
                    low, first[0], pltpu.roll(second[0], HALF, 1)
                ).astype(BF16)
                edge_out[e, 1, i] = jnp.where(
                    low, pltpu.roll(second[1], HALF, 1), first[1]
                ).astype(BF16)
            for way in range(2):

                @pl.when(can_edge[way])
                def _():
                    edge_copy(e, half, way).start()

            return carry

        lax.fori_loop(0, 2, one, 0)

    def columns_pass(e, kind, result):
        def one(half, carry):
            for way in range(2):

                @pl.when(can_edge[1 - way])
                def _():
                    edge_copy(e, half, way).wait_recv()

            for k in range(4):
                s = 4 * half + k
                i = 2 * half + k // 2
                b = kind * SECTORS + s
                value = jnp.dot(mid[s], band_col[b], preferred_element_type=F32)
                value += jnp.dot(
                    edge_in[e, 0, i], band_edge[b, 0:128, :], preferred_element_type=F32
                )
                value += jnp.dot(
                    edge_in[e, 1, i], band_edge[b, 128:256, :], preferred_element_type=F32
                )
                result[s] = value
            return carry

        lax.fori_loop(0, 2, one, 0)

    def make_bands(kind):
        u = lax.broadcasted_iota(jnp.int32, (COLS, COLS), 0)
        x = lax.broadcasted_iota(jnp.int32, (COLS, COLS), 1)
        inside = jnp.abs(u - x) <= 128

        def one(s, carry):
            b = kind * SECTORS + s
            line = jnp.broadcast_to(tap_row[pl.ds(b, 1), :], (ROWS, COLS))
            rows_band = pltpu.roll(line, 0, 1, stride=1, stride_axis=0)
            band_row[b] = rows_band.astype(BF16)
            circle = jnp.concatenate(
                [pltpu.roll(rows_band, COLS - HALF, 1), pltpu.roll(rows_band, HALF, 1)], axis=0
            )
            band_col[b] = jnp.where(inside, circle, 0.0).astype(BF16)
            rest = jnp.where(inside, 0.0, circle)
            even = jnp.concatenate([rest[128:256], rest[0:128]], axis=0)
            odd = jnp.concatenate(
                [rest[192:256], rest[128:192], rest[64:128], rest[0:64]], axis=0
            )
            band_edge[b] = jnp.where(lax.rem(s, 2) == 0, even, odd).astype(BF16)
            return carry

        lax.fori_loop(0, SECTORS, one, 0)

    def first_copy(a, y, x):
        return pltpu.make_async_remote_copy(
            src_ref=one_out.at[a, y * chips_x + x],
            dst_ref=one_in.at[a, mine],
            send_sem=one_send.at[a],
            recv_sem=one_recv.at[a],
            device_id=(y, 2 * x + core),
            device_id_type=MESH,
        )

    def first_all(a):
        return pltpu.make_async_remote_copy(
            src_ref=one_out.at[a, pl.ds(0, chips - 1)],
            dst_ref=one_in.at[a, pl.ds(0, chips - 1)],
            send_sem=one_send.at[a],
            recv_sem=one_recv.at[a],
            device_id=(my, sibling),
            device_id_type=MESH,
        )

    def second_copy(a):
        return pltpu.make_async_remote_copy(
            src_ref=two_out.at[a],
            dst_ref=two_in.at[a, 1],
            send_sem=two_send.at[a],
            recv_sem=two_recv.at[a],
            device_id=(my, sibling),
            device_id_type=MESH,
        )

    def start_first(a):
        def one(j, carry):
            first_copy(a, *chip_at(j)).start()
            return carry

        lax.fori_loop(1, chips, one, 0)
        one_in[a, mine] = one_out[a, mine]

    def pass_on(a):
        first_all(a).wait_recv()
        parts = one_in[a].astype(F32).reshape(chips, 2, CAP, 128)
        low, high = parts[:, 0], parts[:, 1]
        two_out[a] = jnp.where(core == 0, high, low).reshape(chips * CAP, 128).astype(BF16)
        second_copy(a).start()
        two_in[a, 0] = jnp.where(core == 0, low, high).reshape(chips * CAP, 128).astype(BF16)

    def sum_copy(x):
        return pltpu.make_async_remote_copy(
            src_ref=sum_out,
            dst_ref=sum_in.at[chip_x],
            send_sem=sum_send.at[0],
            recv_sem=sum_recv.at[0],
            device_id=(my, 2 * x + core),
            device_id_type=MESH,
        )

    def total_copy(y):
        return pltpu.make_async_remote_copy(
            src_ref=total_out,
            dst_ref=total_in.at[my],
            send_sem=sum_send.at[1],
            recv_sem=sum_recv.at[1],
            device_id=(y, mx),
            device_id_type=MESH,
        )

    def sum_all():
        return pltpu.make_async_remote_copy(
            src_ref=sum_in.at[pl.ds(0, chips_x - 1)],
            dst_ref=sum_in.at[pl.ds(0, chips_x - 1)],
            send_sem=sum_send.at[0],
            recv_sem=sum_recv.at[0],
            device_id=(my, sibling),
            device_id_type=MESH,
        )

    def total_all():
        return pltpu.make_async_remote_copy(
            src_ref=total_in.at[pl.ds(0, tiles_y - 1)],
            dst_ref=total_in.at[pl.ds(0, tiles_y - 1)],
            send_sem=sum_send.at[1],
            recv_sem=sum_recv.at[1],
            device_id=(my, sibling),
            device_id_type=MESH,
        )

    def last_copy():
        return pltpu.make_async_remote_copy(
            src_ref=last_in.at[0],
            dst_ref=last_in.at[1],
            send_sem=sum_send.at[2],
            recv_sem=sum_recv.at[2],
            device_id=(my, sibling),
            device_id_type=MESH,
        )

    def unit(r, h):
        return pl.ds(r, CHUNK), pl.ds(pl.multiple_of(128 * h, 128), 128)

    def strip_rows(r, h, g):
        return pl.ds(pl.multiple_of((8 * h + g) * ROWS + r, CHUNK), CHUNK)

    def over_cells(work, sent, carry, wide):
        def step(j, carry):
            def one(u, carry):
                for k in range(wide):
                    number = u * wide + k
                    r = pl.multiple_of((number // 2) * HALF + j * CHUNK, CHUNK)
                    carry = work(r, number % 2, carry)
                return carry

            carry = one(0, carry) if wide == 4 else lax.fori_loop(0, 4 // wide, one, carry)
            if sent is not None:
                send_rows(sent, j)
            return carry

        return lax.fori_loop(0, STEPS, step, carry)

    def shares(it, r, h, wages, revenue):
        rows, lanes = unit(r, h)
        powers = [w * w * w for w in wages]
        inverse = 1.0 / sum(powers[1:], powers[0])
        people = resident_ref[rows, lanes]
        share = [p * inverse for p in powers]
        income = sum([q * w for q, w in zip(share[1:], wages[1:])], share[0] * wages[0])
        income_ref[it, rows, lanes] = income
        supply = [people * q for q in share]
        for s in range(SECTORS):
            ext[2 * it, s, pl.ds(HALF + r, CHUNK), lanes] = supply[s].astype(BF16)
        for g, strip in enumerate(swap_blocks(supply)):
            table[strip_rows(r, h, g), :] = strip.astype(BF16)
        gain = people * rate_ref[rows, lanes] * income
        return revenue + gain[0:8] + gain[8:16]

    def gather(a):
        picked = jnp.dot(source_hot[...], table[...], preferred_element_type=F32).astype(BF16)
        ordered = jnp.dot(slot_hot[...], picked, preferred_element_type=F32).astype(BF16)
        one_out[a] = ordered.reshape(chips, 2 * CAP, 128)

    zero = jnp.zeros((8, 128), F32)

    def first_cells(r, h, carry):
        people_sum, revenue = carry
        rows, lanes = unit(r, h)
        bracket = bracket_ref[rows, lanes]
        rate = jnp.zeros((CHUNK, 128), F32)
        for b in range(8):
            rate = jnp.where(bracket == b, tax_ref[b], rate)
        rate_ref[rows, lanes] = rate
        people = resident_ref[rows, lanes]
        people_sum = people_sum + people[0:8] + people[8:16]
        wages = [base_ref[s, rows, lanes].astype(F32) for s in range(SECTORS)]
        return people_sum, shares(0, r, h, wages, revenue)

    for load in loads:
        load.wait()
    people_sum, revenue0 = over_cells(first_cells, None, (zero, zero), 4)
    pl.semaphore_wait(barrier, chips + 1)
    for j in range(STEPS):
        send_rows(0, j)

    line = lax.broadcasted_iota(jnp.int32, (8, far_pairs), 0)
    source, target = src_ref[...], dst_ref[...]
    row, group = target >> 4, target & 15
    fields = [
        dest_ref[...],
        (source & 15) * ROWS + (source >> 4),
        ((((row >> 4) & 3) * 2 + (row >> 6)) * GROUPS) + group,
        row & 15,
        count_ref[...],
    ]
    pairs = jnp.zeros((8, far_pairs), jnp.int32)
    for k, field in enumerate(fields):
        pairs = jnp.where(line == k, field, pairs)
    pairs = pairs.astype(F32)
    across = jnp.concatenate([pairs, jnp.zeros((120, far_pairs), F32)], axis=0).T
    dest_row = pairs[0:1, :]
    earlier = lax.broadcasted_iota(jnp.int32, (far_pairs, far_pairs), 0) < (
        lax.broadcasted_iota(jnp.int32, (far_pairs, far_pairs), 1)
    )
    same = (across[:, 0:1] == dest_row) & earlier
    rank = jnp.sum(jnp.where(same, 1.0, 0.0), axis=0, keepdims=True)
    slot_of = (dest_row * CAP + rank).astype(jnp.int32)
    slot_ids = lax.broadcasted_iota(jnp.int32, (slots, far_pairs), 0)
    slot_hot[...] = jnp.where(slot_ids == slot_of, 1.0, 0.0).astype(BF16)
    strip_ids = lax.broadcasted_iota(jnp.int32, (far_pairs, GROUPS * ROWS), 1)
    source_hot[...] = jnp.where(
        strip_ids == across[:, 1:2].astype(jnp.int32), 1.0, 0.0
    ).astype(BF16)
    one_out[ITERS] = (
        jnp.dot(slot_hot[...], across.astype(BF16), preferred_element_type=F32)
        .astype(BF16)
        .reshape(chips, 2 * CAP, 128)
    )
    start_first(ITERS)
    gather(0)
    start_first(0)

    @pl.when(my == 0)
    def _():
        ext[:, :, 0:HALF, :] = jnp.zeros((2 * ITERS, SECTORS, HALF, COLS), BF16)

    @pl.when(my == tiles_y - 1)
    def _():
        ext[:, :, HALF + ROWS :, :] = jnp.zeros((2 * ITERS, SECTORS, HALF, COLS), BF16)

    @pl.when(mx == 0)
    def _():
        edge_in[:, 0] = jnp.zeros((2 * ITERS, PAIRS2, ROWS, 128), BF16)

    @pl.when(mx == tiles_x - 1)
    def _():
        edge_in[:, 1] = jnp.zeros((2 * ITERS, PAIRS2, ROWS, 128), BF16)

    sector = lax.broadcasted_iota(jnp.int32, (2 * SECTORS, COLS), 0)
    tap = lax.broadcasted_iota(jnp.int32, (2 * SECTORS, COLS), 1)
    decay = jnp.zeros((2 * SECTORS, COLS), F32)
    for s in range(SECTORS):
        decay = jnp.where(sector == s, commute_ref[s], decay)
        decay = jnp.where(sector == SECTORS + s, spill_ref[s], decay)
    offset = jnp.abs(tap - HALF).astype(F32) / HALF
    unscaled = jnp.where(tap <= 2 * HALF, jnp.exp(-decay * offset), 0.0)
    tap_row[...] = (unscaled / jnp.sum(unscaled, axis=1, keepdims=True)).astype(BF16).astype(F32)
    make_bands(0)

    pass_on(ITERS)

    def build_place():
        second_copy(ITERS).wait_recv()
        routing = two_in[ITERS].reshape(slots, 128)
        line = lax.broadcasted_iota(jnp.int32, (16, 128), 0)
        lane = lax.broadcasted_iota(jnp.int32, (16, 128), 1)
        pick = jnp.where((line == 0) & (lane == 2), float(CHUNK), 0.0)
        pick = jnp.where((line == 0) & (lane == 3), 1.0, pick)
        pick = jnp.where((line == 1) & (lane == 4), 1.0, pick).astype(BF16)
        found = lax.dot_general(
            pick, routing, (((1,), (1,)), ((), ())), preferred_element_type=F32
        )
        where_to, weight = found[0:1, :].astype(jnp.int32), found[1:2, :]

        def one(g, carry):
            strip = g * ROWS + lax.broadcasted_iota(jnp.int32, (ROWS, slots), 0)
            place[pl.ds(pl.multiple_of(g * ROWS, ROWS), ROWS), :] = jnp.where(
                strip == where_to, weight, 0.0
            ).astype(BF16)
            return carry

        lax.fori_loop(0, GROUPS, one, 0)

    revenues = [revenue0]
    for it in range(ITERS):
        if it > 0:
            gather(it)
            start_first(it)
        if it == ITERS - 1:
            line = lax.broadcasted_iota(jnp.int32, (8, 128), 0)
            parts = zero
            for k, part in enumerate([people_sum] + revenues):
                parts = jnp.where(line == k, jnp.sum(part, axis=0, keepdims=True), parts)
            sum_out[...] = parts

            def start_sum(j, carry):
                sum_copy(lax.rem(chip_x + j, chips_x)).start()
                return carry

            lax.fori_loop(1, chips_x, start_sum, 0)
            sum_in[chip_x] = parts
        rows_pass(2 * it, 0)
        pass_on(it)
        if it == ITERS - 1:
            sum_all().wait_recv()
            halfway = jnp.sum(sum_in[...], axis=0)
            total_out[...] = halfway

            def start_total(j, carry):
                total_copy(lax.rem(my + j, tiles_y)).start()
                return carry

            lax.fori_loop(1, tiles_y, start_total, 0)
            total_in[my] = halfway
        columns_pass(2 * it, 0, near)
        if it == ITERS - 1:
            total_all().wait_recv()
            last_in[0] = jnp.sum(total_in[...], axis=0)
            last_copy().start()
        if it == 0:
            build_place()
        second_copy(it).wait_recv()

        def labor_step(j, carry):
            block = 2 * GROUPS * CHUNK
            far[...] = jnp.dot(
                place[pl.ds(pl.multiple_of(j * block, block), block), :],
                two_in[it].reshape(slots, 128),
                preferred_element_type=F32,
            )
            for number in range(4):
                way, h = number // 2, number % 2
                r = pl.multiple_of(way * HALF + j * CHUNK, CHUNK)
                rows, lanes = unit(r, h)
                first = (way * GROUPS + 8 * h) * CHUNK
                strips = [far[first + CHUNK * g : first + CHUNK * (g + 1), :] for g in range(8)]
                for s, flow in enumerate(swap_blocks(strips)):
                    value = near[s, rows, lanes] + FAR_SCALE * flow
                    labor[s, rows, lanes] = value
                    ext[2 * it + 1, s, pl.ds(HALF + r, CHUNK), lanes] = value.astype(BF16)
            send_rows(2 * it + 1, j)
            return carry

        lax.fori_loop(0, STEPS, labor_step, 0)
        if it == 0:
            make_bands(1)
        if it == ITERS - 1:
            last_copy().wait_recv()
            sums = jnp.sum(last_in[0] + last_in[1], axis=1, keepdims=True)
            people_all = sums[0:1, 0:1]
            transfers = [sums[1 + k : 2 + k, 0:1] / people_all for k in range(ITERS)]

            def rent_chunk(c, carry):
                rows = pl.ds(pl.multiple_of(c * CHUNK, CHUNK), CHUNK)
                keep = 1.0 - rate_ref[rows, :]
                people, space = resident_ref[rows, :], floor_ref[rows, :]
                ratio = people / space
                square = None
                for k in range(ITERS):
                    net = keep * income_ref[k, rows, :] + transfers[k]
                    level = ratio if square is None else jnp.sqrt(square) * ratio
                    square = level * net
                rent_ref[rows, :] = square
                return carry

            lax.fori_loop(0, ROWS // CHUNK, rent_chunk, 0)
        rows_pass(2 * it + 1, 1)
        columns_pass(2 * it + 1, 1, near)

        def wage_cells(r, h, revenue):
            rows, lanes = unit(r, h)
            logs = [jnp.log(1.0 + near[s, rows, lanes]) for s in range(SECTORS)]
            wages = []
            for s in range(SECTORS):
                power = -BETA_WAGE * jnp.log(1.0 + labor[s, rows, lanes])
                for t in range(SECTORS):
                    power = power + mixing_ref[s, t] * logs[t]
                if it == ITERS - 1:
                    power_ref[s, rows, lanes] = power
                else:
                    wages.append(base_ref[s, rows, lanes].astype(F32) * jnp.exp(power))
            if it < ITERS - 1:
                revenue = shares(it + 1, r, h, wages, revenue)
            return revenue

        sent = 2 * it + 2 if it < ITERS - 1 else None
        revenues.append(over_cells(wage_cells, sent, zero, 2))

    for e in range(2 * ITERS):
        for way in range(2):

            @pl.when(can_row[way])
            def _():
                row_drain(e, way).wait_send()

            @pl.when(can_edge[way])
            def _():
                edge_drain(e, way).wait_send()

    for a in range(ITERS + 1):
        first_all(a).wait_send()
        second_copy(a).wait_send()
    sum_all().wait_send()
    total_all().wait_send()
    last_copy().wait_send()


def body(
    base_prod,
    resident,
    floor_space,
    bracket,
    tax_rate,
    mixing,
    spill_decay,
    commute_decay,
    pair_dest,
    pair_src,
    pair_dst,
    pair_count,
):
    tiles_y = lax.axis_size("gy")
    tiles_x = lax.axis_size("gx")
    slots = tiles_y * tiles_x * CAP
    chips = tiles_y * tiles_x // 2
    far_pairs = pair_src.shape[0]
    vmem = pl.BlockSpec(memory_space=pltpu.VMEM)
    whole = pl.BlockSpec(memory_space=pl.ANY)
    smem = pltpu.SMEM
    exchanges = 2 * ITERS
    dma = pltpu.SemaphoreType.DMA
    power, square = pl.pallas_call(
        functools.partial(kernel, tiles_y, tiles_x),
        out_shape=(
            jax.ShapeDtypeStruct(base_prod.shape, F32),
            jax.ShapeDtypeStruct(resident.shape, F32),
        ),
        in_specs=[vmem] * 8 + [whole] * 4,
        out_specs=(vmem, vmem),
        scratch_shapes=[
            pltpu.VMEM((exchanges, SECTORS, ROWS + 2 * HALF, COLS), BF16),
            pltpu.VMEM((exchanges, 2, PAIRS2, ROWS, 128), BF16),
            pltpu.VMEM((exchanges, 2, PAIRS2, ROWS, 128), BF16),
            pltpu.VMEM((SECTORS, ROWS, COLS), BF16),
            pltpu.VMEM((SECTORS, ROWS, COLS), F32),
            pltpu.VMEM((SECTORS, ROWS, COLS), F32),
            pltpu.VMEM((2 * SECTORS, COLS), F32),
            pltpu.VMEM((2 * SECTORS, ROWS, COLS), BF16),
            pltpu.VMEM((2 * SECTORS, COLS, COLS), BF16),
            pltpu.VMEM((2 * SECTORS, COLS, COLS), BF16),
            pltpu.VMEM((GROUPS * ROWS, 128), BF16),
            pltpu.VMEM((far_pairs, GROUPS * ROWS), BF16),
            pltpu.VMEM((slots, far_pairs), BF16),
            pltpu.VMEM((GROUPS * ROWS, slots), BF16),
            pltpu.VMEM((2 * GROUPS * CHUNK, 128), F32),
            pltpu.VMEM((ITERS + 1, chips, 2 * CAP, 128), BF16),
            pltpu.VMEM((ITERS + 1, chips, 2 * CAP, 128), BF16),
            pltpu.VMEM((ITERS + 1, chips * CAP, 128), BF16),
            pltpu.VMEM((ITERS + 1, 2, chips * CAP, 128), BF16),
            pltpu.VMEM((8, 128), F32),
            pltpu.VMEM((tiles_x // 2, 8, 128), F32),
            pltpu.VMEM((8, 128), F32),
            pltpu.VMEM((tiles_y, 8, 128), F32),
            pltpu.VMEM((ROWS, COLS), F32),
            pltpu.VMEM((ITERS, ROWS, COLS), F32),
            pltpu.VMEM((2, 8, 128), F32),
            smem((8,), F32),
            smem((SECTORS,), F32),
            smem((SECTORS,), F32),
            smem((SECTORS, SECTORS), F32),
            dma((4,)),
            dma((exchanges, 2)),
            dma((exchanges, 2, STEPS)),
            dma((exchanges, 2)),
            dma((exchanges, 2, 2)),
            dma((ITERS + 1,)),
            dma((ITERS + 1,)),
            dma((ITERS + 1,)),
            dma((ITERS + 1,)),
            dma((3,)),
            dma((3,)),
        ],
        compiler_params=pltpu.CompilerParams(
            collective_id=0, has_side_effects=True, vmem_limit_bytes=60 * 1024 * 1024
        ),
    )(
        base_prod,
        resident,
        floor_space,
        bracket,
        pair_dest.reshape(1, far_pairs),
        pair_src.reshape(1, far_pairs),
        pair_dst.reshape(1, far_pairs),
        pair_count.reshape(1, far_pairs),
        tax_rate,
        commute_decay,
        spill_decay,
        mixing,
    )
    return base_prod.astype(F32) * jnp.exp(power), jnp.sqrt(square)


def solution(mesh):
    return jax.shard_map(
        body,
        mesh=mesh,
        in_specs=(
            P(None, "gy", "gx"),
            P("gy", "gx"),
            P("gy", "gx"),
            P("gy", "gx"),
            P(),
            P(),
            P(),
            P(),
            P(("gy", "gx"), None),
            P(("gy", "gx")),
            P(("gy", "gx")),
            P(("gy", "gx")),
        ),
        out_specs=(P(None, "gy", "gx"), P("gy", "gx")),
        check_vma=False,
    )
```

```python
import functools

import jax
import jax.numpy as jnp
from jax import lax
from jax.experimental import pallas as pl
from jax.experimental.pallas import tpu as pltpu
from jax.sharding import PartitionSpec as P

HALF = 64
ITERS = 3
SECTORS = 8
CAP = 8
BETA_WAGE = 0.3
FAR_SCALE = 0.125
ROWS = 128
COLS = 256
GROUPS = COLS // 16
PAIRS2 = SECTORS // 2
CHUNK = 16
STEPS = HALF // CHUNK
MESH = pl.DeviceIdType.MESH
F32 = jnp.float32
BF16 = jnp.bfloat16


def swap_blocks(values):
    values = [pltpu.roll(v, 16 * s, 1) if s else v for s, v in enumerate(values)]
    block = lax.broadcasted_iota(jnp.int32, values[0].shape, 1) // 16
    for d in (1, 2, 4):
        moved = (block & d) != 0
        values = [jnp.where(moved, values[(a + d) % 8], values[a]) for a in range(8)]
    values = [values[-g % 8] for g in range(8)]
    return [pltpu.roll(v, 128 - 16 * g, 1) if g else v for g, v in enumerate(values)]


def kernel(
    tiles_y,
    tiles_x,
    base_any,
    resident_any,
    floor_any,
    bracket_any,
    dest_any,
    src_any,
    dst_any,
    count_any,
    tax_any,
    commute_any,
    spill_any,
    mixing_any,
    power_ref,
    rent_ref,
    ext,
    edge_out,
    edge_in,
    mid,
    near,
    labor,
    tap_row,
    band_row,
    band_col,
    band_edge,
    table,
    source_hot,
    slot_hot,
    place,
    far,
    one_out,
    one_in,
    two_out,
    two_in,
    sum_out,
    sum_in,
    total_out,
    total_in,
    rate_ref,
    income_ref,
    last_in,
    base_ref,
    resident_ref,
    floor_ref,
    bracket_ref,
    dest_ref,
    src_ref,
    dst_ref,
    count_ref,
    tax_ref,
    commute_ref,
    spill_ref,
    mixing_ref,
    load_sem,
    row_send,
    row_recv,
    edge_send,
    edge_recv,
    one_send,
    one_recv,
    two_send,
    two_recv,
    sum_send,
    sum_recv,
):
    my = lax.axis_index("gy")
    mx = lax.axis_index("gx")
    chips_x = tiles_x // 2
    chips = tiles_y * chips_x
    core = lax.rem(mx, 2)
    chip_x = mx // 2
    sibling = mx + 1 - 2 * core
    beyond = lax.rem(mx + 2 * core - 1 + tiles_x, tiles_x)
    mine = my * chips_x + chip_x
    slots = tiles_y * tiles_x * CAP
    far_pairs = dest_ref.shape[1]

    loads = [
        pltpu.make_async_copy(source, target, load_sem.at[k])
        for k, (source, target) in enumerate(
            (
                (base_any, base_ref),
                (resident_any, resident_ref),
                (bracket_any, bracket_ref),
                (floor_any, floor_ref),
                (dest_any, dest_ref),
                (src_any, src_ref),
                (dst_any, dst_ref),
                (count_any, count_ref),
                (tax_any, tax_ref),
                (commute_any, commute_ref),
                (spill_any, spill_ref),
                (mixing_any, mixing_ref),
            )
        )
    ]
    for load in loads:
        load.start()

    barrier = pltpu.get_barrier_semaphore()

    def chip_at(j):
        return lax.rem(my + j // chips_x, tiles_y), lax.rem(chip_x + lax.rem(j, chips_x), chips_x)

    def greet(y, x):
        pl.semaphore_signal(barrier, inc=1, device_id=(y, x), device_id_type=MESH)

    def greet_chip(j, carry):
        y, x = chip_at(j)
        greet(y, 2 * x + core)
        return carry

    greet(my, sibling)
    greet(my, beyond)
    lax.fori_loop(1, chips, greet_chip, 0)

    def row_copy(e, j, way):
        start = HALF if way == 0 else ROWS
        land = HALF + ROWS if way == 0 else 0
        target = my - 1 if way == 0 else my + 1
        step = pl.multiple_of(j * CHUNK, CHUNK)
        return pltpu.make_async_remote_copy(
            src_ref=ext.at[e, :, pl.ds(start + step, CHUNK), :],
            dst_ref=ext.at[e, :, pl.ds(land + step, CHUNK), :],
            send_sem=row_send.at[e, way],
            recv_sem=row_recv.at[e, way, j],
            device_id=(target, mx),
            device_id_type=MESH,
        )

    def row_drain(e, way):
        start = HALF if way == 0 else ROWS
        target = my - 1 if way == 0 else my + 1
        return pltpu.make_async_remote_copy(
            src_ref=ext.at[e, :, pl.ds(start, HALF), :],
            dst_ref=ext.at[e, :, pl.ds(start, HALF), :],
            send_sem=row_send.at[e, way],
            recv_sem=row_recv.at[e, way, 0],
            device_id=(target, mx),
            device_id_type=MESH,
        )

    can_row = (my > 0, my < tiles_y - 1)
    can_edge = (mx > 0, mx < tiles_x - 1)

    def send_rows(e, j):
        for way in range(2):

            @pl.when(can_row[way])
            def _():
                row_copy(e, j, way).start()

    def wait_rows(e):
        for way in range(2):

            @pl.when(can_row[1 - way])
            def _():
                for j in range(STEPS):
                    row_copy(e, j, way).wait_recv()

    def edge_copy(e, i, way):
        target = mx - 1 if way == 0 else mx + 1
        return pltpu.make_async_remote_copy(
            src_ref=edge_out.at[e, way, pl.ds(2 * i, 2)],
            dst_ref=edge_in.at[e, 1 - way, pl.ds(2 * i, 2)],
            send_sem=edge_send.at[e, way],
            recv_sem=edge_recv.at[e, way, i],
            device_id=(my, target),
            device_id_type=MESH,
        )

    def edge_drain(e, way):
        target = mx - 1 if way == 0 else mx + 1
        return pltpu.make_async_remote_copy(
            src_ref=edge_out.at[e, way],
            dst_ref=edge_in.at[e, 1 - way],
            send_sem=edge_send.at[e, way],
            recv_sem=edge_recv.at[e, way, 0],
            device_id=(my, target),
            device_id_type=MESH,
        )

    lane128 = lax.broadcasted_iota(jnp.int32, (ROWS, 128), 1)

    def rows_pass(e, kind):
        wait_rows(e)

        def one(half, carry):
            for k in range(2):
                i = 2 * half + k
                ends = []
                for s in (2 * i, 2 * i + 1):
                    passed = jnp.dot(
                        band_row[kind * SECTORS + s], ext[e, s], preferred_element_type=F32
                    )
                    mid[s] = passed.astype(BF16)
                    ends.append((passed[:, 0:128], passed[:, 128:256]))
                first, second = ends
                low = lane128 < HALF
                edge_out[e, 0, i] = jnp.where(
                    low, first[0], pltpu.roll(second[0], HALF, 1)
                ).astype(BF16)
                edge_out[e, 1, i] = jnp.where(
                    low, pltpu.roll(second[1], HALF, 1), first[1]
                ).astype(BF16)
            for way in range(2):

                @pl.when(can_edge[way])
                def _():
                    edge_copy(e, half, way).start()

            return carry

        lax.fori_loop(0, 2, one, 0)

    def columns_pass(e, kind, result):
        def one(half, carry):
            for way in range(2):

                @pl.when(can_edge[1 - way])
                def _():
                    edge_copy(e, half, way).wait_recv()

            for k in range(4):
                s = 4 * half + k
                i = 2 * half + k // 2
                b = kind * SECTORS + s
                value = jnp.dot(mid[s], band_col[b], preferred_element_type=F32)
                value += jnp.dot(
                    edge_in[e, 0, i], band_edge[b, 0:128, :], preferred_element_type=F32
                )
                value += jnp.dot(
                    edge_in[e, 1, i], band_edge[b, 128:256, :], preferred_element_type=F32
                )
                result[s] = value
            return carry

        lax.fori_loop(0, 2, one, 0)

    def make_bands(kind):
        u = lax.broadcasted_iota(jnp.int32, (COLS, COLS), 0)
        x = lax.broadcasted_iota(jnp.int32, (COLS, COLS), 1)
        inside = jnp.abs(u - x) <= 128

        def one(s, carry):
            b = kind * SECTORS + s
            line = jnp.broadcast_to(tap_row[pl.ds(b, 1), :], (ROWS, COLS))
            rows_band = pltpu.roll(line, 0, 1, stride=1, stride_axis=0)
            band_row[b] = rows_band.astype(BF16)
            circle = jnp.concatenate(
                [pltpu.roll(rows_band, COLS - HALF, 1), pltpu.roll(rows_band, HALF, 1)], axis=0
            )
            band_col[b] = jnp.where(inside, circle, 0.0).astype(BF16)
            rest = jnp.where(inside, 0.0, circle)
            even = jnp.concatenate([rest[128:256], rest[0:128]], axis=0)
            odd = jnp.concatenate(
                [rest[192:256], rest[128:192], rest[64:128], rest[0:64]], axis=0
            )
            band_edge[b] = jnp.where(lax.rem(s, 2) == 0, even, odd).astype(BF16)
            return carry

        lax.fori_loop(0, SECTORS, one, 0)

    def first_copy(a, y, x):
        return pltpu.make_async_remote_copy(
            src_ref=one_out.at[a, y * chips_x + x],
            dst_ref=one_in.at[a, mine],
            send_sem=one_send.at[a],
            recv_sem=one_recv.at[a],
            device_id=(y, 2 * x + core),
            device_id_type=MESH,
        )

    def first_all(a):
        return pltpu.make_async_remote_copy(
            src_ref=one_out.at[a, pl.ds(0, chips - 1)],
            dst_ref=one_in.at[a, pl.ds(0, chips - 1)],
            send_sem=one_send.at[a],
            recv_sem=one_recv.at[a],
            device_id=(my, sibling),
            device_id_type=MESH,
        )

    def second_copy(a):
        return pltpu.make_async_remote_copy(
            src_ref=two_out.at[a],
            dst_ref=two_in.at[a, 1],
            send_sem=two_send.at[a],
            recv_sem=two_recv.at[a],
            device_id=(my, sibling),
            device_id_type=MESH,
        )

    def start_first(a):
        def one(j, carry):
            first_copy(a, *chip_at(j)).start()
            return carry

        lax.fori_loop(1, chips, one, 0)
        one_in[a, mine] = one_out[a, mine]

    def pass_on(a):
        first_all(a).wait_recv()
        parts = one_in[a].astype(F32).reshape(chips, 2, CAP, 128)
        low, high = parts[:, 0], parts[:, 1]
        two_out[a] = jnp.where(core == 0, high, low).reshape(chips * CAP, 128).astype(BF16)
        second_copy(a).start()
        two_in[a, 0] = jnp.where(core == 0, low, high).reshape(chips * CAP, 128).astype(BF16)

    def sum_copy(x):
        return pltpu.make_async_remote_copy(
            src_ref=sum_out,
            dst_ref=sum_in.at[chip_x],
            send_sem=sum_send.at[0],
            recv_sem=sum_recv.at[0],
            device_id=(my, 2 * x + core),
            device_id_type=MESH,
        )

    def total_copy(y):
        return pltpu.make_async_remote_copy(
            src_ref=total_out,
            dst_ref=total_in.at[my],
            send_sem=sum_send.at[1],
            recv_sem=sum_recv.at[1],
            device_id=(y, mx),
            device_id_type=MESH,
        )

    def sum_all():
        return pltpu.make_async_remote_copy(
            src_ref=sum_in.at[pl.ds(0, chips_x - 1)],
            dst_ref=sum_in.at[pl.ds(0, chips_x - 1)],
            send_sem=sum_send.at[0],
            recv_sem=sum_recv.at[0],
            device_id=(my, sibling),
            device_id_type=MESH,
        )

    def total_all():
        return pltpu.make_async_remote_copy(
            src_ref=total_in.at[pl.ds(0, tiles_y - 1)],
            dst_ref=total_in.at[pl.ds(0, tiles_y - 1)],
            send_sem=sum_send.at[1],
            recv_sem=sum_recv.at[1],
            device_id=(my, sibling),
            device_id_type=MESH,
        )

    def last_copy():
        return pltpu.make_async_remote_copy(
            src_ref=last_in.at[0],
            dst_ref=last_in.at[1],
            send_sem=sum_send.at[2],
            recv_sem=sum_recv.at[2],
            device_id=(my, sibling),
            device_id_type=MESH,
        )

    def unit(r, h):
        return pl.ds(r, CHUNK), pl.ds(pl.multiple_of(128 * h, 128), 128)

    def strip_rows(r, h, g):
        return pl.ds(pl.multiple_of((8 * h + g) * ROWS + r, CHUNK), CHUNK)

    def over_cells(work, sent, carry, wide):
        def step(j, carry):
            def one(u, carry):
                for k in range(wide):
                    number = u * wide + k
                    r = pl.multiple_of((number // 2) * HALF + j * CHUNK, CHUNK)
                    carry = work(r, number % 2, carry)
                return carry

            carry = one(0, carry) if wide == 4 else lax.fori_loop(0, 4 // wide, one, carry)
            if sent is not None:
                send_rows(sent, j)
            return carry

        return lax.fori_loop(0, STEPS, step, carry)

    def shares(it, r, h, wages, revenue):
        rows, lanes = unit(r, h)
        powers = [w * w * w for w in wages]
        inverse = 1.0 / sum(powers[1:], powers[0])
        people = resident_ref[rows, lanes]
        share = [p * inverse for p in powers]
        income = sum([q * w for q, w in zip(share[1:], wages[1:])], share[0] * wages[0])
        income_ref[it, rows, lanes] = income
        supply = [people * q for q in share]
        for s in range(SECTORS):
            ext[2 * it, s, pl.ds(HALF + r, CHUNK), lanes] = supply[s].astype(BF16)
        for g, strip in enumerate(swap_blocks(supply)):
            table[strip_rows(r, h, g), :] = strip.astype(BF16)
        gain = people * rate_ref[rows, lanes] * income
        return revenue + gain[0:8] + gain[8:16]

    def gather(a):
        picked = jnp.dot(source_hot[...], table[...], preferred_element_type=F32).astype(BF16)
        ordered = jnp.dot(slot_hot[...], picked, preferred_element_type=F32).astype(BF16)
        one_out[a] = ordered.reshape(chips, 2 * CAP, 128)

    zero = jnp.zeros((8, 128), F32)

    def first_cells(r, h, carry):
        people_sum, revenue = carry
        rows, lanes = unit(r, h)
        bracket = bracket_ref[rows, lanes]
        rate = jnp.zeros((CHUNK, 128), F32)
        for b in range(8):
            rate = jnp.where(bracket == b, tax_ref[b], rate)
        rate_ref[rows, lanes] = rate
        people = resident_ref[rows, lanes]
        people_sum = people_sum + people[0:8] + people[8:16]
        wages = [base_ref[s, rows, lanes].astype(F32) for s in range(SECTORS)]
        return people_sum, shares(0, r, h, wages, revenue)

    for load in loads:
        load.wait()
    people_sum, revenue0 = over_cells(first_cells, None, (zero, zero), 4)
    pl.semaphore_wait(barrier, chips + 1)
    for j in range(STEPS):
        send_rows(0, j)

    line = lax.broadcasted_iota(jnp.int32, (8, far_pairs), 0)
    source, target = src_ref[...], dst_ref[...]
    row, group = target >> 4, target & 15
    fields = [
        dest_ref[...],
        (source & 15) * ROWS + (source >> 4),
        ((((row >> 4) & 3) * 2 + (row >> 6)) * GROUPS) + group,
        row & 15,
        count_ref[...],
    ]
    pairs = jnp.zeros((8, far_pairs), jnp.int32)
    for k, field in enumerate(fields):
        pairs = jnp.where(line == k, field, pairs)
    pairs = pairs.astype(F32)
    across = jnp.concatenate([pairs, jnp.zeros((120, far_pairs), F32)], axis=0).T
    dest_row = pairs[0:1, :]
    earlier = lax.broadcasted_iota(jnp.int32, (far_pairs, far_pairs), 0) < (
        lax.broadcasted_iota(jnp.int32, (far_pairs, far_pairs), 1)
    )
    same = (across[:, 0:1] == dest_row) & earlier
    rank = jnp.sum(jnp.where(same, 1.0, 0.0), axis=0, keepdims=True)
    slot_of = (dest_row * CAP + rank).astype(jnp.int32)
    slot_ids = lax.broadcasted_iota(jnp.int32, (slots, far_pairs), 0)
    slot_hot[...] = jnp.where(slot_ids == slot_of, 1.0, 0.0).astype(BF16)
    strip_ids = lax.broadcasted_iota(jnp.int32, (far_pairs, GROUPS * ROWS), 1)
    source_hot[...] = jnp.where(
        strip_ids == across[:, 1:2].astype(jnp.int32), 1.0, 0.0
    ).astype(BF16)
    one_out[ITERS] = (
        jnp.dot(slot_hot[...], across.astype(BF16), preferred_element_type=F32)
        .astype(BF16)
        .reshape(chips, 2 * CAP, 128)
    )
    start_first(ITERS)
    gather(0)
    start_first(0)

    @pl.when(my == 0)
    def _():
        ext[:, :, 0:HALF, :] = jnp.zeros((2 * ITERS, SECTORS, HALF, COLS), BF16)

    @pl.when(my == tiles_y - 1)
    def _():
        ext[:, :, HALF + ROWS :, :] = jnp.zeros((2 * ITERS, SECTORS, HALF, COLS), BF16)

    @pl.when(mx == 0)
    def _():
        edge_in[:, 0] = jnp.zeros((2 * ITERS, PAIRS2, ROWS, 128), BF16)

    @pl.when(mx == tiles_x - 1)
    def _():
        edge_in[:, 1] = jnp.zeros((2 * ITERS, PAIRS2, ROWS, 128), BF16)

    sector = lax.broadcasted_iota(jnp.int32, (2 * SECTORS, COLS), 0)
    tap = lax.broadcasted_iota(jnp.int32, (2 * SECTORS, COLS), 1)
    decay = jnp.zeros((2 * SECTORS, COLS), F32)
    for s in range(SECTORS):
        decay = jnp.where(sector == s, commute_ref[s], decay)
        decay = jnp.where(sector == SECTORS + s, spill_ref[s], decay)
    offset = jnp.abs(tap - HALF).astype(F32) / HALF
    unscaled = jnp.where(tap <= 2 * HALF, jnp.exp(-decay * offset), 0.0)
    tap_row[...] = (unscaled / jnp.sum(unscaled, axis=1, keepdims=True)).astype(BF16).astype(F32)
    make_bands(0)

    pass_on(ITERS)

    def build_place():
        second_copy(ITERS).wait_recv()
        routing = two_in[ITERS].reshape(slots, 128)
        line = lax.broadcasted_iota(jnp.int32, (16, 128), 0)
        lane = lax.broadcasted_iota(jnp.int32, (16, 128), 1)
        pick = jnp.where((line == 0) & (lane == 2), float(CHUNK), 0.0)
        pick = jnp.where((line == 0) & (lane == 3), 1.0, pick)
        pick = jnp.where((line == 1) & (lane == 4), 1.0, pick).astype(BF16)
        found = lax.dot_general(
            pick, routing, (((1,), (1,)), ((), ())), preferred_element_type=F32
        )
        where_to, weight = found[0:1, :].astype(jnp.int32), found[1:2, :]

        def one(g, carry):
            strip = g * ROWS + lax.broadcasted_iota(jnp.int32, (ROWS, slots), 0)
            place[pl.ds(pl.multiple_of(g * ROWS, ROWS), ROWS), :] = jnp.where(
                strip == where_to, weight, 0.0
            ).astype(BF16)
            return carry

        lax.fori_loop(0, GROUPS, one, 0)

    revenues = [revenue0]
    for it in range(ITERS):
        if it > 0:
            gather(it)
            start_first(it)
        if it == ITERS - 1:
            line = lax.broadcasted_iota(jnp.int32, (8, 128), 0)
            parts = zero
            for k, part in enumerate([people_sum] + revenues):
                parts = jnp.where(line == k, jnp.sum(part, axis=0, keepdims=True), parts)
            sum_out[...] = parts

            def start_sum(j, carry):
                sum_copy(lax.rem(chip_x + j, chips_x)).start()
                return carry

            lax.fori_loop(1, chips_x, start_sum, 0)
            sum_in[chip_x] = parts
        rows_pass(2 * it, 0)
        pass_on(it)
        if it == ITERS - 1:
            sum_all().wait_recv()
            halfway = jnp.sum(sum_in[...], axis=0)
            total_out[...] = halfway

            def start_total(j, carry):
                total_copy(lax.rem(my + j, tiles_y)).start()
                return carry

            lax.fori_loop(1, tiles_y, start_total, 0)
            total_in[my] = halfway
        columns_pass(2 * it, 0, near)
        if it == ITERS - 1:
            total_all().wait_recv()
            last_in[0] = jnp.sum(total_in[...], axis=0)
            last_copy().start()
        if it == 0:
            build_place()
        second_copy(it).wait_recv()

        def labor_step(j, carry):
            block = 2 * GROUPS * CHUNK
            far[...] = jnp.dot(
                place[pl.ds(pl.multiple_of(j * block, block), block), :],
                two_in[it].reshape(slots, 128),
                preferred_element_type=F32,
            )
            for number in range(4):
                way, h = number // 2, number % 2
                r = pl.multiple_of(way * HALF + j * CHUNK, CHUNK)
                rows, lanes = unit(r, h)
                first = (way * GROUPS + 8 * h) * CHUNK
                strips = [far[first + CHUNK * g : first + CHUNK * (g + 1), :] for g in range(8)]
                for s, flow in enumerate(swap_blocks(strips)):
                    value = near[s, rows, lanes] + FAR_SCALE * flow
                    labor[s, rows, lanes] = value
                    ext[2 * it + 1, s, pl.ds(HALF + r, CHUNK), lanes] = value.astype(BF16)
            send_rows(2 * it + 1, j)
            return carry

        lax.fori_loop(0, STEPS, labor_step, 0)
        if it == 0:
            make_bands(1)
        if it == ITERS - 1:
            last_copy().wait_recv()
            sums = jnp.sum(last_in[0] + last_in[1], axis=1, keepdims=True)
            people_all = sums[0:1, 0:1]
            transfers = [sums[1 + k : 2 + k, 0:1] / people_all for k in range(ITERS)]

            def rent_chunk(c, carry):
                rows = pl.ds(pl.multiple_of(c * CHUNK, CHUNK), CHUNK)
                keep = 1.0 - rate_ref[rows, :]
                people, space = resident_ref[rows, :], floor_ref[rows, :]
                ratio = people / space
                square = None
                for k in range(ITERS):
                    net = keep * income_ref[k, rows, :] + transfers[k]
                    level = ratio if square is None else jnp.sqrt(square) * ratio
                    square = level * net
                rent_ref[rows, :] = square
                return carry

            lax.fori_loop(0, ROWS // CHUNK, rent_chunk, 0)
        rows_pass(2 * it + 1, 1)
        columns_pass(2 * it + 1, 1, near)

        def wage_cells(r, h, revenue):
            rows, lanes = unit(r, h)
            logs = [jnp.log(1.0 + near[s, rows, lanes]) for s in range(SECTORS)]
            wages = []
            for s in range(SECTORS):
                power = -BETA_WAGE * jnp.log(1.0 + labor[s, rows, lanes])
                for t in range(SECTORS):
                    power = power + mixing_ref[s, t] * logs[t]
                if it == ITERS - 1:
                    power_ref[s, rows, lanes] = power
                else:
                    wages.append(base_ref[s, rows, lanes].astype(F32) * jnp.exp(power))
            if it < ITERS - 1:
                revenue = shares(it + 1, r, h, wages, revenue)
            return revenue

        sent = 2 * it + 2 if it < ITERS - 1 else None
        revenues.append(over_cells(wage_cells, sent, zero, 2))

    for e in range(2 * ITERS):
        for way in range(2):

            @pl.when(can_row[way])
            def _():
                row_drain(e, way).wait_send()

            @pl.when(can_edge[way])
            def _():
                edge_drain(e, way).wait_send()

    for a in range(ITERS + 1):
        first_all(a).wait_send()
        second_copy(a).wait_send()
    sum_all().wait_send()
    total_all().wait_send()
    last_copy().wait_send()


def body(
    base_prod,
    resident,
    floor_space,
    bracket,
    tax_rate,
    mixing,
    spill_decay,
    commute_decay,
    pair_dest,
    pair_src,
    pair_dst,
    pair_count,
):
    tiles_y = lax.axis_size("gy")
    tiles_x = lax.axis_size("gx")
    slots = tiles_y * tiles_x * CAP
    chips = tiles_y * tiles_x // 2
    far_pairs = pair_src.shape[0]
    vmem = pl.BlockSpec(memory_space=pltpu.VMEM)
    whole = pl.BlockSpec(memory_space=pltpu.HBM)
    smem = pltpu.SMEM
    exchanges = 2 * ITERS
    dma = pltpu.SemaphoreType.DMA
    power, square = pl.pallas_call(
        functools.partial(kernel, tiles_y, tiles_x),
        out_shape=(
            jax.ShapeDtypeStruct(base_prod.shape, F32),
            jax.ShapeDtypeStruct(resident.shape, F32),
        ),
        in_specs=[whole] * 12,
        out_specs=(vmem, vmem),
        scratch_shapes=[
            pltpu.VMEM((exchanges, SECTORS, ROWS + 2 * HALF, COLS), BF16),
            pltpu.VMEM((exchanges, 2, PAIRS2, ROWS, 128), BF16),
            pltpu.VMEM((exchanges, 2, PAIRS2, ROWS, 128), BF16),
            pltpu.VMEM((SECTORS, ROWS, COLS), BF16),
            pltpu.VMEM((SECTORS, ROWS, COLS), F32),
            pltpu.VMEM((SECTORS, ROWS, COLS), F32),
            pltpu.VMEM((2 * SECTORS, COLS), F32),
            pltpu.VMEM((2 * SECTORS, ROWS, COLS), BF16),
            pltpu.VMEM((2 * SECTORS, COLS, COLS), BF16),
            pltpu.VMEM((2 * SECTORS, COLS, COLS), BF16),
            pltpu.VMEM((GROUPS * ROWS, 128), BF16),
            pltpu.VMEM((far_pairs, GROUPS * ROWS), BF16),
            pltpu.VMEM((slots, far_pairs), BF16),
            pltpu.VMEM((GROUPS * ROWS, slots), BF16),
            pltpu.VMEM((2 * GROUPS * CHUNK, 128), F32),
            pltpu.VMEM((ITERS + 1, chips, 2 * CAP, 128), BF16),
            pltpu.VMEM((ITERS + 1, chips, 2 * CAP, 128), BF16),
            pltpu.VMEM((ITERS + 1, chips * CAP, 128), BF16),
            pltpu.VMEM((ITERS + 1, 2, chips * CAP, 128), BF16),
            pltpu.VMEM((8, 128), F32),
            pltpu.VMEM((tiles_x // 2, 8, 128), F32),
            pltpu.VMEM((8, 128), F32),
            pltpu.VMEM((tiles_y, 8, 128), F32),
            pltpu.VMEM((ROWS, COLS), F32),
            pltpu.VMEM((ITERS, ROWS, COLS), F32),
            pltpu.VMEM((2, 8, 128), F32),
            pltpu.VMEM((SECTORS, ROWS, COLS), BF16),
            pltpu.VMEM((ROWS, COLS), F32),
            pltpu.VMEM((ROWS, COLS), F32),
            pltpu.VMEM((ROWS, COLS), jnp.int32),
            pltpu.VMEM((1, far_pairs), jnp.int32),
            pltpu.VMEM((1, far_pairs), jnp.int32),
            pltpu.VMEM((1, far_pairs), jnp.int32),
            pltpu.VMEM((1, far_pairs), jnp.int32),
            smem((8,), F32),
            smem((SECTORS,), F32),
            smem((SECTORS,), F32),
            smem((SECTORS, SECTORS), F32),
            dma((12,)),
            dma((exchanges, 2)),
            dma((exchanges, 2, STEPS)),
            dma((exchanges, 2)),
            dma((exchanges, 2, 2)),
            dma((ITERS + 1,)),
            dma((ITERS + 1,)),
            dma((ITERS + 1,)),
            dma((ITERS + 1,)),
            dma((3,)),
            dma((3,)),
        ],
        compiler_params=pltpu.CompilerParams(
            collective_id=0, has_side_effects=True, vmem_limit_bytes=40 * 1024 * 1024
        ),
    )(
        *(
            pltpu.with_memory_space_constraint(x, pltpu.HBM)
            for x in (
                base_prod,
                resident,
                floor_space,
                bracket,
                pair_dest.reshape(1, far_pairs),
                pair_src.reshape(1, far_pairs),
                pair_dst.reshape(1, far_pairs),
                pair_count.reshape(1, far_pairs),
                tax_rate,
                commute_decay,
                spill_decay,
                mixing,
            )
        )
    )
    return base_prod.astype(F32) * jnp.exp(power), jnp.sqrt(square)


def solution(mesh):
    return jax.shard_map(
        body,
        mesh=mesh,
        in_specs=(
            P(None, "gy", "gx"),
            P("gy", "gx"),
            P("gy", "gx"),
            P("gy", "gx"),
            P(),
            P(),
            P(),
            P(),
            P(("gy", "gx"), None),
            P(("gy", "gx")),
            P(("gy", "gx")),
            P(("gy", "gx")),
        ),
        out_specs=(P(None, "gy", "gx"), P("gy", "gx")),
        check_vma=False,
    )
```

```python
import functools

import jax
import jax.numpy as jnp
from jax import lax
from jax.experimental import pallas as pl
from jax.experimental.pallas import tpu as pltpu
from jax.sharding import PartitionSpec as P

HALF = 64
ITERS = 3
SECTORS = 8
CAP = 8
BETA_WAGE = 0.3
FAR_SCALE = 0.125
ROWS = 128
COLS = 256
GROUPS = COLS // 16
PAIRS2 = SECTORS // 2
CHUNK = 16
STEPS = HALF // CHUNK
MESH = pl.DeviceIdType.MESH
F32 = jnp.float32
BF16 = jnp.bfloat16


def swap_blocks(values):
    values = [pltpu.roll(v, 16 * s, 1) if s else v for s, v in enumerate(values)]
    block = lax.broadcasted_iota(jnp.int32, values[0].shape, 1) // 16
    for d in (1, 2, 4):
        moved = (block & d) != 0
        values = [jnp.where(moved, values[(a + d) % 8], values[a]) for a in range(8)]
    values = [values[-g % 8] for g in range(8)]
    return [pltpu.roll(v, 128 - 16 * g, 1) if g else v for g, v in enumerate(values)]


def kernel(
    tiles_y,
    tiles_x,
    base_any,
    resident_any,
    floor_any,
    bracket_any,
    dest_any,
    src_any,
    dst_any,
    count_any,
    tax_any,
    commute_any,
    spill_any,
    mixing_any,
    power_ref,
    rent_ref,
    ext,
    edge_out,
    edge_in,
    mid,
    near,
    labor,
    tap_row,
    band_row,
    band_col,
    band_edge,
    table,
    source_hot,
    slot_hot,
    place,
    far,
    one_out,
    one_in,
    two_out,
    two_in,
    sum_out,
    sum_in,
    total_out,
    total_in,
    rate_ref,
    income_ref,
    last_in,
    base_ref,
    resident_ref,
    floor_ref,
    bracket_ref,
    dest_ref,
    src_ref,
    dst_ref,
    count_ref,
    tax_ref,
    commute_ref,
    spill_ref,
    mixing_ref,
    load_sem,
    row_send,
    row_recv,
    edge_send,
    edge_recv,
    one_send,
    one_recv,
    two_send,
    two_recv,
    sum_send,
    sum_recv,
):
    my = lax.axis_index("gy")
    mx = lax.axis_index("gx")
    chips_x = tiles_x // 2
    chips = tiles_y * chips_x
    core = lax.rem(mx, 2)
    chip_x = mx // 2
    sibling = mx + 1 - 2 * core
    beyond = lax.rem(mx + 2 * core - 1 + tiles_x, tiles_x)
    mine = my * chips_x + chip_x
    slots = tiles_y * tiles_x * CAP
    far_pairs = dest_ref.shape[1]

    loads = [
        pltpu.make_async_copy(source, target, load_sem.at[k])
        for k, (source, target) in enumerate(
            (
                (base_any, base_ref),
                (resident_any, resident_ref),
                (bracket_any, bracket_ref),
                (floor_any, floor_ref),
                (dest_any, dest_ref),
                (src_any, src_ref),
                (dst_any, dst_ref),
                (count_any, count_ref),
                (tax_any, tax_ref),
                (commute_any, commute_ref),
                (spill_any, spill_ref),
                (mixing_any, mixing_ref),
            )
        )
    ]
    for load in loads:
        load.start()

    barrier = pltpu.get_barrier_semaphore()

    def chip_at(j):
        return lax.rem(my + j // chips_x, tiles_y), lax.rem(chip_x + lax.rem(j, chips_x), chips_x)

    def greet(y, x):
        pl.semaphore_signal(barrier, inc=1, device_id=(y, x), device_id_type=MESH)

    def greet_chip(j, carry):
        y, x = chip_at(j)
        greet(y, 2 * x + core)
        return carry

    greet(my, sibling)
    greet(my, beyond)
    lax.fori_loop(1, chips, greet_chip, 0)

    def row_copy(e, j, way):
        start = HALF if way == 0 else ROWS
        land = HALF + ROWS if way == 0 else 0
        target = my - 1 if way == 0 else my + 1
        step = pl.multiple_of(j * CHUNK, CHUNK)
        return pltpu.make_async_remote_copy(
            src_ref=ext.at[e, :, pl.ds(start + step, CHUNK), :],
            dst_ref=ext.at[e, :, pl.ds(land + step, CHUNK), :],
            send_sem=row_send.at[e, way],
            recv_sem=row_recv.at[e, way, j],
            device_id=(target, mx),
            device_id_type=MESH,
        )

    def row_drain(e, way):
        start = HALF if way == 0 else ROWS
        target = my - 1 if way == 0 else my + 1
        return pltpu.make_async_remote_copy(
            src_ref=ext.at[e, :, pl.ds(start, HALF), :],
            dst_ref=ext.at[e, :, pl.ds(start, HALF), :],
            send_sem=row_send.at[e, way],
            recv_sem=row_recv.at[e, way, 0],
            device_id=(target, mx),
            device_id_type=MESH,
        )

    can_row = (my > 0, my < tiles_y - 1)
    can_edge = (mx > 0, mx < tiles_x - 1)

    def send_rows(e, j):
        for way in range(2):

            @pl.when(can_row[way])
            def _():
                row_copy(e, j, way).start()

    def wait_rows(e):
        for way in range(2):

            @pl.when(can_row[1 - way])
            def _():
                for j in range(STEPS):
                    row_copy(e, j, way).wait_recv()

    def edge_copy(e, i, way):
        target = mx - 1 if way == 0 else mx + 1
        return pltpu.make_async_remote_copy(
            src_ref=edge_out.at[e, way, pl.ds(2 * i, 2)],
            dst_ref=edge_in.at[e, 1 - way, pl.ds(2 * i, 2)],
            send_sem=edge_send.at[e, way],
            recv_sem=edge_recv.at[e, way, i],
            device_id=(my, target),
            device_id_type=MESH,
        )

    def edge_drain(e, way):
        target = mx - 1 if way == 0 else mx + 1
        return pltpu.make_async_remote_copy(
            src_ref=edge_out.at[e, way],
            dst_ref=edge_in.at[e, 1 - way],
            send_sem=edge_send.at[e, way],
            recv_sem=edge_recv.at[e, way, 0],
            device_id=(my, target),
            device_id_type=MESH,
        )

    lane128 = lax.broadcasted_iota(jnp.int32, (ROWS, 128), 1)

    def rows_pass(e, kind):
        wait_rows(e)

        def one(half, carry):
            for k in range(2):
                i = 2 * half + k
                ends = []
                for s in (2 * i, 2 * i + 1):
                    passed = jnp.dot(
                        band_row[kind * SECTORS + s], ext[e, s], preferred_element_type=F32
                    )
                    mid[s] = passed.astype(BF16)
                    ends.append((passed[:, 0:128], passed[:, 128:256]))
                first, second = ends
                low = lane128 < HALF
                edge_out[e, 0, i] = jnp.where(
                    low, first[0], pltpu.roll(second[0], HALF, 1)
                ).astype(BF16)
                edge_out[e, 1, i] = jnp.where(
                    low, pltpu.roll(second[1], HALF, 1), first[1]
                ).astype(BF16)
            for way in range(2):

                @pl.when(can_edge[way])
                def _():
                    edge_copy(e, half, way).start()

            return carry

        lax.fori_loop(0, 2, one, 0)

    def columns_start(kind, result):
        def one(half, carry):
            for k in range(4):
                s = 4 * half + k
                result[s] = jnp.dot(
                    mid[s], band_col[kind * SECTORS + s], preferred_element_type=F32
                )
            return carry

        lax.fori_loop(0, 2, one, 0)

    def columns_finish(e, kind, result):
        def one(half, carry):
            for way in range(2):

                @pl.when(can_edge[1 - way])
                def _():
                    edge_copy(e, half, way).wait_recv()

            for k in range(4):
                s = 4 * half + k
                for side in range(2):
                    lanes = slice(128 * side, 128 * side + 128)
                    result[s, :, lanes] += jnp.dot(
                        edge_in[e, side, 2 * half + k // 2],
                        band_edge[kind * SECTORS + s, side],
                        preferred_element_type=F32,
                    )
            return carry

        lax.fori_loop(0, 2, one, 0)

    def make_bands(kind):
        u = lax.broadcasted_iota(jnp.int32, (COLS, COLS), 0)
        x = lax.broadcasted_iota(jnp.int32, (COLS, COLS), 1)
        inside = jnp.abs(u - x) <= 128

        def one(s, carry):
            b = kind * SECTORS + s
            line = jnp.broadcast_to(tap_row[pl.ds(b, 1), :], (ROWS, COLS))
            rows_band = pltpu.roll(line, 0, 1, stride=1, stride_axis=0)
            band_row[b] = rows_band.astype(BF16)
            circle = jnp.concatenate(
                [pltpu.roll(rows_band, COLS - HALF, 1), pltpu.roll(rows_band, HALF, 1)], axis=0
            )
            band_col[b] = jnp.where(inside, circle, 0.0).astype(BF16)
            rest = jnp.where(inside, 0.0, circle)
            swap = lax.rem(s, 2) == 1
            for side in range(2):
                block = rest[128 - 128 * side : 256 - 128 * side, 128 * side : 128 * side + 128]
                turned = jnp.concatenate([block[HALF:], block[:HALF]], axis=0)
                band_edge[b, side] = jnp.where(swap, turned, block).astype(BF16)
            return carry

        lax.fori_loop(0, SECTORS, one, 0)

    def parts_of(a):
        return 2 if a == 0 else 1

    def first_copy(a, y, x):
        return pltpu.make_async_remote_copy(
            src_ref=one_out.at[a, y * chips_x + x, pl.ds(0, parts_of(a))],
            dst_ref=one_in.at[a, mine, pl.ds(0, parts_of(a))],
            send_sem=one_send.at[a],
            recv_sem=one_recv.at[a],
            device_id=(y, 2 * x + core),
            device_id_type=MESH,
        )

    def first_all(a):
        return pltpu.make_async_remote_copy(
            src_ref=one_out.at[a, pl.ds(0, chips - 1), pl.ds(0, parts_of(a))],
            dst_ref=one_in.at[a, pl.ds(0, chips - 1), pl.ds(0, parts_of(a))],
            send_sem=one_send.at[a],
            recv_sem=one_recv.at[a],
            device_id=(my, sibling),
            device_id_type=MESH,
        )

    def second_copy(a):
        return pltpu.make_async_remote_copy(
            src_ref=two_out.at[a, pl.ds(0, parts_of(a))],
            dst_ref=two_in.at[a, pl.ds(0, parts_of(a)), 1],
            send_sem=two_send.at[a],
            recv_sem=two_recv.at[a],
            device_id=(my, sibling),
            device_id_type=MESH,
        )

    def start_first(a):
        for k in range(1, chips_x):
            first_copy(a, my, lax.rem(chip_x + k, chips_x)).start()

        def one(j, carry):
            for k in range(chips_x):
                first_copy(a, lax.rem(my + j, tiles_y), lax.rem(chip_x + k, chips_x)).start()
            return carry

        lax.fori_loop(1, tiles_y, one, 0)
        for part in range(parts_of(a)):
            one_in[a, mine, part] = one_out[a, mine, part]

    def pass_on(a):
        first_all(a).wait_recv()
        kept = []
        for part in range(parts_of(a)):
            parts = one_in[a, :, part].astype(F32).reshape(chips, 2, CAP, 128)
            low, high = parts[:, 0], parts[:, 1]
            other = jnp.where(core == 0, high, low).reshape(chips * CAP, 128)
            two_out[a, part] = other.astype(BF16)
            own = jnp.where(core == 0, low, high).reshape(chips * CAP, 128)
            kept.append(own.astype(BF16))
        second_copy(a).start()
        for part in range(parts_of(a)):
            two_in[a, part, 0] = kept[part]

    def sum_copy(x):
        return pltpu.make_async_remote_copy(
            src_ref=sum_out,
            dst_ref=sum_in.at[chip_x],
            send_sem=sum_send.at[0],
            recv_sem=sum_recv.at[0],
            device_id=(my, 2 * x + core),
            device_id_type=MESH,
        )

    def total_copy(y):
        return pltpu.make_async_remote_copy(
            src_ref=total_out,
            dst_ref=total_in.at[my],
            send_sem=sum_send.at[1],
            recv_sem=sum_recv.at[1],
            device_id=(y, mx),
            device_id_type=MESH,
        )

    def sum_all():
        return pltpu.make_async_remote_copy(
            src_ref=sum_in.at[pl.ds(0, chips_x - 1)],
            dst_ref=sum_in.at[pl.ds(0, chips_x - 1)],
            send_sem=sum_send.at[0],
            recv_sem=sum_recv.at[0],
            device_id=(my, sibling),
            device_id_type=MESH,
        )

    def total_all():
        return pltpu.make_async_remote_copy(
            src_ref=total_in.at[pl.ds(0, tiles_y - 1)],
            dst_ref=total_in.at[pl.ds(0, tiles_y - 1)],
            send_sem=sum_send.at[1],
            recv_sem=sum_recv.at[1],
            device_id=(my, sibling),
            device_id_type=MESH,
        )

    def last_copy():
        return pltpu.make_async_remote_copy(
            src_ref=last_in.at[0],
            dst_ref=last_in.at[1],
            send_sem=sum_send.at[2],
            recv_sem=sum_recv.at[2],
            device_id=(my, sibling),
            device_id_type=MESH,
        )

    def unit(r, h):
        return pl.ds(r, CHUNK), pl.ds(pl.multiple_of(128 * h, 128), 128)

    def strip_rows(r, h, g):
        return pl.ds(pl.multiple_of((8 * h + g) * ROWS + r, CHUNK), CHUNK)

    def over_cells(work, sent, carry, wide):
        def step(j, carry):
            def one(u, carry):
                for k in range(wide):
                    number = u * wide + k
                    r = pl.multiple_of((number // 2) * HALF + j * CHUNK, CHUNK)
                    carry = work(r, number % 2, carry)
                return carry

            carry = one(0, carry) if wide == 4 else lax.fori_loop(0, 4 // wide, one, carry)
            if sent is not None:
                send_rows(sent, j)
            return carry

        return lax.fori_loop(0, STEPS, step, carry)

    def shares(it, r, h, wages, revenue):
        rows, lanes = unit(r, h)
        powers = [w * w * w for w in wages]
        inverse = 1.0 / sum(powers[1:], powers[0])
        people = resident_ref[rows, lanes]
        share = [p * inverse for p in powers]
        income = sum([q * w for q, w in zip(share[1:], wages[1:])], share[0] * wages[0])
        income_ref[it, rows, lanes] = income
        supply = [people * q for q in share]
        for s in range(SECTORS):
            ext[2 * it, s, pl.ds(HALF + r, CHUNK), lanes] = supply[s].astype(BF16)
        for g, strip in enumerate(swap_blocks(supply)):
            table[strip_rows(r, h, g), :] = strip.astype(BF16)
        gain = people * rate_ref[rows, lanes] * income
        return revenue + gain[0:8] + gain[8:16]

    def gather(a):
        picked = jnp.dot(source_hot[...], table[...], preferred_element_type=F32).astype(BF16)
        ordered = jnp.dot(slot_hot[...], picked, preferred_element_type=F32).astype(BF16)
        one_out[a, :, 0] = ordered.reshape(chips, 2 * CAP, 128)

    zero = jnp.zeros((8, 128), F32)

    def first_cells(r, h, carry):
        people_sum, revenue = carry
        rows, lanes = unit(r, h)
        bracket = bracket_ref[rows, lanes]
        rate = jnp.zeros((CHUNK, 128), F32)
        for b in range(8):
            rate = jnp.where(bracket == b, tax_ref[b], rate)
        rate_ref[rows, lanes] = rate
        people = resident_ref[rows, lanes]
        people_sum = people_sum + people[0:8] + people[8:16]
        wages = [base_ref[s, rows, lanes].astype(F32) for s in range(SECTORS)]
        return people_sum, shares(0, r, h, wages, revenue)

    for load in loads:
        load.wait()
    people_sum, revenue0 = over_cells(first_cells, None, (zero, zero), 4)
    pl.semaphore_wait(barrier, chips + 1)
    for j in range(STEPS):
        send_rows(0, j)

    line = lax.broadcasted_iota(jnp.int32, (8, far_pairs), 0)
    source, target = src_ref[...], dst_ref[...]
    row, group = target >> 4, target & 15
    fields = [
        dest_ref[...],
        (source & 15) * ROWS + (source >> 4),
        ((((row >> 4) & 3) * 2 + (row >> 6)) * GROUPS) + group,
        row & 15,
        count_ref[...],
    ]
    pairs = jnp.zeros((8, far_pairs), jnp.int32)
    for k, field in enumerate(fields):
        pairs = jnp.where(line == k, field, pairs)
    pairs = pairs.astype(F32)
    across = jnp.concatenate([pairs, jnp.zeros((120, far_pairs), F32)], axis=0).T
    dest_row = pairs[0:1, :]
    earlier = lax.broadcasted_iota(jnp.int32, (far_pairs, far_pairs), 0) < (
        lax.broadcasted_iota(jnp.int32, (far_pairs, far_pairs), 1)
    )
    same = (across[:, 0:1] == dest_row) & earlier
    rank = jnp.sum(jnp.where(same, 1.0, 0.0), axis=0, keepdims=True)
    slot_of = (dest_row * CAP + rank).astype(jnp.int32)
    slot_ids = lax.broadcasted_iota(jnp.int32, (slots, far_pairs), 0)
    slot_hot[...] = jnp.where(slot_ids == slot_of, 1.0, 0.0).astype(BF16)
    strip_ids = lax.broadcasted_iota(jnp.int32, (far_pairs, GROUPS * ROWS), 1)
    source_hot[...] = jnp.where(
        strip_ids == across[:, 1:2].astype(jnp.int32), 1.0, 0.0
    ).astype(BF16)
    one_out[0, :, 1] = (
        jnp.dot(slot_hot[...], across.astype(BF16), preferred_element_type=F32)
        .astype(BF16)
        .reshape(chips, 2 * CAP, 128)
    )
    gather(0)
    start_first(0)

    @pl.when(my == 0)
    def _():
        ext[:, :, 0:HALF, :] = jnp.zeros((2 * ITERS, SECTORS, HALF, COLS), BF16)

    @pl.when(my == tiles_y - 1)
    def _():
        ext[:, :, HALF + ROWS :, :] = jnp.zeros((2 * ITERS, SECTORS, HALF, COLS), BF16)

    @pl.when(mx == 0)
    def _():
        edge_in[:, 0] = jnp.zeros((2 * ITERS, PAIRS2, ROWS, 128), BF16)

    @pl.when(mx == tiles_x - 1)
    def _():
        edge_in[:, 1] = jnp.zeros((2 * ITERS, PAIRS2, ROWS, 128), BF16)

    sector = lax.broadcasted_iota(jnp.int32, (2 * SECTORS, COLS), 0)
    tap = lax.broadcasted_iota(jnp.int32, (2 * SECTORS, COLS), 1)
    decay = jnp.zeros((2 * SECTORS, COLS), F32)
    for s in range(SECTORS):
        decay = jnp.where(sector == s, commute_ref[s], decay)
        decay = jnp.where(sector == SECTORS + s, spill_ref[s], decay)
    offset = jnp.abs(tap - HALF).astype(F32) / HALF
    unscaled = jnp.where(tap <= 2 * HALF, jnp.exp(-decay * offset), 0.0)
    tap_row[...] = (unscaled / jnp.sum(unscaled, axis=1, keepdims=True)).astype(BF16).astype(F32)
    make_bands(0)


    def build_place():
        routing = two_in[0, 1].reshape(slots, 128)
        line = lax.broadcasted_iota(jnp.int32, (16, 128), 0)
        lane = lax.broadcasted_iota(jnp.int32, (16, 128), 1)
        pick = jnp.where((line == 0) & (lane == 2), float(CHUNK), 0.0)
        pick = jnp.where((line == 0) & (lane == 3), 1.0, pick)
        pick = jnp.where((line == 1) & (lane == 4), 1.0, pick).astype(BF16)
        found = lax.dot_general(
            pick, routing, (((1,), (1,)), ((), ())), preferred_element_type=F32
        )
        where_to, weight = found[0:1, :].astype(jnp.int32), found[1:2, :]

        def one(g, carry):
            strip = g * ROWS + lax.broadcasted_iota(jnp.int32, (ROWS, slots), 0)
            place[pl.ds(pl.multiple_of(g * ROWS, ROWS), ROWS), :] = jnp.where(
                strip == where_to, weight, 0.0
            ).astype(BF16)
            return carry

        lax.fori_loop(0, GROUPS, one, 0)

    revenues = [revenue0]
    for it in range(ITERS):
        if it > 0:
            gather(it)
            start_first(it)
        if it == ITERS - 1:
            line = lax.broadcasted_iota(jnp.int32, (8, 128), 0)
            parts = zero
            for k, part in enumerate([people_sum] + revenues):
                parts = jnp.where(line == k, jnp.sum(part, axis=0, keepdims=True), parts)
            sum_out[...] = parts

            def start_sum(j, carry):
                sum_copy(lax.rem(chip_x + j, chips_x)).start()
                return carry

            lax.fori_loop(1, chips_x, start_sum, 0)
            sum_in[chip_x] = parts
        rows_pass(2 * it, 0)
        columns_start(0, near)
        pass_on(it)
        if it == ITERS - 1:
            sum_all().wait_recv()
            halfway = jnp.sum(sum_in[...], axis=0)
            total_out[...] = halfway

            def start_total(j, carry):
                total_copy(lax.rem(my + j, tiles_y)).start()
                return carry

            lax.fori_loop(1, tiles_y, start_total, 0)
            total_in[my] = halfway
        columns_finish(2 * it, 0, near)
        if it == ITERS - 1:
            total_all().wait_recv()
            last_in[0] = jnp.sum(total_in[...], axis=0)
            last_copy().start()
        second_copy(it).wait_recv()
        if it == 0:
            build_place()

        def labor_step(j, carry):
            block = 2 * GROUPS * CHUNK
            far[...] = jnp.dot(
                place[pl.ds(pl.multiple_of(j * block, block), block), :],
                two_in[it, 0].reshape(slots, 128),
                preferred_element_type=F32,
            )
            for number in range(4):
                way, h = number // 2, number % 2
                r = pl.multiple_of(way * HALF + j * CHUNK, CHUNK)
                rows, lanes = unit(r, h)
                first = (way * GROUPS + 8 * h) * CHUNK
                strips = [far[first + CHUNK * g : first + CHUNK * (g + 1), :] for g in range(8)]
                for s, flow in enumerate(swap_blocks(strips)):
                    value = near[s, rows, lanes] + FAR_SCALE * flow
                    labor[s, rows, lanes] = value
                    ext[2 * it + 1, s, pl.ds(HALF + r, CHUNK), lanes] = value.astype(BF16)
            send_rows(2 * it + 1, j)
            return carry

        lax.fori_loop(0, STEPS, labor_step, 0)
        if it == 0:
            make_bands(1)
        if it == ITERS - 1:
            last_copy().wait_recv()
            sums = jnp.sum(last_in[0] + last_in[1], axis=1, keepdims=True)
            people_all = sums[0:1, 0:1]
            transfers = [sums[1 + k : 2 + k, 0:1] / people_all for k in range(ITERS)]

            def rent_chunk(c, carry):
                rows = pl.ds(pl.multiple_of(c * CHUNK, CHUNK), CHUNK)
                keep = 1.0 - rate_ref[rows, :]
                people, space = resident_ref[rows, :], floor_ref[rows, :]
                ratio = people / space
                square = None
                for k in range(ITERS):
                    net = keep * income_ref[k, rows, :] + transfers[k]
                    level = ratio if square is None else jnp.sqrt(square) * ratio
                    square = level * net
                rent_ref[rows, :] = square
                return carry

            lax.fori_loop(0, ROWS // CHUNK, rent_chunk, 0)
        rows_pass(2 * it + 1, 1)
        columns_start(1, near)
        columns_finish(2 * it + 1, 1, near)

        def wage_cells(r, h, revenue):
            rows, lanes = unit(r, h)
            logs = [jnp.log(1.0 + near[s, rows, lanes]) for s in range(SECTORS)]
            wages = []
            for s in range(SECTORS):
                power = -BETA_WAGE * jnp.log(1.0 + labor[s, rows, lanes])
                for t in range(SECTORS):
                    power = power + mixing_ref[s, t] * logs[t]
                if it == ITERS - 1:
                    power_ref[s, rows, lanes] = power
                else:
                    wages.append(base_ref[s, rows, lanes].astype(F32) * jnp.exp(power))
            if it < ITERS - 1:
                revenue = shares(it + 1, r, h, wages, revenue)
            return revenue

        sent = 2 * it + 2 if it < ITERS - 1 else None
        revenues.append(over_cells(wage_cells, sent, zero, 2))

    for e in range(2 * ITERS):
        for way in range(2):

            @pl.when(can_row[way])
            def _():
                row_drain(e, way).wait_send()

            @pl.when(can_edge[way])
            def _():
                edge_drain(e, way).wait_send()

    for a in range(ITERS):
        first_all(a).wait_send()
        second_copy(a).wait_send()
    sum_all().wait_send()
    total_all().wait_send()
    last_copy().wait_send()


def body(
    base_prod,
    resident,
    floor_space,
    bracket,
    tax_rate,
    mixing,
    spill_decay,
    commute_decay,
    pair_dest,
    pair_src,
    pair_dst,
    pair_count,
):
    tiles_y = lax.axis_size("gy")
    tiles_x = lax.axis_size("gx")
    slots = tiles_y * tiles_x * CAP
    chips = tiles_y * tiles_x // 2
    far_pairs = pair_src.shape[0]
    vmem = pl.BlockSpec(memory_space=pltpu.VMEM)
    whole = pl.BlockSpec(memory_space=pltpu.HBM)
    smem = pltpu.SMEM
    exchanges = 2 * ITERS
    dma = pltpu.SemaphoreType.DMA
    power, square = pl.pallas_call(
        functools.partial(kernel, tiles_y, tiles_x),
        out_shape=(
            jax.ShapeDtypeStruct(base_prod.shape, F32),
            jax.ShapeDtypeStruct(resident.shape, F32),
        ),
        in_specs=[whole] * 12,
        out_specs=(vmem, vmem),
        scratch_shapes=[
            pltpu.VMEM((exchanges, SECTORS, ROWS + 2 * HALF, COLS), BF16),
            pltpu.VMEM((exchanges, 2, PAIRS2, ROWS, 128), BF16),
            pltpu.VMEM((exchanges, 2, PAIRS2, ROWS, 128), BF16),
            pltpu.VMEM((SECTORS, ROWS, COLS), BF16),
            pltpu.VMEM((SECTORS, ROWS, COLS), F32),
            pltpu.VMEM((SECTORS, ROWS, COLS), F32),
            pltpu.VMEM((2 * SECTORS, COLS), F32),
            pltpu.VMEM((2 * SECTORS, ROWS, COLS), BF16),
            pltpu.VMEM((2 * SECTORS, COLS, COLS), BF16),
            pltpu.VMEM((2 * SECTORS, 2, 128, 128), BF16),
            pltpu.VMEM((GROUPS * ROWS, 128), BF16),
            pltpu.VMEM((far_pairs, GROUPS * ROWS), BF16),
            pltpu.VMEM((slots, far_pairs), BF16),
            pltpu.VMEM((GROUPS * ROWS, slots), BF16),
            pltpu.VMEM((2 * GROUPS * CHUNK, 128), F32),
            pltpu.VMEM((ITERS, chips, 2, 2 * CAP, 128), BF16),
            pltpu.VMEM((ITERS, chips, 2, 2 * CAP, 128), BF16),
            pltpu.VMEM((ITERS, 2, chips * CAP, 128), BF16),
            pltpu.VMEM((ITERS, 2, 2, chips * CAP, 128), BF16),
            pltpu.VMEM((8, 128), F32),
            pltpu.VMEM((tiles_x // 2, 8, 128), F32),
            pltpu.VMEM((8, 128), F32),
            pltpu.VMEM((tiles_y, 8, 128), F32),
            pltpu.VMEM((ROWS, COLS), F32),
            pltpu.VMEM((ITERS, ROWS, COLS), F32),
            pltpu.VMEM((2, 8, 128), F32),
            pltpu.VMEM((SECTORS, ROWS, COLS), BF16),
            pltpu.VMEM((ROWS, COLS), F32),
            pltpu.VMEM((ROWS, COLS), F32),
            pltpu.VMEM((ROWS, COLS), jnp.int32),
            pltpu.VMEM((1, far_pairs), jnp.int32),
            pltpu.VMEM((1, far_pairs), jnp.int32),
            pltpu.VMEM((1, far_pairs), jnp.int32),
            pltpu.VMEM((1, far_pairs), jnp.int32),
            smem((8,), F32),
            smem((SECTORS,), F32),
            smem((SECTORS,), F32),
            smem((SECTORS, SECTORS), F32),
            dma((12,)),
            dma((exchanges, 2)),
            dma((exchanges, 2, STEPS)),
            dma((exchanges, 2)),
            dma((exchanges, 2, 2)),
            dma((ITERS,)),
            dma((ITERS,)),
            dma((ITERS,)),
            dma((ITERS,)),
            dma((3,)),
            dma((3,)),
        ],
        compiler_params=pltpu.CompilerParams(
            collective_id=0, has_side_effects=True, vmem_limit_bytes=40 * 1024 * 1024
        ),
    )(
        *(
            pltpu.with_memory_space_constraint(x, pltpu.HBM)
            for x in (
                base_prod,
                resident,
                floor_space,
                bracket,
                pair_dest.reshape(1, far_pairs),
                pair_src.reshape(1, far_pairs),
                pair_dst.reshape(1, far_pairs),
                pair_count.reshape(1, far_pairs),
                tax_rate,
                commute_decay,
                spill_decay,
                mixing,
            )
        )
    )
    return base_prod.astype(F32) * jnp.exp(power), jnp.sqrt(square)


def solution(mesh):
    return jax.shard_map(
        body,
        mesh=mesh,
        in_specs=(
            P(None, "gy", "gx"),
            P("gy", "gx"),
            P("gy", "gx"),
            P("gy", "gx"),
            P(),
            P(),
            P(),
            P(),
            P(("gy", "gx"), None),
            P(("gy", "gx")),
            P(("gy", "gx")),
            P(("gy", "gx")),
        ),
        out_specs=(P(None, "gy", "gx"), P("gy", "gx")),
        check_vma=False,
    )
```

```python
import functools

import jax
import jax.numpy as jnp
from jax import lax
from jax.experimental import pallas as pl
from jax.experimental.pallas import tpu as pltpu
from jax.sharding import PartitionSpec as P

HALF = 64
ITERS = 3
SECTORS = 8
CAP = 8
BETA_WAGE = 0.3
FAR_SCALE = 0.125
ROWS = 128
COLS = 256
GROUPS = COLS // 16
PAIRS2 = SECTORS // 2
CHUNK = 16
STEPS = HALF // CHUNK
PARTS = ((0, 3), (3, 1))
MESH = pl.DeviceIdType.MESH
F32 = jnp.float32
BF16 = jnp.bfloat16


def swap_blocks(values):
    values = [pltpu.roll(v, 16 * s, 1) if s else v for s, v in enumerate(values)]
    block = lax.broadcasted_iota(jnp.int32, values[0].shape, 1) // 16
    for d in (1, 2, 4):
        moved = (block & d) != 0
        values = [jnp.where(moved, values[(a + d) % 8], values[a]) for a in range(8)]
    values = [values[-g % 8] for g in range(8)]
    return [pltpu.roll(v, 128 - 16 * g, 1) if g else v for g, v in enumerate(values)]


def kernel(
    tiles_y,
    tiles_x,
    base_any,
    resident_any,
    floor_any,
    bracket_any,
    dest_any,
    src_any,
    dst_any,
    count_any,
    tax_any,
    commute_any,
    spill_any,
    mixing_any,
    power_ref,
    rent_ref,
    ext,
    edge_out,
    edge_in,
    mid,
    near,
    labor,
    tap_row,
    band_row,
    band_col,
    band_edge,
    table,
    source_hot,
    slot_hot,
    place,
    far,
    one_out,
    one_in,
    two_out,
    two_in,
    sum_out,
    sum_in,
    total_out,
    total_in,
    rate_ref,
    income_ref,
    last_in,
    base_ref,
    resident_ref,
    floor_ref,
    bracket_ref,
    dest_ref,
    src_ref,
    dst_ref,
    count_ref,
    tax_ref,
    commute_ref,
    spill_ref,
    mixing_ref,
    load_sem,
    row_send,
    row_recv,
    edge_send,
    edge_recv,
    one_send,
    one_recv,
    two_send,
    two_recv,
    sum_send,
    sum_recv,
):
    my = lax.axis_index("gy")
    mx = lax.axis_index("gx")
    chips_x = tiles_x // 2
    chips = tiles_y * chips_x
    core = lax.rem(mx, 2)
    chip_x = mx // 2
    sibling = mx + 1 - 2 * core
    beyond = lax.rem(mx + 2 * core - 1 + tiles_x, tiles_x)
    mine = my * chips_x + chip_x
    slots = tiles_y * tiles_x * CAP
    far_pairs = dest_ref.shape[1]

    loads = [
        pltpu.make_async_copy(source, target, load_sem.at[k])
        for k, (source, target) in enumerate(
            (
                (base_any, base_ref),
                (resident_any, resident_ref),
                (bracket_any, bracket_ref),
                (floor_any, floor_ref),
                (dest_any, dest_ref),
                (src_any, src_ref),
                (dst_any, dst_ref),
                (count_any, count_ref),
                (tax_any, tax_ref),
                (commute_any, commute_ref),
                (spill_any, spill_ref),
                (mixing_any, mixing_ref),
            )
        )
    ]
    for load in loads:
        load.start()

    barrier = pltpu.get_barrier_semaphore()

    def chip_at(j):
        return lax.rem(my + j // chips_x, tiles_y), lax.rem(chip_x + lax.rem(j, chips_x), chips_x)

    def greet(y, x):
        pl.semaphore_signal(barrier, inc=1, device_id=(y, x), device_id_type=MESH)

    def greet_chip(j, carry):
        y, x = chip_at(j)
        greet(y, 2 * x + core)
        return carry

    greet(my, sibling)
    greet(my, beyond)
    lax.fori_loop(1, chips, greet_chip, 0)

    def row_copy(e, way, sectors, j, height, slot):
        start = HALF if way == 0 else ROWS
        land = HALF + ROWS if way == 0 else 0
        target = my - 1 if way == 0 else my + 1
        step = pl.multiple_of(j * height, height)
        return pltpu.make_async_remote_copy(
            src_ref=ext.at[e, sectors, pl.ds(start + step, height), :],
            dst_ref=ext.at[e, sectors, pl.ds(land + step, height), :],
            send_sem=row_send.at[e, way],
            recv_sem=row_recv.at[e, way, slot],
            device_id=(target, mx),
            device_id_type=MESH,
        )

    def row_step(e, way, j):
        return row_copy(e, way, pl.ds(0, 2 * PARTS[0][1]), j, CHUNK, j)

    def row_rest(e, way):
        return row_copy(e, way, pl.ds(2 * PARTS[1][0], 2 * PARTS[1][1]), 0, HALF, STEPS)

    def row_drain(e, way):
        start = HALF if way == 0 else ROWS
        target = my - 1 if way == 0 else my + 1
        return pltpu.make_async_remote_copy(
            src_ref=ext.at[e, :, pl.ds(start, HALF), :],
            dst_ref=ext.at[e, :, pl.ds(start, HALF), :],
            send_sem=row_send.at[e, way],
            recv_sem=row_recv.at[e, way, 0],
            device_id=(target, mx),
            device_id_type=MESH,
        )

    can_row = (my > 0, my < tiles_y - 1)
    can_edge = (mx > 0, mx < tiles_x - 1)

    def send_rows(e, j):
        for way in range(2):

            @pl.when(can_row[way])
            def _():
                row_step(e, way, j).start()

    def send_rest(e):
        for way in range(2):

            @pl.when(can_row[way])
            def _():
                row_rest(e, way).start()

    def wait_rows(e, part):
        for way in range(2):

            @pl.when(can_row[1 - way])
            def _():
                if part == 0:
                    for j in range(STEPS):
                        row_step(e, way, j).wait_recv()
                else:
                    row_rest(e, way).wait_recv()

    def edge_copy(e, part, way):
        target = mx - 1 if way == 0 else mx + 1
        pairs = pl.ds(*PARTS[part])
        return pltpu.make_async_remote_copy(
            src_ref=edge_out.at[e, way, pairs],
            dst_ref=edge_in.at[e, 1 - way, pairs],
            send_sem=edge_send.at[e, way],
            recv_sem=edge_recv.at[e, way, part],
            device_id=(my, target),
            device_id_type=MESH,
        )

    def edge_drain(e, way):
        target = mx - 1 if way == 0 else mx + 1
        return pltpu.make_async_remote_copy(
            src_ref=edge_out.at[e, way],
            dst_ref=edge_in.at[e, 1 - way],
            send_sem=edge_send.at[e, way],
            recv_sem=edge_recv.at[e, way, 0],
            device_id=(my, target),
            device_id_type=MESH,
        )

    lane128 = lax.broadcasted_iota(jnp.int32, (ROWS, 128), 1)

    def rows_pass(e, kind):
        for part, (first_pair, count) in enumerate(PARTS):
            wait_rows(e, part)
            for i in range(first_pair, first_pair + count):
                ends = []
                for s in (2 * i, 2 * i + 1):
                    passed = jnp.dot(
                        band_row[kind * SECTORS + s], ext[e, s], preferred_element_type=F32
                    )
                    mid[s] = passed.astype(BF16)
                    ends.append((passed[:, 0:128], passed[:, 128:256]))
                first, second = ends
                low = lane128 < HALF
                edge_out[e, 0, i] = jnp.where(
                    low, first[0], pltpu.roll(second[0], HALF, 1)
                ).astype(BF16)
                edge_out[e, 1, i] = jnp.where(
                    low, pltpu.roll(second[1], HALF, 1), first[1]
                ).astype(BF16)
            for way in range(2):

                @pl.when(can_edge[way])
                def _():
                    edge_copy(e, part, way).start()

    def columns_start(kind, result):
        def one(half, carry):
            for k in range(4):
                s = 4 * half + k
                result[s] = jnp.dot(
                    mid[s], band_col[kind * SECTORS + s], preferred_element_type=F32
                )
            return carry

        lax.fori_loop(0, 2, one, 0)

    def columns_finish(e, kind, result):
        for part, (first_pair, count) in enumerate(PARTS):
            for way in range(2):

                @pl.when(can_edge[1 - way])
                def _():
                    edge_copy(e, part, way).wait_recv()

            for s in range(2 * first_pair, 2 * (first_pair + count)):
                for side in range(2):
                    lanes = slice(128 * side, 128 * side + 128)
                    result[s, :, lanes] += jnp.dot(
                        edge_in[e, side, s // 2],
                        band_edge[kind * SECTORS + s, side],
                        preferred_element_type=F32,
                    )

    def make_bands(kind):
        u = lax.broadcasted_iota(jnp.int32, (COLS, COLS), 0)
        x = lax.broadcasted_iota(jnp.int32, (COLS, COLS), 1)
        inside = jnp.abs(u - x) <= 128

        def one(s, carry):
            b = kind * SECTORS + s
            line = jnp.broadcast_to(tap_row[pl.ds(b, 1), :], (ROWS, COLS))
            rows_band = pltpu.roll(line, 0, 1, stride=1, stride_axis=0)
            band_row[b] = rows_band.astype(BF16)
            circle = jnp.concatenate(
                [pltpu.roll(rows_band, COLS - HALF, 1), pltpu.roll(rows_band, HALF, 1)], axis=0
            )
            band_col[b] = jnp.where(inside, circle, 0.0).astype(BF16)
            rest = jnp.where(inside, 0.0, circle)
            swap = lax.rem(s, 2) == 1
            for side in range(2):
                block = rest[128 - 128 * side : 256 - 128 * side, 128 * side : 128 * side + 128]
                turned = jnp.concatenate([block[HALF:], block[:HALF]], axis=0)
                band_edge[b, side] = jnp.where(swap, turned, block).astype(BF16)
            return carry

        lax.fori_loop(0, SECTORS, one, 0)

    def parts_of(a):
        return 2 if a == 0 else 1

    def first_copy(a, y, x):
        return pltpu.make_async_remote_copy(
            src_ref=one_out.at[a, y * chips_x + x, pl.ds(0, parts_of(a))],
            dst_ref=one_in.at[a, mine, pl.ds(0, parts_of(a))],
            send_sem=one_send.at[a],
            recv_sem=one_recv.at[a],
            device_id=(y, 2 * x + core),
            device_id_type=MESH,
        )

    def first_all(a):
        return pltpu.make_async_remote_copy(
            src_ref=one_out.at[a, pl.ds(0, chips - 1), pl.ds(0, parts_of(a))],
            dst_ref=one_in.at[a, pl.ds(0, chips - 1), pl.ds(0, parts_of(a))],
            send_sem=one_send.at[a],
            recv_sem=one_recv.at[a],
            device_id=(my, sibling),
            device_id_type=MESH,
        )

    def second_copy(a):
        return pltpu.make_async_remote_copy(
            src_ref=two_out.at[a, pl.ds(0, parts_of(a))],
            dst_ref=two_in.at[a, pl.ds(0, parts_of(a)), 1],
            send_sem=two_send.at[a],
            recv_sem=two_recv.at[a],
            device_id=(my, sibling),
            device_id_type=MESH,
        )

    def start_first(a):
        for k in range(1, chips_x):
            first_copy(a, my, lax.rem(chip_x + k, chips_x)).start()

        def one(j, carry):
            for k in range(chips_x):
                first_copy(a, lax.rem(my + j, tiles_y), lax.rem(chip_x + k, chips_x)).start()
            return carry

        lax.fori_loop(1, tiles_y, one, 0)
        for part in range(parts_of(a)):
            one_in[a, mine, part] = one_out[a, mine, part]

    def pass_on(a):
        first_all(a).wait_recv()
        kept = []
        for part in range(parts_of(a)):
            parts = one_in[a, :, part].astype(F32).reshape(chips, 2, CAP, 128)
            low, high = parts[:, 0], parts[:, 1]
            other = jnp.where(core == 0, high, low).reshape(chips * CAP, 128)
            two_out[a, part] = other.astype(BF16)
            own = jnp.where(core == 0, low, high).reshape(chips * CAP, 128)
            kept.append(own.astype(BF16))
        second_copy(a).start()
        for part in range(parts_of(a)):
            two_in[a, part, 0] = kept[part]

    def sum_copy(x):
        return pltpu.make_async_remote_copy(
            src_ref=sum_out,
            dst_ref=sum_in.at[chip_x],
            send_sem=sum_send.at[0],
            recv_sem=sum_recv.at[0],
            device_id=(my, 2 * x + core),
            device_id_type=MESH,
        )

    def total_copy(y):
        return pltpu.make_async_remote_copy(
            src_ref=total_out,
            dst_ref=total_in.at[my],
            send_sem=sum_send.at[1],
            recv_sem=sum_recv.at[1],
            device_id=(y, mx),
            device_id_type=MESH,
        )

    def sum_all():
        return pltpu.make_async_remote_copy(
            src_ref=sum_in.at[pl.ds(0, chips_x - 1)],
            dst_ref=sum_in.at[pl.ds(0, chips_x - 1)],
            send_sem=sum_send.at[0],
            recv_sem=sum_recv.at[0],
            device_id=(my, sibling),
            device_id_type=MESH,
        )

    def total_all():
        return pltpu.make_async_remote_copy(
            src_ref=total_in.at[pl.ds(0, tiles_y - 1)],
            dst_ref=total_in.at[pl.ds(0, tiles_y - 1)],
            send_sem=sum_send.at[1],
            recv_sem=sum_recv.at[1],
            device_id=(my, sibling),
            device_id_type=MESH,
        )

    def last_copy():
        return pltpu.make_async_remote_copy(
            src_ref=last_in.at[0],
            dst_ref=last_in.at[1],
            send_sem=sum_send.at[2],
            recv_sem=sum_recv.at[2],
            device_id=(my, sibling),
            device_id_type=MESH,
        )

    def unit(r, h):
        return pl.ds(r, CHUNK), pl.ds(pl.multiple_of(128 * h, 128), 128)

    def strip_rows(r, h, g):
        return pl.ds(pl.multiple_of((8 * h + g) * ROWS + r, CHUNK), CHUNK)

    def over_cells(work, sent, carry, wide):
        def step(j, carry):
            def one(u, carry):
                for k in range(wide):
                    number = u * wide + k
                    r = pl.multiple_of((number // 2) * HALF + j * CHUNK, CHUNK)
                    carry = work(r, number % 2, carry)
                return carry

            carry = one(0, carry) if wide == 4 else lax.fori_loop(0, 4 // wide, one, carry)
            if sent is not None:
                send_rows(sent, j)
            return carry

        carry = lax.fori_loop(0, STEPS, step, carry)
        if sent is not None:
            send_rest(sent)
        return carry

    def shares(it, r, h, wages, revenue):
        rows, lanes = unit(r, h)
        powers = [w * w * w for w in wages]
        inverse = 1.0 / sum(powers[1:], powers[0])
        people = resident_ref[rows, lanes]
        share = [p * inverse for p in powers]
        income = sum([q * w for q, w in zip(share[1:], wages[1:])], share[0] * wages[0])
        income_ref[it, rows, lanes] = income
        supply = [people * q for q in share]
        for s in range(SECTORS):
            ext[2 * it, s, pl.ds(HALF + r, CHUNK), lanes] = supply[s].astype(BF16)
        for g, strip in enumerate(swap_blocks(supply)):
            table[strip_rows(r, h, g), :] = strip.astype(BF16)
        gain = people * rate_ref[rows, lanes] * income
        return revenue + gain[0:8] + gain[8:16]

    def gather(a):
        picked = jnp.dot(source_hot[...], table[...], preferred_element_type=F32).astype(BF16)
        ordered = jnp.dot(slot_hot[...], picked, preferred_element_type=F32).astype(BF16)
        one_out[a, :, 0] = ordered.reshape(chips, 2 * CAP, 128)

    zero = jnp.zeros((8, 128), F32)

    def first_cells(r, h, carry):
        people_sum, revenue = carry
        rows, lanes = unit(r, h)
        bracket = bracket_ref[rows, lanes]
        rate = jnp.zeros((CHUNK, 128), F32)
        for b in range(8):
            rate = jnp.where(bracket == b, tax_ref[b], rate)
        rate_ref[rows, lanes] = rate
        people = resident_ref[rows, lanes]
        people_sum = people_sum + people[0:8] + people[8:16]
        wages = [base_ref[s, rows, lanes].astype(F32) for s in range(SECTORS)]
        return people_sum, shares(0, r, h, wages, revenue)

    for load in loads:
        load.wait()
    people_sum, revenue0 = over_cells(first_cells, None, (zero, zero), 4)
    pl.semaphore_wait(barrier, chips + 1)
    for j in range(STEPS):
        send_rows(0, j)
    send_rest(0)

    line = lax.broadcasted_iota(jnp.int32, (8, far_pairs), 0)
    source, target = src_ref[...], dst_ref[...]
    row, group = target >> 4, target & 15
    fields = [
        dest_ref[...],
        (source & 15) * ROWS + (source >> 4),
        ((((row >> 4) & 3) * 2 + (row >> 6)) * GROUPS) + group,
        row & 15,
        count_ref[...],
    ]
    pairs = jnp.zeros((8, far_pairs), jnp.int32)
    for k, field in enumerate(fields):
        pairs = jnp.where(line == k, field, pairs)
    pairs = pairs.astype(F32)
    across = jnp.concatenate([pairs, jnp.zeros((120, far_pairs), F32)], axis=0).T
    dest_row = pairs[0:1, :]
    earlier = lax.broadcasted_iota(jnp.int32, (far_pairs, far_pairs), 0) < (
        lax.broadcasted_iota(jnp.int32, (far_pairs, far_pairs), 1)
    )
    same = (across[:, 0:1] == dest_row) & earlier
    rank = jnp.sum(jnp.where(same, 1.0, 0.0), axis=0, keepdims=True)
    slot_of = (dest_row * CAP + rank).astype(jnp.int32)
    slot_ids = lax.broadcasted_iota(jnp.int32, (slots, far_pairs), 0)
    slot_hot[...] = jnp.where(slot_ids == slot_of, 1.0, 0.0).astype(BF16)
    strip_ids = lax.broadcasted_iota(jnp.int32, (far_pairs, GROUPS * ROWS), 1)
    source_hot[...] = jnp.where(
        strip_ids == across[:, 1:2].astype(jnp.int32), 1.0, 0.0
    ).astype(BF16)
    one_out[0, :, 1] = (
        jnp.dot(slot_hot[...], across.astype(BF16), preferred_element_type=F32)
        .astype(BF16)
        .reshape(chips, 2 * CAP, 128)
    )
    gather(0)
    start_first(0)

    @pl.when(my == 0)
    def _():
        ext[:, :, 0:HALF, :] = jnp.zeros((2 * ITERS, SECTORS, HALF, COLS), BF16)

    @pl.when(my == tiles_y - 1)
    def _():
        ext[:, :, HALF + ROWS :, :] = jnp.zeros((2 * ITERS, SECTORS, HALF, COLS), BF16)

    @pl.when(mx == 0)
    def _():
        edge_in[:, 0] = jnp.zeros((2 * ITERS, PAIRS2, ROWS, 128), BF16)

    @pl.when(mx == tiles_x - 1)
    def _():
        edge_in[:, 1] = jnp.zeros((2 * ITERS, PAIRS2, ROWS, 128), BF16)

    sector = lax.broadcasted_iota(jnp.int32, (2 * SECTORS, COLS), 0)
    tap = lax.broadcasted_iota(jnp.int32, (2 * SECTORS, COLS), 1)
    decay = jnp.zeros((2 * SECTORS, COLS), F32)
    for s in range(SECTORS):
        decay = jnp.where(sector == s, commute_ref[s], decay)
        decay = jnp.where(sector == SECTORS + s, spill_ref[s], decay)
    offset = jnp.abs(tap - HALF).astype(F32) / HALF
    unscaled = jnp.where(tap <= 2 * HALF, jnp.exp(-decay * offset), 0.0)
    tap_row[...] = (unscaled / jnp.sum(unscaled, axis=1, keepdims=True)).astype(BF16).astype(F32)
    make_bands(0)


    def build_place():
        routing = two_in[0, 1].reshape(slots, 128)
        line = lax.broadcasted_iota(jnp.int32, (16, 128), 0)
        lane = lax.broadcasted_iota(jnp.int32, (16, 128), 1)
        pick = jnp.where((line == 0) & (lane == 2), float(CHUNK), 0.0)
        pick = jnp.where((line == 0) & (lane == 3), 1.0, pick)
        pick = jnp.where((line == 1) & (lane == 4), 1.0, pick).astype(BF16)
        found = lax.dot_general(
            pick, routing, (((1,), (1,)), ((), ())), preferred_element_type=F32
        )
        where_to, weight = found[0:1, :].astype(jnp.int32), found[1:2, :]

        def one(g, carry):
            strip = g * ROWS + lax.broadcasted_iota(jnp.int32, (ROWS, slots), 0)
            place[pl.ds(pl.multiple_of(g * ROWS, ROWS), ROWS), :] = jnp.where(
                strip == where_to, weight, 0.0
            ).astype(BF16)
            return carry

        lax.fori_loop(0, GROUPS, one, 0)

    revenues = [revenue0]
    for it in range(ITERS):
        if it > 0:
            gather(it)
            start_first(it)
        if it == ITERS - 1:
            line = lax.broadcasted_iota(jnp.int32, (8, 128), 0)
            parts = zero
            for k, part in enumerate([people_sum] + revenues):
                parts = jnp.where(line == k, jnp.sum(part, axis=0, keepdims=True), parts)
            sum_out[...] = parts

            def start_sum(j, carry):
                sum_copy(lax.rem(chip_x + j, chips_x)).start()
                return carry

            lax.fori_loop(1, chips_x, start_sum, 0)
            sum_in[chip_x] = parts
        rows_pass(2 * it, 0)
        columns_start(0, near)
        pass_on(it)
        if it == ITERS - 1:
            sum_all().wait_recv()
            halfway = jnp.sum(sum_in[...], axis=0)
            total_out[...] = halfway

            def start_total(j, carry):
                total_copy(lax.rem(my + j, tiles_y)).start()
                return carry

            lax.fori_loop(1, tiles_y, start_total, 0)
            total_in[my] = halfway
        columns_finish(2 * it, 0, near)
        if it == ITERS - 1:
            total_all().wait_recv()
            last_in[0] = jnp.sum(total_in[...], axis=0)
            last_copy().start()
        second_copy(it).wait_recv()
        if it == 0:
            build_place()

        def labor_step(j, carry):
            block = 2 * GROUPS * CHUNK
            far[...] = jnp.dot(
                place[pl.ds(pl.multiple_of(j * block, block), block), :],
                two_in[it, 0].reshape(slots, 128),
                preferred_element_type=F32,
            )
            for number in range(4):
                way, h = number // 2, number % 2
                r = pl.multiple_of(way * HALF + j * CHUNK, CHUNK)
                rows, lanes = unit(r, h)
                first = (way * GROUPS + 8 * h) * CHUNK
                strips = [far[first + CHUNK * g : first + CHUNK * (g + 1), :] for g in range(8)]
                for s, flow in enumerate(swap_blocks(strips)):
                    value = near[s, rows, lanes] + FAR_SCALE * flow
                    labor[s, rows, lanes] = value
                    ext[2 * it + 1, s, pl.ds(HALF + r, CHUNK), lanes] = value.astype(BF16)
            send_rows(2 * it + 1, j)
            return carry

        lax.fori_loop(0, STEPS, labor_step, 0)
        send_rest(2 * it + 1)
        if it == 0:
            make_bands(1)
        if it == ITERS - 1:
            last_copy().wait_recv()
            sums = jnp.sum(last_in[0] + last_in[1], axis=1, keepdims=True)
            people_all = sums[0:1, 0:1]
            transfers = [sums[1 + k : 2 + k, 0:1] / people_all for k in range(ITERS)]

            def rent_chunk(c, carry):
                rows = pl.ds(pl.multiple_of(c * CHUNK, CHUNK), CHUNK)
                keep = 1.0 - rate_ref[rows, :]
                people, space = resident_ref[rows, :], floor_ref[rows, :]
                ratio = people / space
                square = None
                for k in range(ITERS):
                    net = keep * income_ref[k, rows, :] + transfers[k]
                    level = ratio if square is None else jnp.sqrt(square) * ratio
                    square = level * net
                rent_ref[rows, :] = square
                return carry

            lax.fori_loop(0, ROWS // CHUNK, rent_chunk, 0)
        rows_pass(2 * it + 1, 1)
        columns_start(1, near)
        columns_finish(2 * it + 1, 1, near)

        def wage_cells(r, h, revenue):
            rows, lanes = unit(r, h)
            logs = [jnp.log(1.0 + near[s, rows, lanes]) for s in range(SECTORS)]
            wages = []
            for s in range(SECTORS):
                power = -BETA_WAGE * jnp.log(1.0 + labor[s, rows, lanes])
                for t in range(SECTORS):
                    power = power + mixing_ref[s, t] * logs[t]
                if it == ITERS - 1:
                    power_ref[s, rows, lanes] = power
                else:
                    wages.append(base_ref[s, rows, lanes].astype(F32) * jnp.exp(power))
            if it < ITERS - 1:
                revenue = shares(it + 1, r, h, wages, revenue)
            return revenue

        sent = 2 * it + 2 if it < ITERS - 1 else None
        revenues.append(over_cells(wage_cells, sent, zero, 2))

    for e in range(2 * ITERS):
        for way in range(2):

            @pl.when(can_row[way])
            def _():
                row_drain(e, way).wait_send()

            @pl.when(can_edge[way])
            def _():
                edge_drain(e, way).wait_send()

    for a in range(ITERS):
        first_all(a).wait_send()
        second_copy(a).wait_send()
    sum_all().wait_send()
    total_all().wait_send()
    last_copy().wait_send()


def body(
    base_prod,
    resident,
    floor_space,
    bracket,
    tax_rate,
    mixing,
    spill_decay,
    commute_decay,
    pair_dest,
    pair_src,
    pair_dst,
    pair_count,
):
    tiles_y = lax.axis_size("gy")
    tiles_x = lax.axis_size("gx")
    slots = tiles_y * tiles_x * CAP
    chips = tiles_y * tiles_x // 2
    far_pairs = pair_src.shape[0]
    vmem = pl.BlockSpec(memory_space=pltpu.VMEM)
    whole = pl.BlockSpec(memory_space=pltpu.HBM)
    smem = pltpu.SMEM
    exchanges = 2 * ITERS
    dma = pltpu.SemaphoreType.DMA
    power, square = pl.pallas_call(
        functools.partial(kernel, tiles_y, tiles_x),
        out_shape=(
            jax.ShapeDtypeStruct(base_prod.shape, F32),
            jax.ShapeDtypeStruct(resident.shape, F32),
        ),
        in_specs=[whole] * 12,
        out_specs=(vmem, vmem),
        scratch_shapes=[
            pltpu.VMEM((exchanges, SECTORS, ROWS + 2 * HALF, COLS), BF16),
            pltpu.VMEM((exchanges, 2, PAIRS2, ROWS, 128), BF16),
            pltpu.VMEM((exchanges, 2, PAIRS2, ROWS, 128), BF16),
            pltpu.VMEM((SECTORS, ROWS, COLS), BF16),
            pltpu.VMEM((SECTORS, ROWS, COLS), F32),
            pltpu.VMEM((SECTORS, ROWS, COLS), F32),
            pltpu.VMEM((2 * SECTORS, COLS), F32),
            pltpu.VMEM((2 * SECTORS, ROWS, COLS), BF16),
            pltpu.VMEM((2 * SECTORS, COLS, COLS), BF16),
            pltpu.VMEM((2 * SECTORS, 2, 128, 128), BF16),
            pltpu.VMEM((GROUPS * ROWS, 128), BF16),
            pltpu.VMEM((far_pairs, GROUPS * ROWS), BF16),
            pltpu.VMEM((slots, far_pairs), BF16),
            pltpu.VMEM((GROUPS * ROWS, slots), BF16),
            pltpu.VMEM((2 * GROUPS * CHUNK, 128), F32),
            pltpu.VMEM((ITERS, chips, 2, 2 * CAP, 128), BF16),
            pltpu.VMEM((ITERS, chips, 2, 2 * CAP, 128), BF16),
            pltpu.VMEM((ITERS, 2, chips * CAP, 128), BF16),
            pltpu.VMEM((ITERS, 2, 2, chips * CAP, 128), BF16),
            pltpu.VMEM((8, 128), F32),
            pltpu.VMEM((tiles_x // 2, 8, 128), F32),
            pltpu.VMEM((8, 128), F32),
            pltpu.VMEM((tiles_y, 8, 128), F32),
            pltpu.VMEM((ROWS, COLS), F32),
            pltpu.VMEM((ITERS, ROWS, COLS), F32),
            pltpu.VMEM((2, 8, 128), F32),
            pltpu.VMEM((SECTORS, ROWS, COLS), BF16),
            pltpu.VMEM((ROWS, COLS), F32),
            pltpu.VMEM((ROWS, COLS), F32),
            pltpu.VMEM((ROWS, COLS), jnp.int32),
            pltpu.VMEM((1, far_pairs), jnp.int32),
            pltpu.VMEM((1, far_pairs), jnp.int32),
            pltpu.VMEM((1, far_pairs), jnp.int32),
            pltpu.VMEM((1, far_pairs), jnp.int32),
            smem((8,), F32),
            smem((SECTORS,), F32),
            smem((SECTORS,), F32),
            smem((SECTORS, SECTORS), F32),
            dma((12,)),
            dma((exchanges, 2)),
            dma((exchanges, 2, STEPS + 1)),
            dma((exchanges, 2)),
            dma((exchanges, 2, 2)),
            dma((ITERS,)),
            dma((ITERS,)),
            dma((ITERS,)),
            dma((ITERS,)),
            dma((3,)),
            dma((3,)),
        ],
        compiler_params=pltpu.CompilerParams(
            collective_id=0, has_side_effects=True, vmem_limit_bytes=40 * 1024 * 1024
        ),
    )(
        *(
            pltpu.with_memory_space_constraint(x, pltpu.HBM)
            for x in (
                base_prod,
                resident,
                floor_space,
                bracket,
                pair_dest.reshape(1, far_pairs),
                pair_src.reshape(1, far_pairs),
                pair_dst.reshape(1, far_pairs),
                pair_count.reshape(1, far_pairs),
                tax_rate,
                commute_decay,
                spill_decay,
                mixing,
            )
        )
    )
    return base_prod.astype(F32) * jnp.exp(power), jnp.sqrt(square)


def solution(mesh):
    return jax.shard_map(
        body,
        mesh=mesh,
        in_specs=(
            P(None, "gy", "gx"),
            P("gy", "gx"),
            P("gy", "gx"),
            P("gy", "gx"),
            P(),
            P(),
            P(),
            P(),
            P(("gy", "gx"), None),
            P(("gy", "gx")),
            P(("gy", "gx")),
            P(("gy", "gx")),
        ),
        out_specs=(P(None, "gy", "gx"), P("gy", "gx")),
        check_vma=False,
    )
```

```python
import functools

import jax
import jax.numpy as jnp
from jax import lax
from jax.experimental import pallas as pl
from jax.experimental.pallas import tpu as pltpu
from jax.sharding import PartitionSpec as P

HALF = 64
ITERS = 3
SECTORS = 8
CAP = 8
BETA_WAGE = 0.3
FAR_SCALE = 0.125
ROWS = 128
COLS = 256
GROUPS = COLS // 16
PAIRS2 = SECTORS // 2
CHUNK = 16
STEPS = HALF // CHUNK
PARTS = ((0, 3), (3, 1))
MESH = pl.DeviceIdType.MESH
F32 = jnp.float32
BF16 = jnp.bfloat16


def swap_blocks(values):
    values = [pltpu.roll(v, 16 * s, 1) if s else v for s, v in enumerate(values)]
    block = lax.broadcasted_iota(jnp.int32, values[0].shape, 1) // 16
    for d in (1, 2, 4):
        moved = (block & d) != 0
        values = [jnp.where(moved, values[(a + d) % 8], values[a]) for a in range(8)]
    values = [values[-g % 8] for g in range(8)]
    return [pltpu.roll(v, 128 - 16 * g, 1) if g else v for g, v in enumerate(values)]


def kernel(
    tiles_y,
    tiles_x,
    base_any,
    resident_any,
    floor_any,
    bracket_any,
    dest_any,
    src_any,
    dst_any,
    count_any,
    tax_any,
    commute_any,
    spill_any,
    mixing_any,
    power_ref,
    rent_ref,
    ext,
    edge_out,
    edge_in,
    mid,
    near,
    labor,
    tap_row,
    band_row,
    band_col,
    band_edge,
    table,
    source_hot,
    slot_hot,
    place,
    far,
    one_out,
    one_in,
    two_out,
    two_in,
    sum_out,
    sum_in,
    total_out,
    total_in,
    rate_ref,
    income_ref,
    last_in,
    base_ref,
    resident_ref,
    floor_ref,
    bracket_ref,
    dest_ref,
    src_ref,
    dst_ref,
    count_ref,
    tax_ref,
    commute_ref,
    spill_ref,
    mixing_ref,
    load_sem,
    row_send,
    row_recv,
    edge_send,
    edge_recv,
    one_send,
    one_recv,
    two_send,
    two_recv,
    sum_send,
    sum_recv,
):
    my = lax.axis_index("gy")
    mx = lax.axis_index("gx")
    chips_x = tiles_x // 2
    chips = tiles_y * chips_x
    core = lax.rem(mx, 2)
    chip_x = mx // 2
    sibling = mx + 1 - 2 * core
    beyond = lax.rem(mx + 2 * core - 1 + tiles_x, tiles_x)
    mine = my * chips_x + chip_x
    slots = tiles_y * tiles_x * CAP
    far_pairs = dest_ref.shape[1]

    loads = [
        pltpu.make_async_copy(source, target, load_sem.at[k])
        for k, (source, target) in enumerate(
            (
                (base_any, base_ref),
                (resident_any, resident_ref),
                (bracket_any, bracket_ref),
                (floor_any, floor_ref),
                (dest_any, dest_ref),
                (src_any, src_ref),
                (dst_any, dst_ref),
                (count_any, count_ref),
                (tax_any, tax_ref),
                (commute_any, commute_ref),
                (spill_any, spill_ref),
                (mixing_any, mixing_ref),
            )
        )
    ]
    for load in loads:
        load.start()

    barrier = pltpu.get_barrier_semaphore()

    def chip_at(j):
        return lax.rem(my + j // chips_x, tiles_y), lax.rem(chip_x + lax.rem(j, chips_x), chips_x)

    def greet(y, x):
        pl.semaphore_signal(barrier, inc=1, device_id=(y, x), device_id_type=MESH)

    def greet_chip(j, carry):
        y, x = chip_at(j)
        greet(y, 2 * x + core)
        return carry

    greet(my, sibling)
    greet(my, beyond)
    lax.fori_loop(1, chips, greet_chip, 0)

    def row_copy(e, way, sectors, j, height, slot):
        start = HALF if way == 0 else ROWS
        land = HALF + ROWS if way == 0 else 0
        target = my - 1 if way == 0 else my + 1
        step = pl.multiple_of(j * height, height)
        return pltpu.make_async_remote_copy(
            src_ref=ext.at[e, sectors, pl.ds(start + step, height), :],
            dst_ref=ext.at[e, sectors, pl.ds(land + step, height), :],
            send_sem=row_send.at[e, way],
            recv_sem=row_recv.at[e, way, slot],
            device_id=(target, mx),
            device_id_type=MESH,
        )

    def row_step(e, way, j):
        return row_copy(e, way, pl.ds(0, 2 * PARTS[0][1]), j, CHUNK, 0)

    def row_rest(e, way):
        return row_copy(e, way, pl.ds(2 * PARTS[1][0], 2 * PARTS[1][1]), 0, HALF, 1)

    def row_drain(e, way):
        start = HALF if way == 0 else ROWS
        target = my - 1 if way == 0 else my + 1
        return pltpu.make_async_remote_copy(
            src_ref=ext.at[e, :, pl.ds(start, HALF), :],
            dst_ref=ext.at[e, :, pl.ds(start, HALF), :],
            send_sem=row_send.at[e, way],
            recv_sem=row_recv.at[e, way, 0],
            device_id=(target, mx),
            device_id_type=MESH,
        )

    can_row = (my > 0, my < tiles_y - 1)
    can_edge = (mx > 0, mx < tiles_x - 1)

    def send_rows(e, j):
        for way in range(2):

            @pl.when(can_row[way])
            def _():
                row_step(e, way, j).start()

    def send_rest(e):
        for way in range(2):

            @pl.when(can_row[way])
            def _():
                row_rest(e, way).start()

    def wait_rows(e, part):
        for way in range(2):

            @pl.when(can_row[1 - way])
            def _():
                if part == 0:
                    row_copy(e, way, pl.ds(0, 2 * PARTS[0][1]), 0, HALF, 0).wait_recv()
                else:
                    row_rest(e, way).wait_recv()

    def edge_copy(e, part, way):
        target = mx - 1 if way == 0 else mx + 1
        pairs = pl.ds(*PARTS[part])
        return pltpu.make_async_remote_copy(
            src_ref=edge_out.at[e, way, pairs],
            dst_ref=edge_in.at[e, 1 - way, pairs],
            send_sem=edge_send.at[e, way],
            recv_sem=edge_recv.at[e, way, part],
            device_id=(my, target),
            device_id_type=MESH,
        )

    def edge_drain(e, way):
        target = mx - 1 if way == 0 else mx + 1
        return pltpu.make_async_remote_copy(
            src_ref=edge_out.at[e, way],
            dst_ref=edge_in.at[e, 1 - way],
            send_sem=edge_send.at[e, way],
            recv_sem=edge_recv.at[e, way, 0],
            device_id=(my, target),
            device_id_type=MESH,
        )

    lane128 = lax.broadcasted_iota(jnp.int32, (ROWS, 128), 1)

    def rows_pass(e, kind):
        for part, (first_pair, count) in enumerate(PARTS):
            wait_rows(e, part)
            for i in range(first_pair, first_pair + count):
                ends = []
                for s in (2 * i, 2 * i + 1):
                    passed = jnp.dot(
                        band_row[kind * SECTORS + s], ext[e, s], preferred_element_type=F32
                    )
                    mid[s] = passed.astype(BF16)
                    ends.append((passed[:, 0:128], passed[:, 128:256]))
                first, second = ends
                low = lane128 < HALF
                edge_out[e, 0, i] = jnp.where(
                    low, first[0], pltpu.roll(second[0], HALF, 1)
                ).astype(BF16)
                edge_out[e, 1, i] = jnp.where(
                    low, pltpu.roll(second[1], HALF, 1), first[1]
                ).astype(BF16)
            for way in range(2):

                @pl.when(can_edge[way])
                def _():
                    edge_copy(e, part, way).start()

    def columns_start(kind, result):
        def one(half, carry):
            for k in range(4):
                s = 4 * half + k
                result[s] = jnp.dot(
                    mid[s], band_col[kind * SECTORS + s], preferred_element_type=F32
                )
            return carry

        lax.fori_loop(0, 2, one, 0)

    def columns_finish(e, kind, result):
        for part, (first_pair, count) in enumerate(PARTS):
            for way in range(2):

                @pl.when(can_edge[1 - way])
                def _():
                    edge_copy(e, part, way).wait_recv()

            for s in range(2 * first_pair, 2 * (first_pair + count)):
                for side in range(2):
                    lanes = slice(128 * side, 128 * side + 128)
                    result[s, :, lanes] += jnp.dot(
                        edge_in[e, side, s // 2],
                        band_edge[kind * SECTORS + s, side],
                        preferred_element_type=F32,
                    )

    def make_bands(kind):
        u = lax.broadcasted_iota(jnp.int32, (COLS, COLS), 0)
        x = lax.broadcasted_iota(jnp.int32, (COLS, COLS), 1)
        inside = jnp.abs(u - x) <= 128

        def one(s, carry):
            b = kind * SECTORS + s
            line = jnp.broadcast_to(tap_row[pl.ds(b, 1), :], (ROWS, COLS))
            rows_band = pltpu.roll(line, 0, 1, stride=1, stride_axis=0)
            band_row[b] = rows_band.astype(BF16)
            circle = jnp.concatenate(
                [pltpu.roll(rows_band, COLS - HALF, 1), pltpu.roll(rows_band, HALF, 1)], axis=0
            )
            band_col[b] = jnp.where(inside, circle, 0.0).astype(BF16)
            rest = jnp.where(inside, 0.0, circle)
            swap = lax.rem(s, 2) == 1
            for side in range(2):
                block = rest[128 - 128 * side : 256 - 128 * side, 128 * side : 128 * side + 128]
                turned = jnp.concatenate([block[HALF:], block[:HALF]], axis=0)
                band_edge[b, side] = jnp.where(swap, turned, block).astype(BF16)
            return carry

        lax.fori_loop(0, SECTORS, one, 0)

    def parts_of(a):
        return 2 if a == 0 else 1

    def first_copy(a, y, x):
        return pltpu.make_async_remote_copy(
            src_ref=one_out.at[a, y * chips_x + x, pl.ds(0, parts_of(a))],
            dst_ref=one_in.at[a, mine, pl.ds(0, parts_of(a))],
            send_sem=one_send.at[a],
            recv_sem=one_recv.at[a],
            device_id=(y, 2 * x + core),
            device_id_type=MESH,
        )

    def first_all(a):
        return pltpu.make_async_remote_copy(
            src_ref=one_out.at[a, pl.ds(0, chips - 1), pl.ds(0, parts_of(a))],
            dst_ref=one_in.at[a, pl.ds(0, chips - 1), pl.ds(0, parts_of(a))],
            send_sem=one_send.at[a],
            recv_sem=one_recv.at[a],
            device_id=(my, sibling),
            device_id_type=MESH,
        )

    def second_copy(a):
        return pltpu.make_async_remote_copy(
            src_ref=two_out.at[a, pl.ds(0, parts_of(a))],
            dst_ref=two_in.at[a, pl.ds(0, parts_of(a)), 1],
            send_sem=two_send.at[a],
            recv_sem=two_recv.at[a],
            device_id=(my, sibling),
            device_id_type=MESH,
        )

    def start_first(a):
        for k in range(1, chips_x):
            first_copy(a, my, lax.rem(chip_x + k, chips_x)).start()

        def one(j, carry):
            for k in range(chips_x):
                first_copy(a, lax.rem(my + j, tiles_y), lax.rem(chip_x + k, chips_x)).start()
            return carry

        lax.fori_loop(1, tiles_y, one, 0)
        for part in range(parts_of(a)):
            one_in[a, mine, part] = one_out[a, mine, part]

    def pass_on(a):
        first_all(a).wait_recv()
        kept = []
        for part in range(parts_of(a)):
            parts = one_in[a, :, part].astype(F32).reshape(chips, 2, CAP, 128)
            low, high = parts[:, 0], parts[:, 1]
            other = jnp.where(core == 0, high, low).reshape(chips * CAP, 128)
            two_out[a, part] = other.astype(BF16)
            own = jnp.where(core == 0, low, high).reshape(chips * CAP, 128)
            kept.append(own.astype(BF16))
        second_copy(a).start()
        for part in range(parts_of(a)):
            two_in[a, part, 0] = kept[part]

    def sum_copy(x):
        return pltpu.make_async_remote_copy(
            src_ref=sum_out,
            dst_ref=sum_in.at[chip_x],
            send_sem=sum_send.at[0],
            recv_sem=sum_recv.at[0],
            device_id=(my, 2 * x + core),
            device_id_type=MESH,
        )

    def total_copy(y):
        return pltpu.make_async_remote_copy(
            src_ref=total_out,
            dst_ref=total_in.at[my],
            send_sem=sum_send.at[1],
            recv_sem=sum_recv.at[1],
            device_id=(y, mx),
            device_id_type=MESH,
        )

    def sum_all():
        return pltpu.make_async_remote_copy(
            src_ref=sum_in.at[pl.ds(0, chips_x - 1)],
            dst_ref=sum_in.at[pl.ds(0, chips_x - 1)],
            send_sem=sum_send.at[0],
            recv_sem=sum_recv.at[0],
            device_id=(my, sibling),
            device_id_type=MESH,
        )

    def total_all():
        return pltpu.make_async_remote_copy(
            src_ref=total_in.at[pl.ds(0, tiles_y - 1)],
            dst_ref=total_in.at[pl.ds(0, tiles_y - 1)],
            send_sem=sum_send.at[1],
            recv_sem=sum_recv.at[1],
            device_id=(my, sibling),
            device_id_type=MESH,
        )

    def last_copy():
        return pltpu.make_async_remote_copy(
            src_ref=last_in.at[0],
            dst_ref=last_in.at[1],
            send_sem=sum_send.at[2],
            recv_sem=sum_recv.at[2],
            device_id=(my, sibling),
            device_id_type=MESH,
        )

    def unit(r, h):
        return pl.ds(r, CHUNK), pl.ds(pl.multiple_of(128 * h, 128), 128)

    def strip_rows(r, h, g):
        return pl.ds(pl.multiple_of((8 * h + g) * ROWS + r, CHUNK), CHUNK)

    def over_cells(work, sent, carry, wide):
        def step(j, carry):
            def one(u, carry):
                for k in range(wide):
                    number = u * wide + k
                    r = pl.multiple_of((number // 2) * HALF + j * CHUNK, CHUNK)
                    carry = work(r, number % 2, carry)
                return carry

            carry = one(0, carry) if wide == 4 else lax.fori_loop(0, 4 // wide, one, carry)
            if sent is not None:
                send_rows(sent, j)
            return carry

        carry = lax.fori_loop(0, STEPS, step, carry)
        if sent is not None:
            send_rest(sent)
        return carry

    def shares(it, r, h, wages, revenue):
        rows, lanes = unit(r, h)
        powers = [w * w * w for w in wages]
        inverse = 1.0 / sum(powers[1:], powers[0])
        people = resident_ref[rows, lanes]
        earned = sum([p * w for p, w in zip(powers[1:], wages[1:])], powers[0] * wages[0])
        income = earned * inverse
        income_ref[it, rows, lanes] = income
        scale = people * inverse
        supply = [p * scale for p in powers]
        for s in range(SECTORS):
            ext[2 * it, s, pl.ds(HALF + r, CHUNK), lanes] = supply[s].astype(BF16)
        for g, strip in enumerate(swap_blocks(supply)):
            table[strip_rows(r, h, g), :] = strip.astype(BF16)
        gain = people * rate_ref[rows, lanes] * income
        return revenue + gain[0:8] + gain[8:16]

    def gather(a):
        picked = jnp.dot(source_hot[...], table[...], preferred_element_type=F32).astype(BF16)
        ordered = jnp.dot(slot_hot[...], picked, preferred_element_type=F32).astype(BF16)
        one_out[a, :, 0] = ordered.reshape(chips, 2 * CAP, 128)

    zero = jnp.zeros((8, 128), F32)

    def first_cells(r, h, carry):
        people_sum, revenue = carry
        rows, lanes = unit(r, h)
        bracket = bracket_ref[rows, lanes]
        rate = jnp.zeros((CHUNK, 128), F32)
        for b in range(8):
            rate = jnp.where(bracket == b, tax_ref[b], rate)
        rate_ref[rows, lanes] = rate
        people = resident_ref[rows, lanes]
        people_sum = people_sum + people[0:8] + people[8:16]
        wages = [base_ref[s, rows, lanes].astype(F32) for s in range(SECTORS)]
        return people_sum, shares(0, r, h, wages, revenue)

    for load in loads:
        load.wait()
    people_sum, revenue0 = over_cells(first_cells, None, (zero, zero), 4)
    pl.semaphore_wait(barrier, chips + 1)
    for j in range(STEPS):
        send_rows(0, j)
    send_rest(0)

    line = lax.broadcasted_iota(jnp.int32, (8, far_pairs), 0)
    source, target = src_ref[...], dst_ref[...]
    row, group = target >> 4, target & 15
    fields = [
        dest_ref[...],
        (source & 15) * ROWS + (source >> 4),
        ((((row >> 4) & 3) * 2 + (row >> 6)) * GROUPS) + group,
        row & 15,
        count_ref[...],
    ]
    pairs = jnp.zeros((8, far_pairs), jnp.int32)
    for k, field in enumerate(fields):
        pairs = jnp.where(line == k, field, pairs)
    pairs = pairs.astype(F32)
    across = jnp.concatenate([pairs, jnp.zeros((120, far_pairs), F32)], axis=0).T
    dest_row = pairs[0:1, :]
    earlier = lax.broadcasted_iota(jnp.int32, (far_pairs, far_pairs), 0) < (
        lax.broadcasted_iota(jnp.int32, (far_pairs, far_pairs), 1)
    )
    same = (across[:, 0:1] == dest_row) & earlier
    rank = jnp.sum(jnp.where(same, 1.0, 0.0), axis=0, keepdims=True)
    slot_of = (dest_row * CAP + rank).astype(jnp.int32)
    slot_ids = lax.broadcasted_iota(jnp.int32, (slots, far_pairs), 0)
    slot_hot[...] = jnp.where(slot_ids == slot_of, 1.0, 0.0).astype(BF16)
    strip_ids = lax.broadcasted_iota(jnp.int32, (far_pairs, GROUPS * ROWS), 1)
    source_hot[...] = jnp.where(
        strip_ids == across[:, 1:2].astype(jnp.int32), 1.0, 0.0
    ).astype(BF16)
    one_out[0, :, 1] = (
        jnp.dot(slot_hot[...], across.astype(BF16), preferred_element_type=F32)
        .astype(BF16)
        .reshape(chips, 2 * CAP, 128)
    )
    gather(0)
    start_first(0)

    @pl.when(my == 0)
    def _():
        ext[:, :, 0:HALF, :] = jnp.zeros((2 * ITERS, SECTORS, HALF, COLS), BF16)

    @pl.when(my == tiles_y - 1)
    def _():
        ext[:, :, HALF + ROWS :, :] = jnp.zeros((2 * ITERS, SECTORS, HALF, COLS), BF16)

    @pl.when(mx == 0)
    def _():
        edge_in[:, 0] = jnp.zeros((2 * ITERS, PAIRS2, ROWS, 128), BF16)

    @pl.when(mx == tiles_x - 1)
    def _():
        edge_in[:, 1] = jnp.zeros((2 * ITERS, PAIRS2, ROWS, 128), BF16)

    sector = lax.broadcasted_iota(jnp.int32, (2 * SECTORS, COLS), 0)
    tap = lax.broadcasted_iota(jnp.int32, (2 * SECTORS, COLS), 1)
    decay = jnp.zeros((2 * SECTORS, COLS), F32)
    for s in range(SECTORS):
        decay = jnp.where(sector == s, commute_ref[s], decay)
        decay = jnp.where(sector == SECTORS + s, spill_ref[s], decay)
    offset = jnp.abs(tap - HALF).astype(F32) / HALF
    unscaled = jnp.where(tap <= 2 * HALF, jnp.exp(-decay * offset), 0.0)
    tap_row[...] = (unscaled / jnp.sum(unscaled, axis=1, keepdims=True)).astype(BF16).astype(F32)
    make_bands(0)


    def build_place():
        routing = two_in[0, 1].reshape(slots, 128)
        line = lax.broadcasted_iota(jnp.int32, (16, 128), 0)
        lane = lax.broadcasted_iota(jnp.int32, (16, 128), 1)
        pick = jnp.where((line == 0) & (lane == 2), float(CHUNK), 0.0)
        pick = jnp.where((line == 0) & (lane == 3), 1.0, pick)
        pick = jnp.where((line == 1) & (lane == 4), 1.0, pick).astype(BF16)
        found = lax.dot_general(
            pick, routing, (((1,), (1,)), ((), ())), preferred_element_type=F32
        )
        where_to, weight = found[0:1, :].astype(jnp.int32), found[1:2, :]

        def one(g, carry):
            strip = g * ROWS + lax.broadcasted_iota(jnp.int32, (ROWS, slots), 0)
            place[pl.ds(pl.multiple_of(g * ROWS, ROWS), ROWS), :] = jnp.where(
                strip == where_to, weight, 0.0
            ).astype(BF16)
            return carry

        lax.fori_loop(0, GROUPS, one, 0)

    revenues = [revenue0]
    for it in range(ITERS):
        if it > 0:
            gather(it)
            start_first(it)
        if it == ITERS - 1:
            line = lax.broadcasted_iota(jnp.int32, (8, 128), 0)
            parts = zero
            for k, part in enumerate([people_sum] + revenues):
                parts = jnp.where(line == k, jnp.sum(part, axis=0, keepdims=True), parts)
            sum_out[...] = parts

            def start_sum(j, carry):
                sum_copy(lax.rem(chip_x + j, chips_x)).start()
                return carry

            lax.fori_loop(1, chips_x, start_sum, 0)
            sum_in[chip_x] = parts
        rows_pass(2 * it, 0)
        columns_start(0, near)
        pass_on(it)
        if it == ITERS - 1:
            sum_all().wait_recv()
            halfway = jnp.sum(sum_in[...], axis=0)
            total_out[...] = halfway

            def start_total(j, carry):
                total_copy(lax.rem(my + j, tiles_y)).start()
                return carry

            lax.fori_loop(1, tiles_y, start_total, 0)
            total_in[my] = halfway
        columns_finish(2 * it, 0, near)
        if it == ITERS - 1:
            total_all().wait_recv()
            last_in[0] = jnp.sum(total_in[...], axis=0)
            last_copy().start()
        second_copy(it).wait_recv()
        if it == 0:
            build_place()

        def labor_step(j, carry):
            block = 2 * GROUPS * CHUNK
            far[...] = jnp.dot(
                place[pl.ds(pl.multiple_of(j * block, block), block), :],
                two_in[it, 0].reshape(slots, 128),
                preferred_element_type=F32,
            )
            for number in range(4):
                way, h = number // 2, number % 2
                r = pl.multiple_of(way * HALF + j * CHUNK, CHUNK)
                rows, lanes = unit(r, h)
                first = (way * GROUPS + 8 * h) * CHUNK
                strips = [far[first + CHUNK * g : first + CHUNK * (g + 1), :] for g in range(8)]
                for s, flow in enumerate(swap_blocks(strips)):
                    value = near[s, rows, lanes] + FAR_SCALE * flow
                    labor[s, rows, lanes] = value
                    ext[2 * it + 1, s, pl.ds(HALF + r, CHUNK), lanes] = value.astype(BF16)
            send_rows(2 * it + 1, j)
            return carry

        lax.fori_loop(0, STEPS, labor_step, 0)
        send_rest(2 * it + 1)
        if it == 0:
            make_bands(1)
        if it == ITERS - 1:
            last_copy().wait_recv()
            sums = jnp.sum(last_in[0] + last_in[1], axis=1, keepdims=True)
            people_all = sums[0:1, 0:1]
            transfers = [sums[1 + k : 2 + k, 0:1] / people_all for k in range(ITERS)]

            def rent_chunk(c, carry):
                rows = pl.ds(pl.multiple_of(c * CHUNK, CHUNK), CHUNK)
                keep = 1.0 - rate_ref[rows, :]
                people, space = resident_ref[rows, :], floor_ref[rows, :]
                ratio = people / space
                square = None
                for k in range(ITERS):
                    net = keep * income_ref[k, rows, :] + transfers[k]
                    level = ratio if square is None else jnp.sqrt(square) * ratio
                    square = level * net
                rent_ref[rows, :] = square
                return carry

            lax.fori_loop(0, ROWS // CHUNK, rent_chunk, 0)
        rows_pass(2 * it + 1, 1)
        columns_start(1, near)
        columns_finish(2 * it + 1, 1, near)

        def wage_cells(r, h, revenue):
            rows, lanes = unit(r, h)
            logs = [jnp.log(1.0 + near[s, rows, lanes]) for s in range(SECTORS)]
            wages = []
            for s in range(SECTORS):
                power = -BETA_WAGE * jnp.log(1.0 + labor[s, rows, lanes])
                for t in range(SECTORS):
                    power = power + mixing_ref[s, t] * logs[t]
                if it == ITERS - 1:
                    power_ref[s, rows, lanes] = power
                else:
                    wages.append(base_ref[s, rows, lanes].astype(F32) * jnp.exp(power))
            if it < ITERS - 1:
                revenue = shares(it + 1, r, h, wages, revenue)
            return revenue

        sent = 2 * it + 2 if it < ITERS - 1 else None
        revenues.append(over_cells(wage_cells, sent, zero, 4))

    for e in range(2 * ITERS):
        for way in range(2):

            @pl.when(can_row[way])
            def _():
                row_drain(e, way).wait_send()

            @pl.when(can_edge[way])
            def _():
                edge_drain(e, way).wait_send()

    for a in range(ITERS):
        first_all(a).wait_send()
        second_copy(a).wait_send()
    sum_all().wait_send()
    total_all().wait_send()
    last_copy().wait_send()


def body(
    base_prod,
    resident,
    floor_space,
    bracket,
    tax_rate,
    mixing,
    spill_decay,
    commute_decay,
    pair_dest,
    pair_src,
    pair_dst,
    pair_count,
):
    tiles_y = lax.axis_size("gy")
    tiles_x = lax.axis_size("gx")
    slots = tiles_y * tiles_x * CAP
    chips = tiles_y * tiles_x // 2
    far_pairs = pair_src.shape[0]
    vmem = pl.BlockSpec(memory_space=pltpu.VMEM)
    whole = pl.BlockSpec(memory_space=pltpu.HBM)
    smem = pltpu.SMEM
    exchanges = 2 * ITERS
    dma = pltpu.SemaphoreType.DMA
    power, square = pl.pallas_call(
        functools.partial(kernel, tiles_y, tiles_x),
        out_shape=(
            jax.ShapeDtypeStruct(base_prod.shape, F32),
            jax.ShapeDtypeStruct(resident.shape, F32),
        ),
        in_specs=[whole] * 12,
        out_specs=(vmem, vmem),
        scratch_shapes=[
            pltpu.VMEM((exchanges, SECTORS, ROWS + 2 * HALF, COLS), BF16),
            pltpu.VMEM((exchanges, 2, PAIRS2, ROWS, 128), BF16),
            pltpu.VMEM((exchanges, 2, PAIRS2, ROWS, 128), BF16),
            pltpu.VMEM((SECTORS, ROWS, COLS), BF16),
            pltpu.VMEM((SECTORS, ROWS, COLS), F32),
            pltpu.VMEM((SECTORS, ROWS, COLS), F32),
            pltpu.VMEM((2 * SECTORS, COLS), F32),
            pltpu.VMEM((2 * SECTORS, ROWS, COLS), BF16),
            pltpu.VMEM((2 * SECTORS, COLS, COLS), BF16),
            pltpu.VMEM((2 * SECTORS, 2, 128, 128), BF16),
            pltpu.VMEM((GROUPS * ROWS, 128), BF16),
            pltpu.VMEM((far_pairs, GROUPS * ROWS), BF16),
            pltpu.VMEM((slots, far_pairs), BF16),
            pltpu.VMEM((GROUPS * ROWS, slots), BF16),
            pltpu.VMEM((2 * GROUPS * CHUNK, 128), F32),
            pltpu.VMEM((ITERS, chips, 2, 2 * CAP, 128), BF16),
            pltpu.VMEM((ITERS, chips, 2, 2 * CAP, 128), BF16),
            pltpu.VMEM((ITERS, 2, chips * CAP, 128), BF16),
            pltpu.VMEM((ITERS, 2, 2, chips * CAP, 128), BF16),
            pltpu.VMEM((8, 128), F32),
            pltpu.VMEM((tiles_x // 2, 8, 128), F32),
            pltpu.VMEM((8, 128), F32),
            pltpu.VMEM((tiles_y, 8, 128), F32),
            pltpu.VMEM((ROWS, COLS), F32),
            pltpu.VMEM((ITERS, ROWS, COLS), F32),
            pltpu.VMEM((2, 8, 128), F32),
            pltpu.VMEM((SECTORS, ROWS, COLS), BF16),
            pltpu.VMEM((ROWS, COLS), F32),
            pltpu.VMEM((ROWS, COLS), F32),
            pltpu.VMEM((ROWS, COLS), jnp.int32),
            pltpu.VMEM((1, far_pairs), jnp.int32),
            pltpu.VMEM((1, far_pairs), jnp.int32),
            pltpu.VMEM((1, far_pairs), jnp.int32),
            pltpu.VMEM((1, far_pairs), jnp.int32),
            smem((8,), F32),
            smem((SECTORS,), F32),
            smem((SECTORS,), F32),
            smem((SECTORS, SECTORS), F32),
            dma((12,)),
            dma((exchanges, 2)),
            dma((exchanges, 2, 2)),
            dma((exchanges, 2)),
            dma((exchanges, 2, 2)),
            dma((ITERS,)),
            dma((ITERS,)),
            dma((ITERS,)),
            dma((ITERS,)),
            dma((3,)),
            dma((3,)),
        ],
        compiler_params=pltpu.CompilerParams(
            collective_id=0, has_side_effects=True, vmem_limit_bytes=40 * 1024 * 1024
        ),
    )(
        *(
            pltpu.with_memory_space_constraint(x, pltpu.HBM)
            for x in (
                base_prod,
                resident,
                floor_space,
                bracket,
                pair_dest.reshape(1, far_pairs),
                pair_src.reshape(1, far_pairs),
                pair_dst.reshape(1, far_pairs),
                pair_count.reshape(1, far_pairs),
                tax_rate,
                commute_decay,
                spill_decay,
                mixing,
            )
        )
    )
    return base_prod.astype(F32) * jnp.exp(power), jnp.sqrt(square)


def solution(mesh):
    return jax.shard_map(
        body,
        mesh=mesh,
        in_specs=(
            P(None, "gy", "gx"),
            P("gy", "gx"),
            P("gy", "gx"),
            P("gy", "gx"),
            P(),
            P(),
            P(),
            P(),
            P(("gy", "gx"), None),
            P(("gy", "gx")),
            P(("gy", "gx")),
            P(("gy", "gx")),
        ),
        out_specs=(P(None, "gy", "gx"), P("gy", "gx")),
        check_vma=False,
    )
```

```python
import functools

import jax
import jax.numpy as jnp
from jax import lax
from jax.experimental import pallas as pl
from jax.experimental.pallas import tpu as pltpu
from jax.sharding import PartitionSpec as P

HALF = 64
ITERS = 3
SECTORS = 8
CAP = 8
BETA_WAGE = 0.3
FAR_SCALE = 0.125
ROWS = 128
COLS = 256
GROUPS = COLS // 16
PAIRS2 = SECTORS // 2
CHUNK = 16
STEPS = HALF // CHUNK
PARTS = ((0, 3), (3, 1))
MESH = pl.DeviceIdType.MESH
F32 = jnp.float32
BF16 = jnp.bfloat16


def swap_blocks(values):
    values = [pltpu.roll(v, 16 * s, 1) if s else v for s, v in enumerate(values)]
    block = lax.broadcasted_iota(jnp.int32, values[0].shape, 1) // 16
    for d in (1, 2, 4):
        moved = (block & d) != 0
        values = [jnp.where(moved, values[(a + d) % 8], values[a]) for a in range(8)]
    values = [values[-g % 8] for g in range(8)]
    return [pltpu.roll(v, 128 - 16 * g, 1) if g else v for g, v in enumerate(values)]


def kernel(
    tiles_y,
    tiles_x,
    base_any,
    resident_any,
    floor_any,
    bracket_any,
    dest_any,
    src_any,
    dst_any,
    count_any,
    tax_any,
    commute_any,
    spill_any,
    mixing_any,
    power_ref,
    rent_ref,
    ext,
    edge_out,
    edge_in,
    mid,
    near,
    labor,
    tap_row,
    band_row,
    band_col,
    band_edge,
    table,
    source_hot,
    slot_hot,
    place,
    far,
    one_out,
    one_in,
    two_out,
    two_in,
    sum_out,
    sum_in,
    total_out,
    total_in,
    rate_ref,
    income_ref,
    last_in,
    base_ref,
    resident_ref,
    floor_ref,
    bracket_ref,
    dest_ref,
    src_ref,
    dst_ref,
    count_ref,
    tax_ref,
    commute_ref,
    spill_ref,
    mixing_ref,
    load_sem,
    row_send,
    row_recv,
    edge_send,
    edge_recv,
    one_send,
    one_recv,
    two_send,
    two_recv,
    sum_send,
    sum_recv,
):
    my = lax.axis_index("gy")
    mx = lax.axis_index("gx")
    chips_x = tiles_x // 2
    chips = tiles_y * chips_x
    core = lax.rem(mx, 2)
    chip_x = mx // 2
    sibling = mx + 1 - 2 * core
    beyond = lax.rem(mx + 2 * core - 1 + tiles_x, tiles_x)
    mine = my * chips_x + chip_x
    slots = tiles_y * tiles_x * CAP
    far_pairs = dest_ref.shape[1]

    loads = [
        pltpu.make_async_copy(source, target, load_sem.at[k])
        for k, (source, target) in enumerate(
            (
                (base_any, base_ref),
                (resident_any, resident_ref),
                (bracket_any, bracket_ref),
                (floor_any, floor_ref),
                (dest_any, dest_ref),
                (src_any, src_ref),
                (dst_any, dst_ref),
                (count_any, count_ref),
                (tax_any, tax_ref),
                (commute_any, commute_ref),
                (spill_any, spill_ref),
                (mixing_any, mixing_ref),
            )
        )
    ]
    for load in loads:
        load.start()

    barrier = pltpu.get_barrier_semaphore()

    def greet(y, x):
        pl.semaphore_signal(barrier, inc=1, device_id=(y, x), device_id_type=MESH)

    def greet_row(j, carry):
        for k in range(chips_x):
            greet(lax.rem(my + j, tiles_y), 2 * lax.rem(chip_x + k, chips_x) + core)
        return carry

    greet(my, sibling)
    greet(my, beyond)
    for k in range(1, chips_x):
        greet(my, 2 * lax.rem(chip_x + k, chips_x) + core)
    lax.fori_loop(1, tiles_y, greet_row, 0)

    def row_copy(e, way, sectors, j, height, slot):
        start = HALF if way == 0 else ROWS
        land = HALF + ROWS if way == 0 else 0
        target = my - 1 if way == 0 else my + 1
        step = pl.multiple_of(j * height, height)
        return pltpu.make_async_remote_copy(
            src_ref=ext.at[e, sectors, pl.ds(start + step, height), :],
            dst_ref=ext.at[e, sectors, pl.ds(land + step, height), :],
            send_sem=row_send.at[e, way],
            recv_sem=row_recv.at[e, way, slot],
            device_id=(target, mx),
            device_id_type=MESH,
        )

    def row_step(e, way, j):
        return row_copy(e, way, pl.ds(0, 2 * PARTS[0][1]), j, CHUNK, 0)

    def row_rest(e, way):
        return row_copy(e, way, pl.ds(2 * PARTS[1][0], 2 * PARTS[1][1]), 0, HALF, 1)

    def row_drain(e, way):
        start = HALF if way == 0 else ROWS
        target = my - 1 if way == 0 else my + 1
        return pltpu.make_async_remote_copy(
            src_ref=ext.at[e, :, pl.ds(start, HALF), :],
            dst_ref=ext.at[e, :, pl.ds(start, HALF), :],
            send_sem=row_send.at[e, way],
            recv_sem=row_recv.at[e, way, 0],
            device_id=(target, mx),
            device_id_type=MESH,
        )

    can_row = (my > 0, my < tiles_y - 1)
    can_edge = (mx > 0, mx < tiles_x - 1)

    def send_rows(e, j):
        for way in range(2):

            @pl.when(can_row[way])
            def _():
                row_step(e, way, j).start()

    def send_rest(e):
        for way in range(2):

            @pl.when(can_row[way])
            def _():
                row_rest(e, way).start()

    def wait_rows(e, part):
        for way in range(2):

            @pl.when(can_row[1 - way])
            def _():
                if part == 0:
                    row_copy(e, way, pl.ds(0, 2 * PARTS[0][1]), 0, HALF, 0).wait_recv()
                else:
                    row_rest(e, way).wait_recv()

    def edge_copy(e, part, way):
        target = mx - 1 if way == 0 else mx + 1
        pairs = pl.ds(*PARTS[part])
        return pltpu.make_async_remote_copy(
            src_ref=edge_out.at[e, way, pairs],
            dst_ref=edge_in.at[e, 1 - way, pairs],
            send_sem=edge_send.at[e, way],
            recv_sem=edge_recv.at[e, way, part],
            device_id=(my, target),
            device_id_type=MESH,
        )

    def edge_drain(e, way):
        target = mx - 1 if way == 0 else mx + 1
        return pltpu.make_async_remote_copy(
            src_ref=edge_out.at[e, way],
            dst_ref=edge_in.at[e, 1 - way],
            send_sem=edge_send.at[e, way],
            recv_sem=edge_recv.at[e, way, 0],
            device_id=(my, target),
            device_id_type=MESH,
        )

    lane128 = lax.broadcasted_iota(jnp.int32, (ROWS, 128), 1)

    def rows_pass(e, kind):
        for part, (first_pair, count) in enumerate(PARTS):
            wait_rows(e, part)
            for i in range(first_pair, first_pair + count):
                ends = []
                for s in (2 * i, 2 * i + 1):
                    passed = jnp.dot(
                        band_row[kind * SECTORS + s], ext[e, s], preferred_element_type=F32
                    )
                    mid[s] = passed.astype(BF16)
                    ends.append((passed[:, 0:128], passed[:, 128:256]))
                first, second = ends
                low = lane128 < HALF
                edge_out[e, 0, i] = jnp.where(
                    low, first[0], pltpu.roll(second[0], HALF, 1)
                ).astype(BF16)
                edge_out[e, 1, i] = jnp.where(
                    low, pltpu.roll(second[1], HALF, 1), first[1]
                ).astype(BF16)
            for way in range(2):

                @pl.when(can_edge[way])
                def _():
                    edge_copy(e, part, way).start()

    def columns_start(kind, result):
        def one(half, carry):
            for k in range(4):
                s = 4 * half + k
                result[s] = jnp.dot(
                    mid[s], band_col[kind * SECTORS + s], preferred_element_type=F32
                )
            return carry

        lax.fori_loop(0, 2, one, 0)

    def columns_finish(e, kind, result):
        for part, (first_pair, count) in enumerate(PARTS):
            for way in range(2):

                @pl.when(can_edge[1 - way])
                def _():
                    edge_copy(e, part, way).wait_recv()

            for s in range(2 * first_pair, 2 * (first_pair + count)):
                for side in range(2):
                    lanes = slice(128 * side, 128 * side + 128)
                    result[s, :, lanes] += jnp.dot(
                        edge_in[e, side, s // 2],
                        band_edge[kind * SECTORS + s, side],
                        preferred_element_type=F32,
                    )

    def make_bands(kind):
        u = lax.broadcasted_iota(jnp.int32, (COLS, COLS), 0)
        x = lax.broadcasted_iota(jnp.int32, (COLS, COLS), 1)
        inside = jnp.abs(u - x) <= 128

        def one(s, carry):
            b = kind * SECTORS + s
            line = jnp.broadcast_to(tap_row[pl.ds(b, 1), :], (ROWS, COLS))
            rows_band = pltpu.roll(line, 0, 1, stride=1, stride_axis=0)
            band_row[b] = rows_band.astype(BF16)
            circle = jnp.concatenate(
                [pltpu.roll(rows_band, COLS - HALF, 1), pltpu.roll(rows_band, HALF, 1)], axis=0
            )
            band_col[b] = jnp.where(inside, circle, 0.0).astype(BF16)
            rest = jnp.where(inside, 0.0, circle)
            swap = lax.rem(s, 2) == 1
            for side in range(2):
                block = rest[128 - 128 * side : 256 - 128 * side, 128 * side : 128 * side + 128]
                turned = jnp.concatenate([block[HALF:], block[:HALF]], axis=0)
                band_edge[b, side] = jnp.where(swap, turned, block).astype(BF16)
            return carry

        lax.fori_loop(0, SECTORS, one, 0)

    def parts_of(a):
        return 2 if a == 0 else 1

    def first_copy(a, y, x):
        return pltpu.make_async_remote_copy(
            src_ref=one_out.at[a, y * chips_x + x, pl.ds(0, parts_of(a))],
            dst_ref=one_in.at[a, mine, pl.ds(0, parts_of(a))],
            send_sem=one_send.at[a],
            recv_sem=one_recv.at[a],
            device_id=(y, 2 * x + core),
            device_id_type=MESH,
        )

    def first_all(a):
        return pltpu.make_async_remote_copy(
            src_ref=one_out.at[a, pl.ds(0, chips - 1), pl.ds(0, parts_of(a))],
            dst_ref=one_in.at[a, pl.ds(0, chips - 1), pl.ds(0, parts_of(a))],
            send_sem=one_send.at[a],
            recv_sem=one_recv.at[a],
            device_id=(my, sibling),
            device_id_type=MESH,
        )

    def second_copy(a):
        return pltpu.make_async_remote_copy(
            src_ref=two_out.at[a, pl.ds(0, parts_of(a))],
            dst_ref=two_in.at[a, pl.ds(0, parts_of(a)), 1],
            send_sem=two_send.at[a],
            recv_sem=two_recv.at[a],
            device_id=(my, sibling),
            device_id_type=MESH,
        )

    def start_first(a):
        for k in range(1, chips_x):
            first_copy(a, my, lax.rem(chip_x + k, chips_x)).start()

        def one(j, carry):
            for k in range(chips_x):
                first_copy(a, lax.rem(my + j, tiles_y), lax.rem(chip_x + k, chips_x)).start()
            return carry

        lax.fori_loop(1, tiles_y, one, 0)
        for part in range(parts_of(a)):
            one_in[a, mine, part] = one_out[a, mine, part]

    def pass_on(a):
        first_all(a).wait_recv()
        kept = []
        for part in range(parts_of(a)):
            parts = one_in[a, :, part].astype(F32).reshape(chips, 2, CAP, 128)
            low, high = parts[:, 0], parts[:, 1]
            other = jnp.where(core == 0, high, low).reshape(chips * CAP, 128)
            two_out[a, part] = other.astype(BF16)
            own = jnp.where(core == 0, low, high).reshape(chips * CAP, 128)
            kept.append(own.astype(BF16))
        second_copy(a).start()
        for part in range(parts_of(a)):
            two_in[a, part, 0] = kept[part]

    def sum_copy(x):
        return pltpu.make_async_remote_copy(
            src_ref=sum_out,
            dst_ref=sum_in.at[chip_x],
            send_sem=sum_send.at[0],
            recv_sem=sum_recv.at[0],
            device_id=(my, 2 * x + core),
            device_id_type=MESH,
        )

    def total_copy(y):
        return pltpu.make_async_remote_copy(
            src_ref=total_out,
            dst_ref=total_in.at[my],
            send_sem=sum_send.at[1],
            recv_sem=sum_recv.at[1],
            device_id=(y, mx),
            device_id_type=MESH,
        )

    def sum_all():
        return pltpu.make_async_remote_copy(
            src_ref=sum_in.at[pl.ds(0, chips_x - 1)],
            dst_ref=sum_in.at[pl.ds(0, chips_x - 1)],
            send_sem=sum_send.at[0],
            recv_sem=sum_recv.at[0],
            device_id=(my, sibling),
            device_id_type=MESH,
        )

    def total_all():
        return pltpu.make_async_remote_copy(
            src_ref=total_in.at[pl.ds(0, tiles_y - 1)],
            dst_ref=total_in.at[pl.ds(0, tiles_y - 1)],
            send_sem=sum_send.at[1],
            recv_sem=sum_recv.at[1],
            device_id=(my, sibling),
            device_id_type=MESH,
        )

    def last_copy():
        return pltpu.make_async_remote_copy(
            src_ref=last_in.at[0],
            dst_ref=last_in.at[1],
            send_sem=sum_send.at[2],
            recv_sem=sum_recv.at[2],
            device_id=(my, sibling),
            device_id_type=MESH,
        )

    def unit(r, h):
        return pl.ds(r, CHUNK), pl.ds(pl.multiple_of(128 * h, 128), 128)

    def strip_rows(r, h, g):
        return pl.ds(pl.multiple_of((8 * h + g) * ROWS + r, CHUNK), CHUNK)

    def over_cells(work, sent, carry, wide):
        def step(j, carry):
            def one(u, carry):
                for k in range(wide):
                    number = u * wide + k
                    r = pl.multiple_of((number // 2) * HALF + j * CHUNK, CHUNK)
                    carry = work(r, number % 2, carry)
                return carry

            carry = one(0, carry) if wide == 4 else lax.fori_loop(0, 4 // wide, one, carry)
            if sent is not None:
                send_rows(sent, j)
            return carry

        carry = lax.fori_loop(0, STEPS, step, carry)
        if sent is not None:
            send_rest(sent)
        return carry

    def shares(it, r, h, wages, revenue):
        rows, lanes = unit(r, h)
        powers = [w * w * w for w in wages]
        inverse = 1.0 / sum(powers[1:], powers[0])
        people = resident_ref[rows, lanes]
        earned = sum([p * w for p, w in zip(powers[1:], wages[1:])], powers[0] * wages[0])
        income = earned * inverse
        income_ref[it, rows, lanes] = income
        scale = people * inverse
        supply = [p * scale for p in powers]
        for s in range(SECTORS):
            ext[2 * it, s, pl.ds(HALF + r, CHUNK), lanes] = supply[s].astype(BF16)
        for g, strip in enumerate(swap_blocks(supply)):
            table[strip_rows(r, h, g), :] = strip.astype(BF16)
        gain = people * rate_ref[rows, lanes] * income
        return revenue + gain[0:8] + gain[8:16]

    def gather(a):
        picked = jnp.dot(source_hot[...], table[...], preferred_element_type=F32).astype(BF16)
        ordered = jnp.dot(slot_hot[...], picked, preferred_element_type=F32).astype(BF16)
        one_out[a, :, 0] = ordered.reshape(chips, 2 * CAP, 128)

    zero = jnp.zeros((8, 128), F32)

    def first_cells(r, h, carry):
        people_sum, revenue = carry
        rows, lanes = unit(r, h)
        bracket = bracket_ref[rows, lanes]
        rate = jnp.zeros((CHUNK, 128), F32)
        for b in range(8):
            rate = jnp.where(bracket == b, tax_ref[b], rate)
        rate_ref[rows, lanes] = rate
        people = resident_ref[rows, lanes]
        people_sum = people_sum + people[0:8] + people[8:16]
        wages = [base_ref[s, rows, lanes].astype(F32) for s in range(SECTORS)]
        return people_sum, shares(0, r, h, wages, revenue)

    for load in loads:
        load.wait()
    people_sum, revenue0 = over_cells(first_cells, None, (zero, zero), 4)
    pl.semaphore_wait(barrier, chips + 1)
    for j in range(STEPS):
        send_rows(0, j)
    send_rest(0)

    line = lax.broadcasted_iota(jnp.int32, (8, far_pairs), 0)
    source, target = src_ref[...], dst_ref[...]
    row, group = target >> 4, target & 15
    fields = [
        dest_ref[...],
        (source & 15) * ROWS + (source >> 4),
        ((((row >> 4) & 3) * 2 + (row >> 6)) * GROUPS) + group,
        row & 15,
        count_ref[...],
    ]
    pairs = jnp.zeros((8, far_pairs), jnp.int32)
    for k, field in enumerate(fields):
        pairs = jnp.where(line == k, field, pairs)
    pairs = pairs.astype(F32)
    across = jnp.concatenate([pairs, jnp.zeros((120, far_pairs), F32)], axis=0).T
    dest_row = pairs[0:1, :]
    earlier = lax.broadcasted_iota(jnp.int32, (far_pairs, far_pairs), 0) < (
        lax.broadcasted_iota(jnp.int32, (far_pairs, far_pairs), 1)
    )
    same = (across[:, 0:1] == dest_row) & earlier
    rank = jnp.sum(jnp.where(same, 1.0, 0.0), axis=0, keepdims=True)
    slot_of = (dest_row * CAP + rank).astype(jnp.int32)
    slot_ids = lax.broadcasted_iota(jnp.int32, (slots, far_pairs), 0)
    slot_hot[...] = jnp.where(slot_ids == slot_of, 1.0, 0.0).astype(BF16)
    strip_ids = lax.broadcasted_iota(jnp.int32, (far_pairs, GROUPS * ROWS), 1)
    source_hot[...] = jnp.where(
        strip_ids == across[:, 1:2].astype(jnp.int32), 1.0, 0.0
    ).astype(BF16)
    one_out[0, :, 1] = (
        jnp.dot(slot_hot[...], across.astype(BF16), preferred_element_type=F32)
        .astype(BF16)
        .reshape(chips, 2 * CAP, 128)
    )
    gather(0)
    start_first(0)

    @pl.when(my == 0)
    def _():
        ext[:, :, 0:HALF, :] = jnp.zeros((2 * ITERS, SECTORS, HALF, COLS), BF16)

    @pl.when(my == tiles_y - 1)
    def _():
        ext[:, :, HALF + ROWS :, :] = jnp.zeros((2 * ITERS, SECTORS, HALF, COLS), BF16)

    @pl.when(mx == 0)
    def _():
        edge_in[:, 0] = jnp.zeros((2 * ITERS, PAIRS2, ROWS, 128), BF16)

    @pl.when(mx == tiles_x - 1)
    def _():
        edge_in[:, 1] = jnp.zeros((2 * ITERS, PAIRS2, ROWS, 128), BF16)

    sector = lax.broadcasted_iota(jnp.int32, (2 * SECTORS, COLS), 0)
    tap = lax.broadcasted_iota(jnp.int32, (2 * SECTORS, COLS), 1)
    decay = jnp.zeros((2 * SECTORS, COLS), F32)
    for s in range(SECTORS):
        decay = jnp.where(sector == s, commute_ref[s], decay)
        decay = jnp.where(sector == SECTORS + s, spill_ref[s], decay)
    offset = jnp.abs(tap - HALF).astype(F32) / HALF
    unscaled = jnp.where(tap <= 2 * HALF, jnp.exp(-decay * offset), 0.0)
    tap_row[...] = (unscaled / jnp.sum(unscaled, axis=1, keepdims=True)).astype(BF16).astype(F32)
    make_bands(0)


    def build_place():
        routing = two_in[0, 1].reshape(slots, 128)
        line = lax.broadcasted_iota(jnp.int32, (16, 128), 0)
        lane = lax.broadcasted_iota(jnp.int32, (16, 128), 1)
        pick = jnp.where((line == 0) & (lane == 2), float(CHUNK), 0.0)
        pick = jnp.where((line == 0) & (lane == 3), 1.0, pick)
        pick = jnp.where((line == 1) & (lane == 4), 1.0, pick).astype(BF16)
        found = lax.dot_general(
            pick, routing, (((1,), (1,)), ((), ())), preferred_element_type=F32
        )
        where_to, weight = found[0:1, :].astype(jnp.int32), found[1:2, :]

        def one(g, carry):
            strip = g * ROWS + lax.broadcasted_iota(jnp.int32, (ROWS, slots), 0)
            place[pl.ds(pl.multiple_of(g * ROWS, ROWS), ROWS), :] = jnp.where(
                strip == where_to, weight, 0.0
            ).astype(BF16)
            return carry

        lax.fori_loop(0, GROUPS, one, 0)

    revenues = [revenue0]
    for it in range(ITERS):
        if it > 0:
            gather(it)
            start_first(it)
        if it == ITERS - 1:
            line = lax.broadcasted_iota(jnp.int32, (8, 128), 0)
            parts = zero
            for k, part in enumerate([people_sum] + revenues):
                parts = jnp.where(line == k, jnp.sum(part, axis=0, keepdims=True), parts)
            sum_out[...] = parts

            def start_sum(j, carry):
                sum_copy(lax.rem(chip_x + j, chips_x)).start()
                return carry

            lax.fori_loop(1, chips_x, start_sum, 0)
            sum_in[chip_x] = parts
        rows_pass(2 * it, 0)
        columns_start(0, near)
        pass_on(it)
        if it == ITERS - 1:
            sum_all().wait_recv()
            halfway = jnp.sum(sum_in[...], axis=0)
            total_out[...] = halfway

            def start_total(j, carry):
                total_copy(lax.rem(my + j, tiles_y)).start()
                return carry

            lax.fori_loop(1, tiles_y, start_total, 0)
            total_in[my] = halfway
        columns_finish(2 * it, 0, near)
        if it == ITERS - 1:
            total_all().wait_recv()
            last_in[0] = jnp.sum(total_in[...], axis=0)
            last_copy().start()
        second_copy(it).wait_recv()
        if it == 0:
            build_place()

        def labor_step(j, carry):
            block = 2 * GROUPS * CHUNK
            far[...] = jnp.dot(
                place[pl.ds(pl.multiple_of(j * block, block), block), :],
                two_in[it, 0].reshape(slots, 128),
                preferred_element_type=F32,
            )
            for number in range(4):
                way, h = number // 2, number % 2
                r = pl.multiple_of(way * HALF + j * CHUNK, CHUNK)
                rows, lanes = unit(r, h)
                first = (way * GROUPS + 8 * h) * CHUNK
                strips = [far[first + CHUNK * g : first + CHUNK * (g + 1), :] for g in range(8)]
                for s, flow in enumerate(swap_blocks(strips)):
                    value = near[s, rows, lanes] + FAR_SCALE * flow
                    labor[s, rows, lanes] = value
                    ext[2 * it + 1, s, pl.ds(HALF + r, CHUNK), lanes] = value.astype(BF16)
            send_rows(2 * it + 1, j)
            return carry

        lax.fori_loop(0, STEPS, labor_step, 0)
        send_rest(2 * it + 1)
        if it == 0:
            make_bands(1)

        def labor_power(c, carry):
            rows = pl.ds(pl.multiple_of(c * CHUNK, CHUNK), CHUNK)
            for s in range(SECTORS):
                labor[s, rows, :] = -BETA_WAGE * jnp.log(1.0 + labor[s, rows, :])
            return carry

        lax.fori_loop(0, ROWS // CHUNK, labor_power, 0)
        if it == ITERS - 1:
            last_copy().wait_recv()
            sums = jnp.sum(last_in[0] + last_in[1], axis=1, keepdims=True)
            people_all = sums[0:1, 0:1]
            transfers = [sums[1 + k : 2 + k, 0:1] / people_all for k in range(ITERS)]

            def rent_chunk(c, carry):
                rows = pl.ds(pl.multiple_of(c * CHUNK, CHUNK), CHUNK)
                keep = 1.0 - rate_ref[rows, :]
                people, space = resident_ref[rows, :], floor_ref[rows, :]
                ratio = people / space
                square = None
                for k in range(ITERS):
                    net = keep * income_ref[k, rows, :] + transfers[k]
                    level = ratio if square is None else jnp.sqrt(square) * ratio
                    square = level * net
                rent_ref[rows, :] = square
                return carry

            lax.fori_loop(0, ROWS // CHUNK, rent_chunk, 0)
        rows_pass(2 * it + 1, 1)
        columns_start(1, near)
        columns_finish(2 * it + 1, 1, near)

        def wage_cells(r, h, revenue):
            rows, lanes = unit(r, h)
            logs = [jnp.log(1.0 + near[s, rows, lanes]) for s in range(SECTORS)]
            wages = []
            for s in range(SECTORS):
                power = labor[s, rows, lanes]
                for t in range(SECTORS):
                    power = power + mixing_ref[s, t] * logs[t]
                if it == ITERS - 1:
                    power_ref[s, rows, lanes] = power
                else:
                    wages.append(base_ref[s, rows, lanes].astype(F32) * jnp.exp(power))
            if it < ITERS - 1:
                revenue = shares(it + 1, r, h, wages, revenue)
            return revenue

        sent = 2 * it + 2 if it < ITERS - 1 else None
        revenues.append(over_cells(wage_cells, sent, zero, 4))

    for e in range(2 * ITERS):
        for way in range(2):

            @pl.when(can_row[way])
            def _():
                row_drain(e, way).wait_send()

            @pl.when(can_edge[way])
            def _():
                edge_drain(e, way).wait_send()

    for a in range(ITERS):
        first_all(a).wait_send()
        second_copy(a).wait_send()
    sum_all().wait_send()
    total_all().wait_send()
    last_copy().wait_send()


def body(
    base_prod,
    resident,
    floor_space,
    bracket,
    tax_rate,
    mixing,
    spill_decay,
    commute_decay,
    pair_dest,
    pair_src,
    pair_dst,
    pair_count,
):
    tiles_y = lax.axis_size("gy")
    tiles_x = lax.axis_size("gx")
    slots = tiles_y * tiles_x * CAP
    chips = tiles_y * tiles_x // 2
    far_pairs = pair_src.shape[0]
    vmem = pl.BlockSpec(memory_space=pltpu.VMEM)
    whole = pl.BlockSpec(memory_space=pltpu.HBM)
    smem = pltpu.SMEM
    exchanges = 2 * ITERS
    dma = pltpu.SemaphoreType.DMA
    power, square = pl.pallas_call(
        functools.partial(kernel, tiles_y, tiles_x),
        out_shape=(
            jax.ShapeDtypeStruct(base_prod.shape, F32),
            jax.ShapeDtypeStruct(resident.shape, F32),
        ),
        in_specs=[whole] * 12,
        out_specs=(vmem, vmem),
        scratch_shapes=[
            pltpu.VMEM((exchanges, SECTORS, ROWS + 2 * HALF, COLS), BF16),
            pltpu.VMEM((exchanges, 2, PAIRS2, ROWS, 128), BF16),
            pltpu.VMEM((exchanges, 2, PAIRS2, ROWS, 128), BF16),
            pltpu.VMEM((SECTORS, ROWS, COLS), BF16),
            pltpu.VMEM((SECTORS, ROWS, COLS), F32),
            pltpu.VMEM((SECTORS, ROWS, COLS), F32),
            pltpu.VMEM((2 * SECTORS, COLS), F32),
            pltpu.VMEM((2 * SECTORS, ROWS, COLS), BF16),
            pltpu.VMEM((2 * SECTORS, COLS, COLS), BF16),
            pltpu.VMEM((2 * SECTORS, 2, 128, 128), BF16),
            pltpu.VMEM((GROUPS * ROWS, 128), BF16),
            pltpu.VMEM((far_pairs, GROUPS * ROWS), BF16),
            pltpu.VMEM((slots, far_pairs), BF16),
            pltpu.VMEM((GROUPS * ROWS, slots), BF16),
            pltpu.VMEM((2 * GROUPS * CHUNK, 128), F32),
            pltpu.VMEM((ITERS, chips, 2, 2 * CAP, 128), BF16),
            pltpu.VMEM((ITERS, chips, 2, 2 * CAP, 128), BF16),
            pltpu.VMEM((ITERS, 2, chips * CAP, 128), BF16),
            pltpu.VMEM((ITERS, 2, 2, chips * CAP, 128), BF16),
            pltpu.VMEM((8, 128), F32),
            pltpu.VMEM((tiles_x // 2, 8, 128), F32),
            pltpu.VMEM((8, 128), F32),
            pltpu.VMEM((tiles_y, 8, 128), F32),
            pltpu.VMEM((ROWS, COLS), F32),
            pltpu.VMEM((ITERS, ROWS, COLS), F32),
            pltpu.VMEM((2, 8, 128), F32),
            pltpu.VMEM((SECTORS, ROWS, COLS), BF16),
            pltpu.VMEM((ROWS, COLS), F32),
            pltpu.VMEM((ROWS, COLS), F32),
            pltpu.VMEM((ROWS, COLS), jnp.int32),
            pltpu.VMEM((1, far_pairs), jnp.int32),
            pltpu.VMEM((1, far_pairs), jnp.int32),
            pltpu.VMEM((1, far_pairs), jnp.int32),
            pltpu.VMEM((1, far_pairs), jnp.int32),
            smem((8,), F32),
            smem((SECTORS,), F32),
            smem((SECTORS,), F32),
            smem((SECTORS, SECTORS), F32),
            dma((12,)),
            dma((exchanges, 2)),
            dma((exchanges, 2, 2)),
            dma((exchanges, 2)),
            dma((exchanges, 2, 2)),
            dma((ITERS,)),
            dma((ITERS,)),
            dma((ITERS,)),
            dma((ITERS,)),
            dma((3,)),
            dma((3,)),
        ],
        compiler_params=pltpu.CompilerParams(
            collective_id=0, has_side_effects=True, vmem_limit_bytes=40 * 1024 * 1024
        ),
    )(
        *(
            pltpu.with_memory_space_constraint(x, pltpu.HBM)
            for x in (
                base_prod,
                resident,
                floor_space,
                bracket,
                pair_dest.reshape(1, far_pairs),
                pair_src.reshape(1, far_pairs),
                pair_dst.reshape(1, far_pairs),
                pair_count.reshape(1, far_pairs),
                tax_rate,
                commute_decay,
                spill_decay,
                mixing,
            )
        )
    )
    return base_prod.astype(F32) * jnp.exp(power), jnp.sqrt(square)


def solution(mesh):
    return jax.shard_map(
        body,
        mesh=mesh,
        in_specs=(
            P(None, "gy", "gx"),
            P("gy", "gx"),
            P("gy", "gx"),
            P("gy", "gx"),
            P(),
            P(),
            P(),
            P(),
            P(("gy", "gx"), None),
            P(("gy", "gx")),
            P(("gy", "gx")),
            P(("gy", "gx")),
        ),
        out_specs=(P(None, "gy", "gx"), P("gy", "gx")),
        check_vma=False,
    )
```

```python
import functools

import jax
import jax.numpy as jnp
from jax import lax
from jax.experimental import pallas as pl
from jax.experimental.pallas import tpu as pltpu
from jax.sharding import PartitionSpec as P

HALF = 64
ITERS = 3
SECTORS = 8
CAP = 8
BETA_WAGE = 0.3
FAR_SCALE = 0.125
ROWS = 128
COLS = 256
GROUPS = COLS // 16
PAIRS2 = SECTORS // 2
CHUNK = 16
STEPS = HALF // CHUNK
PARTS = ((0, 3), (3, 1))
MESH = pl.DeviceIdType.MESH
F32 = jnp.float32
BF16 = jnp.bfloat16


def swap_blocks(values):
    values = [pltpu.roll(v, 16 * s, 1) if s else v for s, v in enumerate(values)]
    block = lax.broadcasted_iota(jnp.int32, values[0].shape, 1) // 16
    for d in (1, 2, 4):
        moved = (block & d) != 0
        values = [jnp.where(moved, values[(a + d) % 8], values[a]) for a in range(8)]
    values = [values[-g % 8] for g in range(8)]
    return [pltpu.roll(v, 128 - 16 * g, 1) if g else v for g, v in enumerate(values)]


def kernel(
    tiles_y,
    tiles_x,
    base_any,
    resident_any,
    floor_any,
    bracket_any,
    dest_any,
    src_any,
    dst_any,
    count_any,
    tax_any,
    commute_any,
    spill_any,
    mixing_any,
    power_ref,
    rent_ref,
    ext,
    edge_out,
    edge_in,
    mid,
    near,
    labor,
    tap_row,
    band_row,
    band_col,
    band_edge,
    table,
    source_hot,
    slot_hot,
    place,
    far,
    one_out,
    one_in,
    two_out,
    two_in,
    sum_out,
    sum_in,
    total_out,
    total_in,
    rate_ref,
    income_ref,
    last_in,
    base_ref,
    resident_ref,
    floor_ref,
    bracket_ref,
    dest_ref,
    src_ref,
    dst_ref,
    count_ref,
    tax_ref,
    commute_ref,
    spill_ref,
    mixing_ref,
    load_sem,
    row_send,
    row_recv,
    edge_send,
    edge_recv,
    one_send,
    one_recv,
    two_send,
    two_recv,
    sum_send,
    sum_recv,
):
    my = lax.axis_index("gy")
    mx = lax.axis_index("gx")
    chips_x = tiles_x // 2
    chips = tiles_y * chips_x
    core = lax.rem(mx, 2)
    chip_x = mx // 2
    sibling = mx + 1 - 2 * core
    beyond = lax.rem(mx + 2 * core - 1 + tiles_x, tiles_x)
    mine = my * chips_x + chip_x
    slots = tiles_y * tiles_x * CAP
    far_pairs = dest_ref.shape[1]

    loads = [
        pltpu.make_async_copy(source, target, load_sem.at[k])
        for k, (source, target) in enumerate(
            (
                (base_any, base_ref),
                (resident_any, resident_ref),
                (bracket_any, bracket_ref),
                (floor_any, floor_ref),
                (dest_any, dest_ref),
                (src_any, src_ref),
                (dst_any, dst_ref),
                (count_any, count_ref),
                (tax_any, tax_ref),
                (commute_any, commute_ref),
                (spill_any, spill_ref),
                (mixing_any, mixing_ref),
            )
        )
    ]
    for load in loads:
        load.start()

    barrier = pltpu.get_barrier_semaphore()

    def greet(y, x):
        pl.semaphore_signal(barrier, inc=1, device_id=(y, x), device_id_type=MESH)

    def greet_row(j, carry):
        for k in range(chips_x):
            greet(lax.rem(my + j, tiles_y), 2 * lax.rem(chip_x + k, chips_x) + core)
        return carry

    greet(my, sibling)
    greet(my, beyond)
    for k in range(1, chips_x):
        greet(my, 2 * lax.rem(chip_x + k, chips_x) + core)
    lax.fori_loop(1, tiles_y, greet_row, 0)

    def row_copy(e, way, sectors, j, height, slot):
        start = HALF if way == 0 else ROWS
        land = HALF + ROWS if way == 0 else 0
        target = my - 1 if way == 0 else my + 1
        step = pl.multiple_of(j * height, height)
        return pltpu.make_async_remote_copy(
            src_ref=ext.at[e, sectors, pl.ds(start + step, height), :],
            dst_ref=ext.at[e, sectors, pl.ds(land + step, height), :],
            send_sem=row_send.at[e, way],
            recv_sem=row_recv.at[e, way, slot],
            device_id=(target, mx),
            device_id_type=MESH,
        )

    def row_step(e, way, j):
        return row_copy(e, way, pl.ds(0, 2 * PARTS[0][1]), j, CHUNK, 0)

    def row_rest(e, way):
        return row_copy(e, way, pl.ds(2 * PARTS[1][0], 2 * PARTS[1][1]), 0, HALF, 1)

    def row_drain(e, way):
        start = HALF if way == 0 else ROWS
        target = my - 1 if way == 0 else my + 1
        return pltpu.make_async_remote_copy(
            src_ref=ext.at[e, :, pl.ds(start, HALF), :],
            dst_ref=ext.at[e, :, pl.ds(start, HALF), :],
            send_sem=row_send.at[e, way],
            recv_sem=row_recv.at[e, way, 0],
            device_id=(target, mx),
            device_id_type=MESH,
        )

    can_row = (my > 0, my < tiles_y - 1)
    can_edge = (mx > 0, mx < tiles_x - 1)

    def send_rows(e, j):
        for way in range(2):

            @pl.when(can_row[way])
            def _():
                row_step(e, way, j).start()

    def send_rest(e):
        for way in range(2):

            @pl.when(can_row[way])
            def _():
                row_rest(e, way).start()

    def wait_rows(e, part):
        for way in range(2):

            @pl.when(can_row[1 - way])
            def _():
                if part == 0:
                    row_copy(e, way, pl.ds(0, 2 * PARTS[0][1]), 0, HALF, 0).wait_recv()
                else:
                    row_rest(e, way).wait_recv()

    def edge_copy(e, part, way):
        target = mx - 1 if way == 0 else mx + 1
        pairs = pl.ds(*PARTS[part])
        return pltpu.make_async_remote_copy(
            src_ref=edge_out.at[e, way, pairs],
            dst_ref=edge_in.at[e, 1 - way, pairs],
            send_sem=edge_send.at[e, way],
            recv_sem=edge_recv.at[e, way, part],
            device_id=(my, target),
            device_id_type=MESH,
        )

    def edge_drain(e, way):
        target = mx - 1 if way == 0 else mx + 1
        return pltpu.make_async_remote_copy(
            src_ref=edge_out.at[e, way],
            dst_ref=edge_in.at[e, 1 - way],
            send_sem=edge_send.at[e, way],
            recv_sem=edge_recv.at[e, way, 0],
            device_id=(my, target),
            device_id_type=MESH,
        )

    lane128 = lax.broadcasted_iota(jnp.int32, (ROWS, 128), 1)

    def rows_pass(e, kind):
        for part, (first_pair, count) in enumerate(PARTS):
            wait_rows(e, part)
            for i in range(first_pair, first_pair + count):
                ends = []
                for s in (2 * i, 2 * i + 1):
                    passed = jnp.dot(
                        band_row[kind * SECTORS + s], ext[e, s], preferred_element_type=F32
                    )
                    mid[s] = passed.astype(BF16)
                    ends.append((passed[:, 0:128], passed[:, 128:256]))
                first, second = ends
                low = lane128 < HALF
                edge_out[e, 0, i] = jnp.where(
                    low, first[0], pltpu.roll(second[0], HALF, 1)
                ).astype(BF16)
                edge_out[e, 1, i] = jnp.where(
                    low, pltpu.roll(second[1], HALF, 1), first[1]
                ).astype(BF16)
            for way in range(2):

                @pl.when(can_edge[way])
                def _():
                    edge_copy(e, part, way).start()

    def columns_start(kind, result):
        def one(half, carry):
            for k in range(4):
                s = 4 * half + k
                result[s] = jnp.dot(
                    mid[s], band_col[kind * SECTORS + s], preferred_element_type=F32
                )
            return carry

        lax.fori_loop(0, 2, one, 0)

    def columns_finish(e, kind, result):
        for part, (first_pair, count) in enumerate(PARTS):
            for way in range(2):

                @pl.when(can_edge[1 - way])
                def _():
                    edge_copy(e, part, way).wait_recv()

            for s in range(2 * first_pair, 2 * (first_pair + count)):
                for side in range(2):
                    lanes = slice(128 * side, 128 * side + 128)
                    result[s, :, lanes] += jnp.dot(
                        edge_in[e, side, s // 2],
                        band_edge[kind * SECTORS + s, side],
                        preferred_element_type=F32,
                    )

    def make_bands(kind):
        u = lax.broadcasted_iota(jnp.int32, (COLS, COLS), 0)
        x = lax.broadcasted_iota(jnp.int32, (COLS, COLS), 1)
        inside = jnp.abs(u - x) <= 128

        def one(s, carry):
            b = kind * SECTORS + s
            line = jnp.broadcast_to(tap_row[pl.ds(b, 1), :], (ROWS, COLS))
            rows_band = pltpu.roll(line, 0, 1, stride=1, stride_axis=0)
            band_row[b] = rows_band.astype(BF16)
            circle = jnp.concatenate(
                [pltpu.roll(rows_band, COLS - HALF, 1), pltpu.roll(rows_band, HALF, 1)], axis=0
            )
            band_col[b] = jnp.where(inside, circle, 0.0).astype(BF16)
            rest = jnp.where(inside, 0.0, circle)
            swap = lax.rem(s, 2) == 1
            for side in range(2):
                block = rest[128 - 128 * side : 256 - 128 * side, 128 * side : 128 * side + 128]
                turned = jnp.concatenate([block[HALF:], block[:HALF]], axis=0)
                band_edge[b, side] = jnp.where(swap, turned, block).astype(BF16)
            return carry

        lax.fori_loop(0, SECTORS, one, 0)

    def parts_of(a):
        return 2 if a == 0 else 1

    def first_copy(a, y, x):
        return pltpu.make_async_remote_copy(
            src_ref=one_out.at[a, y * chips_x + x, pl.ds(0, parts_of(a))],
            dst_ref=one_in.at[a, mine, pl.ds(0, parts_of(a))],
            send_sem=one_send.at[a],
            recv_sem=one_recv.at[a],
            device_id=(y, 2 * x + core),
            device_id_type=MESH,
        )

    def first_all(a):
        return pltpu.make_async_remote_copy(
            src_ref=one_out.at[a, pl.ds(0, chips - 1), pl.ds(0, parts_of(a))],
            dst_ref=one_in.at[a, pl.ds(0, chips - 1), pl.ds(0, parts_of(a))],
            send_sem=one_send.at[a],
            recv_sem=one_recv.at[a],
            device_id=(my, sibling),
            device_id_type=MESH,
        )

    def second_copy(a):
        return pltpu.make_async_remote_copy(
            src_ref=two_out.at[a, pl.ds(0, parts_of(a))],
            dst_ref=two_in.at[a, pl.ds(0, parts_of(a)), 1],
            send_sem=two_send.at[a],
            recv_sem=two_recv.at[a],
            device_id=(my, sibling),
            device_id_type=MESH,
        )

    def start_first(a):
        def far_first(count):
            return sorted(range(count), key=lambda d: -min(d % 4, -d % 4) - (d // 4) / 2)

        for j in far_first(tiles_y):
            y = lax.rem(my + j, tiles_y)
            for k in far_first(chips_x):
                if j or k:
                    first_copy(a, y, lax.rem(chip_x + k, chips_x)).start()
        for part in range(parts_of(a)):
            one_in[a, mine, part] = one_out[a, mine, part]

    def pass_on(a):
        first_all(a).wait_recv()
        kept = []
        for part in range(parts_of(a)):
            parts = one_in[a, :, part].astype(F32).reshape(chips, 2, CAP, 128)
            low, high = parts[:, 0], parts[:, 1]
            other = jnp.where(core == 0, high, low).reshape(chips * CAP, 128)
            two_out[a, part] = other.astype(BF16)
            own = jnp.where(core == 0, low, high).reshape(chips * CAP, 128)
            kept.append(own.astype(BF16))
        second_copy(a).start()
        for part in range(parts_of(a)):
            two_in[a, part, 0] = kept[part]

    def sum_copy(x):
        return pltpu.make_async_remote_copy(
            src_ref=sum_out,
            dst_ref=sum_in.at[chip_x],
            send_sem=sum_send.at[0],
            recv_sem=sum_recv.at[0],
            device_id=(my, 2 * x + core),
            device_id_type=MESH,
        )

    def total_copy(y):
        return pltpu.make_async_remote_copy(
            src_ref=total_out,
            dst_ref=total_in.at[my],
            send_sem=sum_send.at[1],
            recv_sem=sum_recv.at[1],
            device_id=(y, mx),
            device_id_type=MESH,
        )

    def sum_all():
        return pltpu.make_async_remote_copy(
            src_ref=sum_in.at[pl.ds(0, chips_x - 1)],
            dst_ref=sum_in.at[pl.ds(0, chips_x - 1)],
            send_sem=sum_send.at[0],
            recv_sem=sum_recv.at[0],
            device_id=(my, sibling),
            device_id_type=MESH,
        )

    def total_all():
        return pltpu.make_async_remote_copy(
            src_ref=total_in.at[pl.ds(0, tiles_y - 1)],
            dst_ref=total_in.at[pl.ds(0, tiles_y - 1)],
            send_sem=sum_send.at[1],
            recv_sem=sum_recv.at[1],
            device_id=(my, sibling),
            device_id_type=MESH,
        )

    def last_copy():
        return pltpu.make_async_remote_copy(
            src_ref=last_in.at[0],
            dst_ref=last_in.at[1],
            send_sem=sum_send.at[2],
            recv_sem=sum_recv.at[2],
            device_id=(my, sibling),
            device_id_type=MESH,
        )

    def unit(r, h):
        return pl.ds(r, CHUNK), pl.ds(pl.multiple_of(128 * h, 128), 128)

    def strip_rows(r, h, g):
        return pl.ds(pl.multiple_of((8 * h + g) * ROWS + r, CHUNK), CHUNK)

    def over_cells(work, sent, carry, wide):
        def step(j, carry):
            def one(u, carry):
                for k in range(wide):
                    number = u * wide + k
                    r = pl.multiple_of((number // 2) * HALF + j * CHUNK, CHUNK)
                    carry = work(r, number % 2, carry)
                return carry

            carry = one(0, carry) if wide == 4 else lax.fori_loop(0, 4 // wide, one, carry)
            if sent is not None:
                send_rows(sent, j)
            return carry

        carry = lax.fori_loop(0, STEPS, step, carry)
        if sent is not None:
            send_rest(sent)
        return carry

    def shares(it, r, h, wages, revenue):
        rows, lanes = unit(r, h)
        powers = [w * w * w for w in wages]
        inverse = 1.0 / sum(powers[1:], powers[0])
        people = resident_ref[rows, lanes]
        earned = sum([p * w for p, w in zip(powers[1:], wages[1:])], powers[0] * wages[0])
        income = earned * inverse
        income_ref[it, rows, lanes] = income
        scale = people * inverse
        supply = [p * scale for p in powers]
        for s in range(SECTORS):
            ext[2 * it, s, pl.ds(HALF + r, CHUNK), lanes] = supply[s].astype(BF16)
        for g, strip in enumerate(swap_blocks(supply)):
            table[strip_rows(r, h, g), :] = strip.astype(BF16)
        gain = people * rate_ref[rows, lanes] * income
        return revenue + gain[0:8] + gain[8:16]

    def gather(a):
        picked = jnp.dot(source_hot[...], table[...], preferred_element_type=F32).astype(BF16)
        ordered = jnp.dot(slot_hot[...], picked, preferred_element_type=F32).astype(BF16)
        one_out[a, :, 0] = ordered.reshape(chips, 2 * CAP, 128)

    zero = jnp.zeros((8, 128), F32)

    def first_cells(r, h, carry):
        people_sum, revenue = carry
        rows, lanes = unit(r, h)
        bracket = bracket_ref[rows, lanes]
        rate = jnp.zeros((CHUNK, 128), F32)
        for b in range(8):
            rate = jnp.where(bracket == b, tax_ref[b], rate)
        rate_ref[rows, lanes] = rate
        people = resident_ref[rows, lanes]
        people_sum = people_sum + people[0:8] + people[8:16]
        wages = [base_ref[s, rows, lanes].astype(F32) for s in range(SECTORS)]
        return people_sum, shares(0, r, h, wages, revenue)

    for load in loads:
        load.wait()
    people_sum, revenue0 = over_cells(first_cells, None, (zero, zero), 4)
    pl.semaphore_wait(barrier, chips + 1)
    for j in range(STEPS):
        send_rows(0, j)
    send_rest(0)

    line = lax.broadcasted_iota(jnp.int32, (8, far_pairs), 0)
    source, target = src_ref[...], dst_ref[...]
    row, group = target >> 4, target & 15
    fields = [
        dest_ref[...],
        (source & 15) * ROWS + (source >> 4),
        ((((row >> 4) & 3) * 2 + (row >> 6)) * GROUPS) + group,
        row & 15,
        count_ref[...],
    ]
    pairs = jnp.zeros((8, far_pairs), jnp.int32)
    for k, field in enumerate(fields):
        pairs = jnp.where(line == k, field, pairs)
    pairs = pairs.astype(F32)
    across = jnp.concatenate([pairs, jnp.zeros((120, far_pairs), F32)], axis=0).T
    dest_row = pairs[0:1, :]
    earlier = lax.broadcasted_iota(jnp.int32, (far_pairs, far_pairs), 0) < (
        lax.broadcasted_iota(jnp.int32, (far_pairs, far_pairs), 1)
    )
    same = (across[:, 0:1] == dest_row) & earlier
    rank = jnp.sum(jnp.where(same, 1.0, 0.0), axis=0, keepdims=True)
    slot_of = (dest_row * CAP + rank).astype(jnp.int32)
    slot_ids = lax.broadcasted_iota(jnp.int32, (slots, far_pairs), 0)
    slot_hot[...] = jnp.where(slot_ids == slot_of, 1.0, 0.0).astype(BF16)
    strip_ids = lax.broadcasted_iota(jnp.int32, (far_pairs, GROUPS * ROWS), 1)
    source_hot[...] = jnp.where(
        strip_ids == across[:, 1:2].astype(jnp.int32), 1.0, 0.0
    ).astype(BF16)
    one_out[0, :, 1] = (
        jnp.dot(slot_hot[...], across.astype(BF16), preferred_element_type=F32)
        .astype(BF16)
        .reshape(chips, 2 * CAP, 128)
    )
    gather(0)
    start_first(0)

    @pl.when(my == 0)
    def _():
        ext[:, :, 0:HALF, :] = jnp.zeros((2 * ITERS, SECTORS, HALF, COLS), BF16)

    @pl.when(my == tiles_y - 1)
    def _():
        ext[:, :, HALF + ROWS :, :] = jnp.zeros((2 * ITERS, SECTORS, HALF, COLS), BF16)

    @pl.when(mx == 0)
    def _():
        edge_in[:, 0] = jnp.zeros((2 * ITERS, PAIRS2, ROWS, 128), BF16)

    @pl.when(mx == tiles_x - 1)
    def _():
        edge_in[:, 1] = jnp.zeros((2 * ITERS, PAIRS2, ROWS, 128), BF16)

    sector = lax.broadcasted_iota(jnp.int32, (2 * SECTORS, COLS), 0)
    tap = lax.broadcasted_iota(jnp.int32, (2 * SECTORS, COLS), 1)
    decay = jnp.zeros((2 * SECTORS, COLS), F32)
    for s in range(SECTORS):
        decay = jnp.where(sector == s, commute_ref[s], decay)
        decay = jnp.where(sector == SECTORS + s, spill_ref[s], decay)
    offset = jnp.abs(tap - HALF).astype(F32) / HALF
    unscaled = jnp.where(tap <= 2 * HALF, jnp.exp(-decay * offset), 0.0)
    tap_row[...] = (unscaled / jnp.sum(unscaled, axis=1, keepdims=True)).astype(BF16).astype(F32)
    make_bands(0)


    def build_place():
        routing = two_in[0, 1].reshape(slots, 128)
        line = lax.broadcasted_iota(jnp.int32, (16, 128), 0)
        lane = lax.broadcasted_iota(jnp.int32, (16, 128), 1)
        pick = jnp.where((line == 0) & (lane == 2), float(CHUNK), 0.0)
        pick = jnp.where((line == 0) & (lane == 3), 1.0, pick)
        pick = jnp.where((line == 1) & (lane == 4), 1.0, pick).astype(BF16)
        found = lax.dot_general(
            pick, routing, (((1,), (1,)), ((), ())), preferred_element_type=F32
        )
        where_to, weight = found[0:1, :].astype(jnp.int32), found[1:2, :]

        def one(g, carry):
            strip = g * ROWS + lax.broadcasted_iota(jnp.int32, (ROWS, slots), 0)
            place[pl.ds(pl.multiple_of(g * ROWS, ROWS), ROWS), :] = jnp.where(
                strip == where_to, weight, 0.0
            ).astype(BF16)
            return carry

        lax.fori_loop(0, GROUPS, one, 0)

    revenues = [revenue0]
    for it in range(ITERS):
        if it > 0:
            gather(it)
            start_first(it)
        if it == ITERS - 1:
            line = lax.broadcasted_iota(jnp.int32, (8, 128), 0)
            parts = zero
            for k, part in enumerate([people_sum] + revenues):
                parts = jnp.where(line == k, jnp.sum(part, axis=0, keepdims=True), parts)
            sum_out[...] = parts

            def start_sum(j, carry):
                sum_copy(lax.rem(chip_x + j, chips_x)).start()
                return carry

            lax.fori_loop(1, chips_x, start_sum, 0)
            sum_in[chip_x] = parts
        rows_pass(2 * it, 0)
        columns_start(0, near)
        pass_on(it)
        if it == ITERS - 1:
            sum_all().wait_recv()
            halfway = jnp.sum(sum_in[...], axis=0)
            total_out[...] = halfway

            def start_total(j, carry):
                total_copy(lax.rem(my + j, tiles_y)).start()
                return carry

            lax.fori_loop(1, tiles_y, start_total, 0)
            total_in[my] = halfway
        columns_finish(2 * it, 0, near)
        if it == ITERS - 1:
            total_all().wait_recv()
            last_in[0] = jnp.sum(total_in[...], axis=0)
            last_copy().start()
        second_copy(it).wait_recv()
        if it == 0:
            build_place()

        def labor_step(j, carry):
            block = 2 * GROUPS * CHUNK
            far[...] = jnp.dot(
                place[pl.ds(pl.multiple_of(j * block, block), block), :],
                two_in[it, 0].reshape(slots, 128),
                preferred_element_type=F32,
            )
            for number in range(4):
                way, h = number // 2, number % 2
                r = pl.multiple_of(way * HALF + j * CHUNK, CHUNK)
                rows, lanes = unit(r, h)
                first = (way * GROUPS + 8 * h) * CHUNK
                strips = [far[first + CHUNK * g : first + CHUNK * (g + 1), :] for g in range(8)]
                for s, flow in enumerate(swap_blocks(strips)):
                    value = near[s, rows, lanes] + FAR_SCALE * flow
                    labor[s, rows, lanes] = value
                    ext[2 * it + 1, s, pl.ds(HALF + r, CHUNK), lanes] = value.astype(BF16)
            send_rows(2 * it + 1, j)
            return carry

        lax.fori_loop(0, STEPS, labor_step, 0)
        send_rest(2 * it + 1)
        if it == 0:
            make_bands(1)

        def labor_power(c, carry):
            rows = pl.ds(pl.multiple_of(c * CHUNK, CHUNK), CHUNK)
            for s in range(SECTORS):
                labor[s, rows, :] = -BETA_WAGE * jnp.log(1.0 + labor[s, rows, :])
            return carry

        lax.fori_loop(0, ROWS // CHUNK, labor_power, 0)
        if it == ITERS - 1:
            last_copy().wait_recv()
            sums = jnp.sum(last_in[0] + last_in[1], axis=1, keepdims=True)
            people_all = sums[0:1, 0:1]
            transfers = [sums[1 + k : 2 + k, 0:1] / people_all for k in range(ITERS)]

            def rent_chunk(c, carry):
                rows = pl.ds(pl.multiple_of(c * CHUNK, CHUNK), CHUNK)
                keep = 1.0 - rate_ref[rows, :]
                people, space = resident_ref[rows, :], floor_ref[rows, :]
                ratio = people / space
                square = None
                for k in range(ITERS):
                    net = keep * income_ref[k, rows, :] + transfers[k]
                    level = ratio if square is None else jnp.sqrt(square) * ratio
                    square = level * net
                rent_ref[rows, :] = square
                return carry

            lax.fori_loop(0, ROWS // CHUNK, rent_chunk, 0)
        rows_pass(2 * it + 1, 1)
        columns_start(1, near)
        columns_finish(2 * it + 1, 1, near)

        def wage_cells(r, h, revenue):
            rows, lanes = unit(r, h)
            logs = [jnp.log(1.0 + near[s, rows, lanes]) for s in range(SECTORS)]
            wages = []
            for s in range(SECTORS):
                power = labor[s, rows, lanes]
                for t in range(SECTORS):
                    power = power + mixing_ref[s, t] * logs[t]
                if it == ITERS - 1:
                    power_ref[s, rows, lanes] = power
                else:
                    wages.append(base_ref[s, rows, lanes].astype(F32) * jnp.exp(power))
            if it < ITERS - 1:
                revenue = shares(it + 1, r, h, wages, revenue)
            return revenue

        sent = 2 * it + 2 if it < ITERS - 1 else None
        revenues.append(over_cells(wage_cells, sent, zero, 4))

    for e in range(2 * ITERS):
        for way in range(2):

            @pl.when(can_row[way])
            def _():
                row_drain(e, way).wait_send()

            @pl.when(can_edge[way])
            def _():
                edge_drain(e, way).wait_send()

    for a in range(ITERS):
        first_all(a).wait_send()
        second_copy(a).wait_send()
    sum_all().wait_send()
    total_all().wait_send()
    last_copy().wait_send()


def body(
    base_prod,
    resident,
    floor_space,
    bracket,
    tax_rate,
    mixing,
    spill_decay,
    commute_decay,
    pair_dest,
    pair_src,
    pair_dst,
    pair_count,
):
    tiles_y = lax.axis_size("gy")
    tiles_x = lax.axis_size("gx")
    slots = tiles_y * tiles_x * CAP
    chips = tiles_y * tiles_x // 2
    far_pairs = pair_src.shape[0]
    vmem = pl.BlockSpec(memory_space=pltpu.VMEM)
    whole = pl.BlockSpec(memory_space=pltpu.HBM)
    smem = pltpu.SMEM
    exchanges = 2 * ITERS
    dma = pltpu.SemaphoreType.DMA
    power, square = pl.pallas_call(
        functools.partial(kernel, tiles_y, tiles_x),
        out_shape=(
            jax.ShapeDtypeStruct(base_prod.shape, F32),
            jax.ShapeDtypeStruct(resident.shape, F32),
        ),
        in_specs=[whole] * 12,
        out_specs=(vmem, vmem),
        scratch_shapes=[
            pltpu.VMEM((exchanges, SECTORS, ROWS + 2 * HALF, COLS), BF16),
            pltpu.VMEM((exchanges, 2, PAIRS2, ROWS, 128), BF16),
            pltpu.VMEM((exchanges, 2, PAIRS2, ROWS, 128), BF16),
            pltpu.VMEM((SECTORS, ROWS, COLS), BF16),
            pltpu.VMEM((SECTORS, ROWS, COLS), F32),
            pltpu.VMEM((SECTORS, ROWS, COLS), F32),
            pltpu.VMEM((2 * SECTORS, COLS), F32),
            pltpu.VMEM((2 * SECTORS, ROWS, COLS), BF16),
            pltpu.VMEM((2 * SECTORS, COLS, COLS), BF16),
            pltpu.VMEM((2 * SECTORS, 2, 128, 128), BF16),
            pltpu.VMEM((GROUPS * ROWS, 128), BF16),
            pltpu.VMEM((far_pairs, GROUPS * ROWS), BF16),
            pltpu.VMEM((slots, far_pairs), BF16),
            pltpu.VMEM((GROUPS * ROWS, slots), BF16),
            pltpu.VMEM((2 * GROUPS * CHUNK, 128), F32),
            pltpu.VMEM((ITERS, chips, 2, 2 * CAP, 128), BF16),
            pltpu.VMEM((ITERS, chips, 2, 2 * CAP, 128), BF16),
            pltpu.VMEM((ITERS, 2, chips * CAP, 128), BF16),
            pltpu.VMEM((ITERS, 2, 2, chips * CAP, 128), BF16),
            pltpu.VMEM((8, 128), F32),
            pltpu.VMEM((tiles_x // 2, 8, 128), F32),
            pltpu.VMEM((8, 128), F32),
            pltpu.VMEM((tiles_y, 8, 128), F32),
            pltpu.VMEM((ROWS, COLS), F32),
            pltpu.VMEM((ITERS, ROWS, COLS), F32),
            pltpu.VMEM((2, 8, 128), F32),
            pltpu.VMEM((SECTORS, ROWS, COLS), BF16),
            pltpu.VMEM((ROWS, COLS), F32),
            pltpu.VMEM((ROWS, COLS), F32),
            pltpu.VMEM((ROWS, COLS), jnp.int32),
            pltpu.VMEM((1, far_pairs), jnp.int32),
            pltpu.VMEM((1, far_pairs), jnp.int32),
            pltpu.VMEM((1, far_pairs), jnp.int32),
            pltpu.VMEM((1, far_pairs), jnp.int32),
            smem((8,), F32),
            smem((SECTORS,), F32),
            smem((SECTORS,), F32),
            smem((SECTORS, SECTORS), F32),
            dma((12,)),
            dma((exchanges, 2)),
            dma((exchanges, 2, 2)),
            dma((exchanges, 2)),
            dma((exchanges, 2, 2)),
            dma((ITERS,)),
            dma((ITERS,)),
            dma((ITERS,)),
            dma((ITERS,)),
            dma((3,)),
            dma((3,)),
        ],
        compiler_params=pltpu.CompilerParams(
            collective_id=0, has_side_effects=True, vmem_limit_bytes=40 * 1024 * 1024
        ),
    )(
        *(
            pltpu.with_memory_space_constraint(x, pltpu.HBM)
            for x in (
                base_prod,
                resident,
                floor_space,
                bracket,
                pair_dest.reshape(1, far_pairs),
                pair_src.reshape(1, far_pairs),
                pair_dst.reshape(1, far_pairs),
                pair_count.reshape(1, far_pairs),
                tax_rate,
                commute_decay,
                spill_decay,
                mixing,
            )
        )
    )
    return base_prod.astype(F32) * jnp.exp(power), jnp.sqrt(square)


def solution(mesh):
    return jax.shard_map(
        body,
        mesh=mesh,
        in_specs=(
            P(None, "gy", "gx"),
            P("gy", "gx"),
            P("gy", "gx"),
            P("gy", "gx"),
            P(),
            P(),
            P(),
            P(),
            P(("gy", "gx"), None),
            P(("gy", "gx")),
            P(("gy", "gx")),
            P(("gy", "gx")),
        ),
        out_specs=(P(None, "gy", "gx"), P("gy", "gx")),
        check_vma=False,
    )
```

```python
import functools

import jax
import jax.numpy as jnp
from jax import lax
from jax.experimental import pallas as pl
from jax.experimental.pallas import tpu as pltpu
from jax.sharding import PartitionSpec as P

HALF = 64
ITERS = 3
SECTORS = 8
CAP = 8
BETA_WAGE = 0.3
FAR_SCALE = 0.125
ROWS = 128
COLS = 256
GROUPS = COLS // 16
PAIRS2 = SECTORS // 2
CHUNK = 16
STEPS = HALF // CHUNK
PARTS = ((0, 3), (3, 1))
MESH = pl.DeviceIdType.MESH
F32 = jnp.float32
BF16 = jnp.bfloat16


def swap_blocks(values):
    values = [pltpu.roll(v, 16 * s, 1) if s else v for s, v in enumerate(values)]
    block = lax.broadcasted_iota(jnp.int32, values[0].shape, 1) // 16
    for d in (1, 2, 4):
        moved = (block & d) != 0
        values = [jnp.where(moved, values[(a + d) % 8], values[a]) for a in range(8)]
    values = [values[-g % 8] for g in range(8)]
    return [pltpu.roll(v, 128 - 16 * g, 1) if g else v for g, v in enumerate(values)]


def kernel(
    tiles_y,
    tiles_x,
    base_any,
    resident_any,
    floor_any,
    bracket_any,
    dest_any,
    src_any,
    dst_any,
    count_any,
    tax_any,
    commute_any,
    spill_any,
    mixing_any,
    power_ref,
    rent_ref,
    ext,
    edge_out,
    edge_in,
    mid,
    near,
    labor,
    tap_row,
    band_row,
    band_col,
    band_edge,
    table,
    source_hot,
    slot_hot,
    place,
    far,
    one_out,
    one_in,
    two_out,
    two_in,
    sum_out,
    sum_in,
    total_out,
    total_in,
    rate_ref,
    income_ref,
    last_in,
    base_ref,
    resident_ref,
    floor_ref,
    bracket_ref,
    dest_ref,
    src_ref,
    dst_ref,
    count_ref,
    tax_ref,
    commute_ref,
    spill_ref,
    mixing_ref,
    load_sem,
    row_send,
    row_recv,
    edge_send,
    edge_recv,
    one_send,
    one_recv,
    two_send,
    two_recv,
    sum_send,
    sum_recv,
):
    my = lax.axis_index("gy")
    mx = lax.axis_index("gx")
    chips_x = tiles_x // 2
    chips = tiles_y * chips_x
    core = lax.rem(mx, 2)
    chip_x = mx // 2
    sibling = mx + 1 - 2 * core
    beyond = lax.rem(mx + 2 * core - 1 + tiles_x, tiles_x)
    mine = my * chips_x + chip_x
    slots = tiles_y * tiles_x * CAP
    far_pairs = dest_ref.shape[1]

    loads = [
        pltpu.make_async_copy(source, target, load_sem.at[k])
        for k, (source, target) in enumerate(
            (
                (base_any, base_ref),
                (resident_any, resident_ref),
                (bracket_any, bracket_ref),
                (floor_any, floor_ref),
                (dest_any, dest_ref),
                (src_any, src_ref),
                (dst_any, dst_ref),
                (count_any, count_ref),
                (tax_any, tax_ref),
                (commute_any, commute_ref),
                (spill_any, spill_ref),
                (mixing_any, mixing_ref),
            )
        )
    ]
    for load in loads:
        load.start()

    barrier = pltpu.get_barrier_semaphore()

    def greet(y, x):
        pl.semaphore_signal(barrier, inc=1, device_id=(y, x), device_id_type=MESH)

    def greet_row(j, carry):
        for k in range(chips_x):
            greet(lax.rem(my + j, tiles_y), 2 * lax.rem(chip_x + k, chips_x) + core)
        return carry

    greet(my, sibling)
    greet(my, beyond)
    for k in range(1, chips_x):
        greet(my, 2 * lax.rem(chip_x + k, chips_x) + core)
    lax.fori_loop(1, tiles_y, greet_row, 0)

    def row_copy(e, way, sectors, j, height, slot):
        start = HALF if way == 0 else ROWS
        land = HALF + ROWS if way == 0 else 0
        target = my - 1 if way == 0 else my + 1
        step = pl.multiple_of(j * height, height)
        return pltpu.make_async_remote_copy(
            src_ref=ext.at[e, sectors, pl.ds(start + step, height), :],
            dst_ref=ext.at[e, sectors, pl.ds(land + step, height), :],
            send_sem=row_send.at[e, way],
            recv_sem=row_recv.at[e, way, slot],
            device_id=(target, mx),
            device_id_type=MESH,
        )

    def row_step(e, way, j):
        return row_copy(e, way, pl.ds(0, 2 * PARTS[0][1]), j, CHUNK, 0)

    def row_rest(e, way):
        return row_copy(e, way, pl.ds(2 * PARTS[1][0], 2 * PARTS[1][1]), 0, HALF, 1)

    def row_drain(e, way):
        start = HALF if way == 0 else ROWS
        target = my - 1 if way == 0 else my + 1
        return pltpu.make_async_remote_copy(
            src_ref=ext.at[e, :, pl.ds(start, HALF), :],
            dst_ref=ext.at[e, :, pl.ds(start, HALF), :],
            send_sem=row_send.at[e, way],
            recv_sem=row_recv.at[e, way, 0],
            device_id=(target, mx),
            device_id_type=MESH,
        )

    can_row = (my > 0, my < tiles_y - 1)
    can_edge = (mx > 0, mx < tiles_x - 1)

    def send_rows(e, j):
        for way in range(2):

            @pl.when(can_row[way])
            def _():
                row_step(e, way, j).start()

    def send_rest(e):
        for way in range(2):

            @pl.when(can_row[way])
            def _():
                row_rest(e, way).start()

    def wait_rows(e, part):
        for way in range(2):

            @pl.when(can_row[1 - way])
            def _():
                if part == 0:
                    row_copy(e, way, pl.ds(0, 2 * PARTS[0][1]), 0, HALF, 0).wait_recv()
                else:
                    row_rest(e, way).wait_recv()

    def edge_copy(e, part, way):
        target = mx - 1 if way == 0 else mx + 1
        pairs = pl.ds(*PARTS[part])
        return pltpu.make_async_remote_copy(
            src_ref=edge_out.at[e, way, pairs],
            dst_ref=edge_in.at[e, 1 - way, pairs],
            send_sem=edge_send.at[e, way],
            recv_sem=edge_recv.at[e, way, part],
            device_id=(my, target),
            device_id_type=MESH,
        )

    def edge_drain(e, way):
        target = mx - 1 if way == 0 else mx + 1
        return pltpu.make_async_remote_copy(
            src_ref=edge_out.at[e, way],
            dst_ref=edge_in.at[e, 1 - way],
            send_sem=edge_send.at[e, way],
            recv_sem=edge_recv.at[e, way, 0],
            device_id=(my, target),
            device_id_type=MESH,
        )

    lane128 = lax.broadcasted_iota(jnp.int32, (ROWS, 128), 1)

    def rows_pass(e, kind):
        for part, (first_pair, count) in enumerate(PARTS):
            wait_rows(e, part)
            for i in range(first_pair, first_pair + count):
                ends = []
                for s in (2 * i, 2 * i + 1):
                    passed = jnp.dot(
                        band_row[kind * SECTORS + s], ext[e, s], preferred_element_type=F32
                    )
                    mid[s] = passed.astype(BF16)
                    ends.append((passed[:, 0:128], passed[:, 128:256]))
                first, second = ends
                low = lane128 < HALF
                edge_out[e, 0, i] = jnp.where(
                    low, first[0], pltpu.roll(second[0], HALF, 1)
                ).astype(BF16)
                edge_out[e, 1, i] = jnp.where(
                    low, pltpu.roll(second[1], HALF, 1), first[1]
                ).astype(BF16)
            for way in range(2):

                @pl.when(can_edge[way])
                def _():
                    edge_copy(e, part, way).start()

    def columns_start(kind, result):
        def one(half, carry):
            for k in range(4):
                s = 4 * half + k
                result[s] = jnp.dot(
                    mid[s], band_col[kind * SECTORS + s], preferred_element_type=F32
                )
            return carry

        lax.fori_loop(0, 2, one, 0)

    def columns_finish(e, kind, result):
        for part, (first_pair, count) in enumerate(PARTS):
            for way in range(2):

                @pl.when(can_edge[1 - way])
                def _():
                    edge_copy(e, part, way).wait_recv()

            for s in range(2 * first_pair, 2 * (first_pair + count)):
                for side in range(2):
                    lanes = slice(128 * side, 128 * side + 128)
                    result[s, :, lanes] += jnp.dot(
                        edge_in[e, side, s // 2],
                        band_edge[kind * SECTORS + s, side],
                        preferred_element_type=F32,
                    )

    def make_bands(kind):
        u = lax.broadcasted_iota(jnp.int32, (COLS, COLS), 0)
        x = lax.broadcasted_iota(jnp.int32, (COLS, COLS), 1)
        inside = jnp.abs(u - x) <= 128

        def one(s, carry):
            b = kind * SECTORS + s
            line = jnp.broadcast_to(tap_row[pl.ds(b, 1), :], (ROWS, COLS))
            rows_band = pltpu.roll(line, 0, 1, stride=1, stride_axis=0)
            band_row[b] = rows_band.astype(BF16)
            circle = jnp.concatenate(
                [pltpu.roll(rows_band, COLS - HALF, 1), pltpu.roll(rows_band, HALF, 1)], axis=0
            )
            band_col[b] = jnp.where(inside, circle, 0.0).astype(BF16)
            rest = jnp.where(inside, 0.0, circle)
            swap = lax.rem(s, 2) == 1
            for side in range(2):
                block = rest[128 - 128 * side : 256 - 128 * side, 128 * side : 128 * side + 128]
                turned = jnp.concatenate([block[HALF:], block[:HALF]], axis=0)
                band_edge[b, side] = jnp.where(swap, turned, block).astype(BF16)
            return carry

        lax.fori_loop(0, SECTORS, one, 0)

    def parts_of(a):
        return 2 if a == 0 else 1

    def first_copy(a, y, x):
        return pltpu.make_async_remote_copy(
            src_ref=one_out.at[a, y * chips_x + x, pl.ds(0, parts_of(a))],
            dst_ref=one_in.at[a, mine, pl.ds(0, parts_of(a))],
            send_sem=one_send.at[a],
            recv_sem=one_recv.at[a],
            device_id=(y, 2 * x + core),
            device_id_type=MESH,
        )

    def first_all(a):
        return pltpu.make_async_remote_copy(
            src_ref=one_out.at[a, pl.ds(0, chips - 1), pl.ds(0, parts_of(a))],
            dst_ref=one_in.at[a, pl.ds(0, chips - 1), pl.ds(0, parts_of(a))],
            send_sem=one_send.at[a],
            recv_sem=one_recv.at[a],
            device_id=(my, sibling),
            device_id_type=MESH,
        )

    def second_copy(a):
        return pltpu.make_async_remote_copy(
            src_ref=two_out.at[a, pl.ds(0, parts_of(a))],
            dst_ref=two_in.at[a, pl.ds(0, parts_of(a)), 1],
            send_sem=two_send.at[a],
            recv_sem=two_recv.at[a],
            device_id=(my, sibling),
            device_id_type=MESH,
        )

    def start_first(a):
        for k in range(1, chips_x):
            first_copy(a, my, lax.rem(chip_x + k, chips_x)).start()

        def one(j, carry):
            for k in range(chips_x):
                first_copy(a, lax.rem(my + j, tiles_y), lax.rem(chip_x + k, chips_x)).start()
            return carry

        lax.fori_loop(1, tiles_y, one, 0)
        for part in range(parts_of(a)):
            one_in[a, mine, part] = one_out[a, mine, part]

    def pass_on(a):
        first_all(a).wait_recv()
        kept = []
        for part in range(parts_of(a)):
            parts = one_in[a, :, part].astype(F32).reshape(chips, 2, CAP, 128)
            low, high = parts[:, 0], parts[:, 1]
            other = jnp.where(core == 0, high, low).reshape(chips * CAP, 128)
            two_out[a, part] = other.astype(BF16)
            own = jnp.where(core == 0, low, high).reshape(chips * CAP, 128)
            kept.append(own.astype(BF16))
        second_copy(a).start()
        for part in range(parts_of(a)):
            two_in[a, part, 0] = kept[part]

    def sum_copy(x):
        return pltpu.make_async_remote_copy(
            src_ref=sum_out,
            dst_ref=sum_in.at[chip_x],
            send_sem=sum_send.at[0],
            recv_sem=sum_recv.at[0],
            device_id=(my, 2 * x + core),
            device_id_type=MESH,
        )

    def total_copy(y):
        return pltpu.make_async_remote_copy(
            src_ref=total_out,
            dst_ref=total_in.at[my],
            send_sem=sum_send.at[1],
            recv_sem=sum_recv.at[1],
            device_id=(y, mx),
            device_id_type=MESH,
        )

    def sum_all():
        return pltpu.make_async_remote_copy(
            src_ref=sum_in.at[pl.ds(0, chips_x - 1)],
            dst_ref=sum_in.at[pl.ds(0, chips_x - 1)],
            send_sem=sum_send.at[0],
            recv_sem=sum_recv.at[0],
            device_id=(my, sibling),
            device_id_type=MESH,
        )

    def total_all():
        return pltpu.make_async_remote_copy(
            src_ref=total_in.at[pl.ds(0, tiles_y - 1)],
            dst_ref=total_in.at[pl.ds(0, tiles_y - 1)],
            send_sem=sum_send.at[1],
            recv_sem=sum_recv.at[1],
            device_id=(my, sibling),
            device_id_type=MESH,
        )

    def last_copy():
        return pltpu.make_async_remote_copy(
            src_ref=last_in.at[0],
            dst_ref=last_in.at[1],
            send_sem=sum_send.at[2],
            recv_sem=sum_recv.at[2],
            device_id=(my, sibling),
            device_id_type=MESH,
        )

    def unit(r, h):
        return pl.ds(r, CHUNK), pl.ds(pl.multiple_of(128 * h, 128), 128)

    def strip_rows(r, h, g):
        return pl.ds(pl.multiple_of((8 * h + g) * ROWS + r, CHUNK), CHUNK)

    def over_cells(work, sent, carry, wide):
        def step(j, carry):
            def one(u, carry):
                for k in range(wide):
                    number = u * wide + k
                    r = pl.multiple_of((number // 2) * HALF + j * CHUNK, CHUNK)
                    carry = work(r, number % 2, carry)
                return carry

            carry = one(0, carry) if wide == 4 else lax.fori_loop(0, 4 // wide, one, carry)
            if sent is not None:
                send_rows(sent, j)
            return carry

        carry = lax.fori_loop(0, STEPS, step, carry)
        if sent is not None:
            send_rest(sent)
        return carry

    def shares(it, r, h, wages, revenue):
        rows, lanes = unit(r, h)
        powers = [w * w * w for w in wages]
        inverse = 1.0 / sum(powers[1:], powers[0])
        people = resident_ref[rows, lanes]
        earned = sum([p * w for p, w in zip(powers[1:], wages[1:])], powers[0] * wages[0])
        income = earned * inverse
        income_ref[it, rows, lanes] = income
        scale = people * inverse
        supply = [p * scale for p in powers]
        for s in range(SECTORS):
            ext[2 * it, s, pl.ds(HALF + r, CHUNK), lanes] = supply[s].astype(BF16)
        for g, strip in enumerate(swap_blocks(supply)):
            table[strip_rows(r, h, g), :] = strip.astype(BF16)
        gain = people * rate_ref[rows, lanes] * income
        return revenue + gain[0:8] + gain[8:16]

    def gather(a):
        picked = jnp.dot(source_hot[...], table[...], preferred_element_type=F32).astype(BF16)
        ordered = jnp.dot(slot_hot[...], picked, preferred_element_type=F32).astype(BF16)
        one_out[a, :, 0] = ordered.reshape(chips, 2 * CAP, 128)

    zero = jnp.zeros((8, 128), F32)

    def first_cells(r, h, carry):
        people_sum, revenue = carry
        rows, lanes = unit(r, h)
        bracket = bracket_ref[rows, lanes]
        rate = jnp.zeros((CHUNK, 128), F32)
        for b in range(8):
            rate = jnp.where(bracket == b, tax_ref[b], rate)
        rate_ref[rows, lanes] = rate
        people = resident_ref[rows, lanes]
        people_sum = people_sum + people[0:8] + people[8:16]
        wages = [base_ref[s, rows, lanes].astype(F32) for s in range(SECTORS)]
        return people_sum, shares(0, r, h, wages, revenue)

    for load in loads:
        load.wait()
    people_sum, revenue0 = over_cells(first_cells, None, (zero, zero), 4)
    pl.semaphore_wait(barrier, chips + 1)
    for j in range(STEPS):
        send_rows(0, j)
    send_rest(0)

    line = lax.broadcasted_iota(jnp.int32, (8, far_pairs), 0)
    source, target = src_ref[...], dst_ref[...]
    row, group = target >> 4, target & 15
    fields = [
        dest_ref[...],
        (source & 15) * ROWS + (source >> 4),
        ((((row >> 4) & 3) * 2 + (row >> 6)) * GROUPS) + group,
        row & 15,
        count_ref[...],
    ]
    pairs = jnp.zeros((8, far_pairs), jnp.int32)
    for k, field in enumerate(fields):
        pairs = jnp.where(line == k, field, pairs)
    pairs = pairs.astype(F32)
    across = jnp.concatenate([pairs, jnp.zeros((120, far_pairs), F32)], axis=0).T
    dest_row = pairs[0:1, :]
    earlier = lax.broadcasted_iota(jnp.int32, (far_pairs, far_pairs), 0) < (
        lax.broadcasted_iota(jnp.int32, (far_pairs, far_pairs), 1)
    )
    same = (across[:, 0:1] == dest_row) & earlier
    rank = jnp.sum(jnp.where(same, 1.0, 0.0), axis=0, keepdims=True)
    slot_of = (dest_row * CAP + rank).astype(jnp.int32)
    slot_ids = lax.broadcasted_iota(jnp.int32, (slots, far_pairs), 0)
    slot_hot[...] = jnp.where(slot_ids == slot_of, 1.0, 0.0).astype(BF16)
    strip_ids = lax.broadcasted_iota(jnp.int32, (far_pairs, GROUPS * ROWS), 1)
    source_hot[...] = jnp.where(
        strip_ids == across[:, 1:2].astype(jnp.int32), 1.0, 0.0
    ).astype(BF16)
    one_out[0, :, 1] = (
        jnp.dot(slot_hot[...], across.astype(BF16), preferred_element_type=F32)
        .astype(BF16)
        .reshape(chips, 2 * CAP, 128)
    )
    gather(0)
    start_first(0)

    @pl.when(my == 0)
    def _():
        ext[:, :, 0:HALF, :] = jnp.zeros((2 * ITERS, SECTORS, HALF, COLS), BF16)

    @pl.when(my == tiles_y - 1)
    def _():
        ext[:, :, HALF + ROWS :, :] = jnp.zeros((2 * ITERS, SECTORS, HALF, COLS), BF16)

    @pl.when(mx == 0)
    def _():
        edge_in[:, 0] = jnp.zeros((2 * ITERS, PAIRS2, ROWS, 128), BF16)

    @pl.when(mx == tiles_x - 1)
    def _():
        edge_in[:, 1] = jnp.zeros((2 * ITERS, PAIRS2, ROWS, 128), BF16)

    sector = lax.broadcasted_iota(jnp.int32, (2 * SECTORS, COLS), 0)
    tap = lax.broadcasted_iota(jnp.int32, (2 * SECTORS, COLS), 1)
    decay = jnp.zeros((2 * SECTORS, COLS), F32)
    for s in range(SECTORS):
        decay = jnp.where(sector == s, commute_ref[s], decay)
        decay = jnp.where(sector == SECTORS + s, spill_ref[s], decay)
    offset = jnp.abs(tap - HALF).astype(F32) / HALF
    unscaled = jnp.where(tap <= 2 * HALF, jnp.exp(-decay * offset), 0.0)
    tap_row[...] = (unscaled / jnp.sum(unscaled, axis=1, keepdims=True)).astype(BF16).astype(F32)
    make_bands(0)


    def build_place(half):
        width = chips * CAP
        columns = slice(half * width, (half + 1) * width)
        routing = two_in[0, 1, half]
        line = lax.broadcasted_iota(jnp.int32, (16, 128), 0)
        lane = lax.broadcasted_iota(jnp.int32, (16, 128), 1)
        pick = jnp.where((line == 0) & (lane == 2), float(CHUNK), 0.0)
        pick = jnp.where((line == 0) & (lane == 3), 1.0, pick)
        pick = jnp.where((line == 1) & (lane == 4), 1.0, pick).astype(BF16)
        found = lax.dot_general(
            pick, routing, (((1,), (1,)), ((), ())), preferred_element_type=F32
        )
        where_to, weight = found[0:1, :].astype(jnp.int32), FAR_SCALE * found[1:2, :]

        def one(g, carry):
            strip = g * ROWS + lax.broadcasted_iota(jnp.int32, (ROWS, width), 0)
            place[pl.ds(pl.multiple_of(g * ROWS, ROWS), ROWS), columns] = jnp.where(
                strip == where_to, weight, 0.0
            ).astype(BF16)
            return carry

        lax.fori_loop(0, GROUPS, one, 0)

    revenues = [revenue0]
    for it in range(ITERS):
        if it > 0:
            gather(it)
            start_first(it)
        if it == ITERS - 1:
            line = lax.broadcasted_iota(jnp.int32, (8, 128), 0)
            parts = zero
            for k, part in enumerate([people_sum] + revenues):
                parts = jnp.where(line == k, jnp.sum(part, axis=0, keepdims=True), parts)
            sum_out[...] = parts

            def start_sum(j, carry):
                sum_copy(lax.rem(chip_x + j, chips_x)).start()
                return carry

            lax.fori_loop(1, chips_x, start_sum, 0)
            sum_in[chip_x] = parts
        rows_pass(2 * it, 0)
        columns_start(0, near)
        pass_on(it)
        if it == 0:
            build_place(0)
        if it == ITERS - 1:
            sum_all().wait_recv()
            halfway = jnp.sum(sum_in[...], axis=0)
            total_out[...] = halfway

            def start_total(j, carry):
                total_copy(lax.rem(my + j, tiles_y)).start()
                return carry

            lax.fori_loop(1, tiles_y, start_total, 0)
            total_in[my] = halfway
        columns_finish(2 * it, 0, near)
        if it == ITERS - 1:
            total_all().wait_recv()
            last_in[0] = jnp.sum(total_in[...], axis=0)
            last_copy().start()
        second_copy(it).wait_recv()
        if it == 0:
            build_place(1)

        def labor_step(j, carry):
            block = 2 * GROUPS * CHUNK
            far[...] = jnp.dot(
                place[pl.ds(pl.multiple_of(j * block, block), block), :],
                two_in[it, 0].reshape(slots, 128),
                preferred_element_type=F32,
            )
            for number in range(4):
                way, h = number // 2, number % 2
                r = pl.multiple_of(way * HALF + j * CHUNK, CHUNK)
                rows, lanes = unit(r, h)
                first = (way * GROUPS + 8 * h) * CHUNK
                strips = [far[first + CHUNK * g : first + CHUNK * (g + 1), :] for g in range(8)]
                for s, flow in enumerate(swap_blocks(strips)):
                    value = near[s, rows, lanes] + flow
                    labor[s, rows, lanes] = value
                    ext[2 * it + 1, s, pl.ds(HALF + r, CHUNK), lanes] = value.astype(BF16)
            send_rows(2 * it + 1, j)
            return carry

        lax.fori_loop(0, STEPS, labor_step, 0)
        send_rest(2 * it + 1)
        if it == 0:
            make_bands(1)

        def labor_power(c, carry):
            rows = pl.ds(pl.multiple_of(c * CHUNK, CHUNK), CHUNK)
            for s in range(SECTORS):
                labor[s, rows, :] = -BETA_WAGE * jnp.log(1.0 + labor[s, rows, :])
            return carry

        lax.fori_loop(0, ROWS // CHUNK, labor_power, 0)
        if it == ITERS - 1:
            last_copy().wait_recv()
            sums = jnp.sum(last_in[0] + last_in[1], axis=1, keepdims=True)
            people_all = sums[0:1, 0:1]
            transfers = [sums[1 + k : 2 + k, 0:1] / people_all for k in range(ITERS)]

            def rent_chunk(c, carry):
                rows = pl.ds(pl.multiple_of(c * CHUNK, CHUNK), CHUNK)
                keep = 1.0 - rate_ref[rows, :]
                people, space = resident_ref[rows, :], floor_ref[rows, :]
                ratio = people / space
                square = None
                for k in range(ITERS):
                    net = keep * income_ref[k, rows, :] + transfers[k]
                    level = ratio if square is None else jnp.sqrt(square) * ratio
                    square = level * net
                rent_ref[rows, :] = square
                return carry

            lax.fori_loop(0, ROWS // CHUNK, rent_chunk, 0)
        rows_pass(2 * it + 1, 1)
        columns_start(1, near)
        columns_finish(2 * it + 1, 1, near)

        def wage_cells(r, h, revenue):
            rows, lanes = unit(r, h)
            logs = [jnp.log(1.0 + near[s, rows, lanes]) for s in range(SECTORS)]
            wages = []
            for s in range(SECTORS):
                power = labor[s, rows, lanes]
                for t in range(SECTORS):
                    power = power + mixing_ref[s, t] * logs[t]
                if it == ITERS - 1:
                    power_ref[s, rows, lanes] = power
                else:
                    wages.append(base_ref[s, rows, lanes].astype(F32) * jnp.exp(power))
            if it < ITERS - 1:
                revenue = shares(it + 1, r, h, wages, revenue)
            return revenue

        sent = 2 * it + 2 if it < ITERS - 1 else None
        revenues.append(over_cells(wage_cells, sent, zero, 4))

    for e in range(2 * ITERS):
        for way in range(2):

            @pl.when(can_row[way])
            def _():
                row_drain(e, way).wait_send()

            @pl.when(can_edge[way])
            def _():
                edge_drain(e, way).wait_send()

    for a in range(ITERS):
        first_all(a).wait_send()
        second_copy(a).wait_send()
    sum_all().wait_send()
    total_all().wait_send()
    last_copy().wait_send()


def body(
    base_prod,
    resident,
    floor_space,
    bracket,
    tax_rate,
    mixing,
    spill_decay,
    commute_decay,
    pair_dest,
    pair_src,
    pair_dst,
    pair_count,
):
    tiles_y = lax.axis_size("gy")
    tiles_x = lax.axis_size("gx")
    slots = tiles_y * tiles_x * CAP
    chips = tiles_y * tiles_x // 2
    far_pairs = pair_src.shape[0]
    vmem = pl.BlockSpec(memory_space=pltpu.VMEM)
    whole = pl.BlockSpec(memory_space=pltpu.HBM)
    smem = pltpu.SMEM
    exchanges = 2 * ITERS
    dma = pltpu.SemaphoreType.DMA
    power, square = pl.pallas_call(
        functools.partial(kernel, tiles_y, tiles_x),
        out_shape=(
            jax.ShapeDtypeStruct(base_prod.shape, F32),
            jax.ShapeDtypeStruct(resident.shape, F32),
        ),
        in_specs=[whole] * 12,
        out_specs=(vmem, vmem),
        scratch_shapes=[
            pltpu.VMEM((exchanges, SECTORS, ROWS + 2 * HALF, COLS), BF16),
            pltpu.VMEM((exchanges, 2, PAIRS2, ROWS, 128), BF16),
            pltpu.VMEM((exchanges, 2, PAIRS2, ROWS, 128), BF16),
            pltpu.VMEM((SECTORS, ROWS, COLS), BF16),
            pltpu.VMEM((SECTORS, ROWS, COLS), F32),
            pltpu.VMEM((SECTORS, ROWS, COLS), F32),
            pltpu.VMEM((2 * SECTORS, COLS), F32),
            pltpu.VMEM((2 * SECTORS, ROWS, COLS), BF16),
            pltpu.VMEM((2 * SECTORS, COLS, COLS), BF16),
            pltpu.VMEM((2 * SECTORS, 2, 128, 128), BF16),
            pltpu.VMEM((GROUPS * ROWS, 128), BF16),
            pltpu.VMEM((far_pairs, GROUPS * ROWS), BF16),
            pltpu.VMEM((slots, far_pairs), BF16),
            pltpu.VMEM((GROUPS * ROWS, slots), BF16),
            pltpu.VMEM((2 * GROUPS * CHUNK, 128), F32),
            pltpu.VMEM((ITERS, chips, 2, 2 * CAP, 128), BF16),
            pltpu.VMEM((ITERS, chips, 2, 2 * CAP, 128), BF16),
            pltpu.VMEM((ITERS, 2, chips * CAP, 128), BF16),
            pltpu.VMEM((ITERS, 2, 2, chips * CAP, 128), BF16),
            pltpu.VMEM((8, 128), F32),
            pltpu.VMEM((tiles_x // 2, 8, 128), F32),
            pltpu.VMEM((8, 128), F32),
            pltpu.VMEM((tiles_y, 8, 128), F32),
            pltpu.VMEM((ROWS, COLS), F32),
            pltpu.VMEM((ITERS, ROWS, COLS), F32),
            pltpu.VMEM((2, 8, 128), F32),
            pltpu.VMEM((SECTORS, ROWS, COLS), BF16),
            pltpu.VMEM((ROWS, COLS), F32),
            pltpu.VMEM((ROWS, COLS), F32),
            pltpu.VMEM((ROWS, COLS), jnp.int32),
            pltpu.VMEM((1, far_pairs), jnp.int32),
            pltpu.VMEM((1, far_pairs), jnp.int32),
            pltpu.VMEM((1, far_pairs), jnp.int32),
            pltpu.VMEM((1, far_pairs), jnp.int32),
            smem((8,), F32),
            smem((SECTORS,), F32),
            smem((SECTORS,), F32),
            smem((SECTORS, SECTORS), F32),
            dma((12,)),
            dma((exchanges, 2)),
            dma((exchanges, 2, 2)),
            dma((exchanges, 2)),
            dma((exchanges, 2, 2)),
            dma((ITERS,)),
            dma((ITERS,)),
            dma((ITERS,)),
            dma((ITERS,)),
            dma((3,)),
            dma((3,)),
        ],
        compiler_params=pltpu.CompilerParams(
            collective_id=0, has_side_effects=True, vmem_limit_bytes=40 * 1024 * 1024
        ),
    )(
        *(
            pltpu.with_memory_space_constraint(x, pltpu.HBM)
            for x in (
                base_prod,
                resident,
                floor_space,
                bracket,
                pair_dest.reshape(1, far_pairs),
                pair_src.reshape(1, far_pairs),
                pair_dst.reshape(1, far_pairs),
                pair_count.reshape(1, far_pairs),
                tax_rate,
                commute_decay,
                spill_decay,
                mixing,
            )
        )
    )
    return base_prod.astype(F32) * jnp.exp(power), jnp.sqrt(square)


def solution(mesh):
    return jax.shard_map(
        body,
        mesh=mesh,
        in_specs=(
            P(None, "gy", "gx"),
            P("gy", "gx"),
            P("gy", "gx"),
            P("gy", "gx"),
            P(),
            P(),
            P(),
            P(),
            P(("gy", "gx"), None),
            P(("gy", "gx")),
            P(("gy", "gx")),
            P(("gy", "gx")),
        ),
        out_specs=(P(None, "gy", "gx"), P("gy", "gx")),
        check_vma=False,
    )
```
